512 devices in a mesh: dp: 64 (over y, z), mp: 8 (over x, core).
Axes of the slice: x: 4, y: 4, z: 16, core: 2. Of those that a mesh axis runs over, the one named last changes fastest.
Arguments:
- pre_act: bfloat16 [32768, 16384], P('dp', 'mp'), may hold values from -8 to 8
- out_weight: bfloat16 [16384, 512], P('mp'), may hold values from -0.046875 to 0.046875
- out_grad: bfloat16 [32768, 512], P(('dp', 'mp')), may hold values from -2 to 2
Outputs:
- projected: bfloat16 [32768, 512], P(('dp', 'mp'))
- combined: float32 [16384, 512], P(('mp', 'dp'))
The draws below stay inside these ranges and needn't reach their ends.
All inputs are finite; a program needn't handle non-finite values.
Results may differ from the reference program's by a relative error of at most 0.0005.
Values may be sent and summed in bfloat16 or wider, within the bound.
No kernel may reach another device: no remote copies, remote signals or barrier semaphores. Data moves between devices by JAX's collectives and lax.ppermute only.
A program may use at most 64 MiB of HBM per device.

```python
import math
import jax
import jax.numpy as jnp
from jax import lax

D = 512
FF = 16384
TOK_DEV = 512
TOKENS = 32768
N_DP = 64


def draw_pre_act(key, part):
    base = jax.random.normal(jax.random.fold_in(key, 11), (FF,), jnp.float32)
    noise = jax.random.normal(jax.random.fold_in(key, 12), (TOKENS, FF), jnp.float32)
    values = 0.6 * base[None, :] + noise
    return jnp.clip(values, -8.0, 8.0).astype(jnp.bfloat16)


def draw_out_grad(key, part):
    base = jax.random.normal(jax.random.fold_in(key, 21), (D,), jnp.float32)
    block_count = TOKENS // TOK_DEV
    block_scale = jnp.exp(jax.random.uniform(jax.random.fold_in(key, 23), (block_count,), jnp.float32, 0.0, math.log(10.0)))
    row_scale = jnp.exp(jax.random.uniform(jax.random.fold_in(key, 24), (TOKENS,), jnp.float32, -0.5, 0.5))
    scales = jnp.repeat(block_scale, TOK_DEV) * row_scale
    noise = jax.random.normal(jax.random.fold_in(key, 22), (TOKENS, D), jnp.float32)
    values = 0.06 * base[None, :] + noise
    return jnp.clip(0.025 * scales[:, None] * values, -2.0, 2.0).astype(jnp.bfloat16)


def levels(own_key, dims, split, low, top_value):
    gain, own = 1.0, jax.random.fold_in(own_key, 6)
    for axis_at, shards_of in split:
        draws = jnp.exp(jax.random.uniform(jax.random.fold_in(own, axis_at), (shards_of,), jnp.float32, low / len(split), top_value / len(split)))
        gain = gain * jnp.repeat(draws, dims[axis_at] // shards_of).reshape([-1 if axis == axis_at else 1 for axis in range(len(dims))])
    return gain


def scatter_about(key, shape, spread, reach, shards=(), held_as=jnp.bfloat16):
    entries = jax.random.normal(key, shape, jnp.float32) * spread
    if len(shards) > 0:
        entries = levels(key, shape, shards, -0.22, 0.18) * entries
    return jnp.clip(entries, min=-reach, max=reach).astype(held_as)


def setup_inputs(seed: int = 0) -> dict:
    key_of = jax.random.split(jax.random.key(seed), 4)
    return {
        "pre_act": draw_pre_act(jax.random.fold_in(key_of[3], 71), 0),
        "out_weight": scatter_about(key_of[1], (FF, D), FF ** -0.5, 0.046875, ((0, 8),)),
        "out_grad": draw_out_grad(jax.random.fold_in(key_of[3], 71), 0),
    }


epsilon = 1e-6


def pair(first, second):
    inner = jnp.sum(first * second)
    first_sq = jnp.sum(first * first)
    second_sq = jnp.sum(second * second)
    return (1.0 - inner / (2.0 * (first_sq + epsilon))) * first + (1.0 - inner / (2.0 * (second_sq + epsilon))) * second


def reference(pre_act, out_weight, out_grad):
    act = jnp.maximum(pre_act, jnp.zeros((), jnp.bfloat16))
    projected = jnp.dot(act, out_weight, preferred_element_type=jnp.float32).astype(jnp.bfloat16)

    def leaf(index):
        rows = act[index * TOK_DEV:(index + 1) * TOK_DEV]
        grads = out_grad[index * TOK_DEV:(index + 1) * TOK_DEV]
        return lax.dot_general(rows, grads, (((0,), (0,)), ((), ())), preferred_element_type=jnp.float32)

    def build(low, count):
        if count == 1:
            return leaf(low)
        half = count // 2
        return pair(build(low, half), build(low + half, half))

    combined = build(0, N_DP)
    return projected, combined
```

```python
import functools

import jax
import jax.numpy as jnp
from jax import lax
from jax.experimental import pallas as pl
from jax.experimental.pallas import tpu as pltpu
from jax.sharding import Mesh, PartitionSpec as P

epsilon = 1e-06
LEAVES = 4
NODES = 16
LIMIT = 64 * 1024 * 1024 * 3 // 4
TOP = 16384.0
FLOOR = 1e-15

f32 = jnp.float32
bf16 = jnp.bfloat16
SMEM = pl.BlockSpec(memory_space=pltpu.SMEM)
VMEM = pl.BlockSpec(memory_space=pltpu.VMEM)


def call(kernel, out_shape, in_specs, flops=0, size=0, scratch=()):
    many = isinstance(out_shape, (list, tuple))
    return pl.pallas_call(
        kernel,
        out_shape=out_shape,
        in_specs=in_specs,
        out_specs=[VMEM] * len(out_shape) if many else VMEM,
        scratch_shapes=list(scratch),
        compiler_params=pltpu.CompilerParams(vmem_limit_bytes=LIMIT),
        cost_estimate=pl.CostEstimate(flops=flops, bytes_accessed=size, transcendentals=0),
    )


def from_everyone(array, axes):
    count = lax.axis_size(axes)
    copies = jnp.broadcast_to(array, (count, *array.shape))
    return lax.all_to_all(copies, axes, split_axis=0, concat_axis=0, tiled=True)


def deal_kernel(me_ref, pre_ref, *out_refs):
    me = me_ref[0]
    width = 512
    row = lax.broadcasted_iota(jnp.int32, (width, width), 0)
    col = lax.broadcasted_iota(jnp.int32, (width, width), 1)
    block = row >> 5
    place = (((block & 3) ^ me) << 7) + ((block >> 2) << 5) + (row & 31)
    deal = jnp.where(place == col, 1.0, 0.0).astype(bf16)
    for group in range(pre_ref.shape[1] // width):
        part = jnp.maximum(pre_ref[:, group * width : (group + 1) * width], jnp.zeros((), bf16))
        dealt = jnp.dot(part, deal, preferred_element_type=f32).astype(bf16)
        for k in range(LEAVES):
            out_refs[k][:, group * 128 : (group + 1) * 128] = dealt[:, k * 128 : (k + 1) * 128]


def leaf_kernel(which, act_ref, grads_ref, out_ref):
    peers, _, rows, width = grads_ref.shape
    out_grad = grads_ref[:, which].reshape(peers * rows, width)
    out_ref[...] = lax.dot_general(
        act_ref[...], out_grad, (((0,), (0,)), ((), ())), preferred_element_type=f32
    )


def lanes_of(total):
    return total[:, :128] + total[:, 128:256] + total[:, 256:384] + total[:, 384:512]


def first_gram_kernel(me_ref, *refs):
    leaf_refs, out_ref, held = refs[:LEAVES], refs[LEAVES], refs[LEAVES + 1]
    me = me_ref[0]
    for a in range(LEAVES):
        for b in range(a, LEAVES):
            partial_sum = lanes_of(jnp.sum(leaf_refs[a][...] * leaf_refs[b][...], axis=0, keepdims=True))
            held[pl.ds(LEAVES * (a ^ me) + (b ^ me), 1), :] = partial_sum
            if a != b:
                held[pl.ds(LEAVES * (b ^ me) + (a ^ me), 1), :] = partial_sum
    whole = held[...]
    for copy in range(out_ref.shape[0]):
        out_ref[copy] = whole


def tree(gram, count):
    coef = [None] * count
    weight = [jnp.ones_like(gram[0][0])] * count
    size = 1
    while size < count:
        for low in range(0, count, 2 * size):
            first, second = range(low, low + size), range(low + size, low + 2 * size)

            def inner(left, right):
                return sum(weight[i] * weight[j] * gram[i][j] for i in left for j in right)

            cross = inner(first, second)
            first_sq = jnp.maximum(inner(first, first), 0.0)
            second_sq = jnp.maximum(inner(second, second), 0.0)
            first_coef = 1.0 - cross / (2.0 * (first_sq + epsilon))
            second_coef = 1.0 - cross / (2.0 * (second_sq + epsilon))
            for i in first:
                coef[i] = weight[i] * first_coef
            for i in second:
                coef[i] = weight[i] * second_coef
        weight = list(coef)
        size *= 2
    return weight


def first_merge_kernel(me_ref, sums_ref, *refs):
    leaf_refs, node_ref, inverse_ref = refs[:LEAVES], refs[LEAVES], refs[LEAVES + 1]
    me = me_ref[0]
    total = jnp.sum(jnp.sum(sums_ref[...], axis=0), axis=1, keepdims=True)
    gram = [
        [total[LEAVES * i + j : LEAVES * i + j + 1, :] for j in range(LEAVES)] for i in range(LEAVES)
    ]
    coef = tree(gram, LEAVES)
    bound = sum(jnp.abs(coef[i]) * jnp.sqrt(gram[i][i]) for i in range(LEAVES))
    bound = jnp.maximum(bound, FLOOR)
    scale = TOP / bound
    inverse_ref[...] = jnp.broadcast_to(bound * (1.0 / TOP), inverse_ref.shape)
    merged = None
    for k in range(LEAVES):
        mine = coef[k]
        for other in range(1, LEAVES):
            mine = jnp.where(me == other, coef[k ^ other], mine)
        term = (mine * scale) * leaf_refs[k][...]
        merged = term if merged is None else merged + term
    node_ref[...] = merged


def second_gram_kernel(copies, share, node_ref, nodes_ref, inverse_ref, out_ref):
    node = node_ref[0]
    total, width = nodes_ref.shape
    rows = total // NODES
    held = nodes_ref[...]
    high = held.astype(bf16)
    low = (held - high.astype(f32)).astype(bf16)
    last = (((1,), (1,)), ((), ()))
    products = (
        lax.dot_general(high, high, last, preferred_element_type=f32)
        + lax.dot_general(high, low, last, preferred_element_type=f32)
        + lax.dot_general(low, high, last, preferred_element_type=f32)
        + lax.dot_general(low, low, last, preferred_element_type=f32)
    )
    row = lax.broadcasted_iota(jnp.int32, (total, total), 0)
    col = lax.broadcasted_iota(jnp.int32, (total, total), 1)
    products = jnp.where((row & (rows - 1)) == (col & (rows - 1)), products, 0.0)
    by_node = jnp.sum(products.reshape(NODES, rows, total), axis=1)
    source = lax.broadcasted_iota(jnp.int32, (total, 128), 0)
    lane = lax.broadcasted_iota(jnp.int32, (total, 128), 1)
    spread = jnp.where(source // rows == (lane & (NODES - 1)), 1.0, 0.0)
    gram = jnp.dot(by_node, spread, preferred_element_type=f32, precision=lax.Precision.HIGHEST)
    place = lax.broadcasted_iota(jnp.int32, (NODES, 128), 0)
    lane = lax.broadcasted_iota(jnp.int32, (NODES, 128), 1)
    packed = jnp.where(lane // NODES == (place & 7), gram, 0.0)
    lane = lane[:1]
    inverse = jnp.where(lane == node, inverse_ref[:1] * share, 0.0)
    whole = jnp.concatenate(
        [
            jnp.sum(packed[:8], axis=0, keepdims=True),
            jnp.sum(packed[8:], axis=0, keepdims=True),
            inverse,
            jnp.zeros_like(inverse),
        ],
        axis=0,
    )
    for copy in range(copies):
        out_ref[copy] = whole


def pass_on_kernel(sums_ref, out_ref):
    whole = jnp.sum(sums_ref[...], axis=0)
    for copy in range(out_ref.shape[0]):
        out_ref[copy] = whole


def second_merge_kernel(sums_ref, nodes_ref, out_ref):
    total = jnp.sum(sums_ref[...], axis=0)
    place = lax.broadcasted_iota(jnp.int32, (NODES, 128), 0)
    lane = lax.broadcasted_iota(jnp.int32, (NODES, 128), 1)
    gram = jnp.where(place < 8, total[0:1], total[1:2])
    gram = jnp.where(lane // NODES == (place & 7), gram, 0.0)
    inverse_row = jnp.where(lane[:1] < NODES, total[2:3], 0.0)
    for turn in (16, 32, 64):
        gram = gram + pltpu.roll(gram, turn, 1)
        inverse_row = inverse_row + pltpu.roll(inverse_row, turn, 1)
    other = lane & (NODES - 1)
    first = lane < NODES

    def column(row):
        return jnp.sum(jnp.where(lane == place, row, 0.0), axis=1, keepdims=True)

    inverse_col = column(inverse_row)
    gram = gram * inverse_row * inverse_col
    size, weight = 1, jnp.ones((NODES, 1), f32)
    while size < NODES:
        mine = (place // size) == (other // size)
        sibling = (place // size) == ((other // size) ^ 1)
        own_col = jnp.sum(jnp.where(mine, gram, 0.0), axis=0, keepdims=True)
        cross_col = jnp.sum(jnp.where(sibling, gram, 0.0), axis=0, keepdims=True)
        here = mine & first
        own = jnp.sum(jnp.where(here, own_col, 0.0), axis=1, keepdims=True)
        cross = jnp.sum(jnp.where(here, cross_col, 0.0), axis=1, keepdims=True)
        coef = 1.0 - cross / (2.0 * (jnp.maximum(own, 0.0) + epsilon))
        coef_row = jnp.sum(jnp.where(place == other, coef, 0.0), axis=0, keepdims=True)
        gram = gram * coef * coef_row
        weight = weight * coef
        size *= 2
    weight = weight * inverse_col
    combined = None
    for node in range(NODES):
        term = weight[node : node + 1, :] * nodes_ref[node]
        combined = term if combined is None else combined + term
    out_ref[...] = combined


def local(pre_act, out_weight, out_grad):
    tokens, hidden = pre_act.shape
    width = out_weight.shape[1]
    mp = ("x", "c")
    hi = ("y", "zh")
    peers = lax.axis_size(mp)
    me = lax.axis_index("zl").astype(jnp.int32).reshape(1)
    node = lax.axis_index(hi).astype(jnp.int32).reshape(1)
    quarter = hidden // LEAVES

    def from_neighbour(value, apart):
        return lax.ppermute(value, "zl", [(i, i ^ apart) for i in range(LEAVES)])

    grad_shards = [out_grad] + [from_neighbour(out_grad, k) for k in range(1, LEAVES)]
    dealt = call(
        deal_kernel,
        [jax.ShapeDtypeStruct((tokens, quarter), bf16)] * LEAVES,
        [SMEM, VMEM],
        flops=2 * tokens * hidden * 512,
        size=4 * tokens * hidden,
    )(me, pre_act)
    acts = [dealt[0]] + [from_neighbour(dealt[k], k) for k in range(1, LEAVES)]
    grads = from_everyone(jnp.stack(grad_shards), mp)

    act = jnp.maximum(pre_act, jnp.zeros((), bf16))
    partial_out = jnp.dot(act, out_weight, preferred_element_type=f32)
    parts = partial_out.reshape(peers, tokens // peers, width)
    arrived = lax.all_to_all(parts, mp, split_axis=0, concat_axis=0, tiled=True)
    projected = arrived.sum(axis=0).astype(bf16)

    leaf_shape = jax.ShapeDtypeStruct((quarter, width), f32)
    leaves = [
        call(
            functools.partial(leaf_kernel, k),
            leaf_shape,
            [VMEM, VMEM],
            flops=2 * tokens * quarter * width,
            size=4 * quarter * width,
        )(acts[k], grads)
        for k in range(LEAVES)
    ]
    group = ("zl", *mp)
    sums = call(
        first_gram_kernel,
        jax.ShapeDtypeStruct((LEAVES * peers, 16, 128), f32),
        [SMEM] + [VMEM] * LEAVES,
        flops=20 * quarter * width,
        size=16 * quarter * width,
        scratch=[pltpu.VMEM((16, 128), f32)],
    )(me, *leaves)
    sums = lax.all_to_all(sums, group, split_axis=0, concat_axis=0, tiled=True)
    scaled, inverse = call(
        first_merge_kernel,
        [leaf_shape, jax.ShapeDtypeStruct((8, 128), f32)],
        [SMEM] + [VMEM] * (LEAVES + 1),
        flops=8 * quarter * width,
        size=20 * quarter * width,
    )(me, sums, *leaves)

    rows = quarter // NODES
    sent = scaled.astype(jnp.float16).reshape(NODES, rows, width)
    nodes = lax.all_to_all(sent, hi, split_axis=0, concat_axis=0, tiled=True).astype(f32)
    share = 1.0 / (LEAVES * peers)
    sums = call(
        functools.partial(second_gram_kernel, peers, share),
        jax.ShapeDtypeStruct((peers, 4, 128), f32),
        [SMEM, VMEM, VMEM],
        flops=8 * quarter * quarter * width,
        size=4 * quarter * width,
    )(node, nodes.reshape(quarter, width), inverse)
    sums = lax.all_to_all(sums, mp, split_axis=0, concat_axis=0, tiled=True)
    dp = ("y", "zh", "zl")
    sums = call(pass_on_kernel, jax.ShapeDtypeStruct((lax.axis_size(dp), 4, 128), f32), [VMEM])(sums)
    sums = lax.all_to_all(sums, dp, split_axis=0, concat_axis=0, tiled=True)
    combined = call(
        second_merge_kernel,
        jax.ShapeDtypeStruct((rows, width), f32),
        [VMEM, VMEM],
        flops=2 * quarter * width,
        size=4 * quarter * width,
    )(sums, nodes)
    return projected, combined


def solution(mesh):
    devices = mesh.devices.reshape(4, 4, LEAVES, 4, 2)
    finer = Mesh(devices, ("y", "zh", "zl", "x", "c"))
    dp, mp = ("y", "zh", "zl"), ("x", "c")
    return jax.shard_map(
        local,
        mesh=finer,
        in_specs=(P(dp, mp), P(mp, None), P((*dp, *mp), None)),
        out_specs=(P((*dp, *mp), None), P((*mp, *dp), None)),
        check_vma=False,
    )
```

```python
import functools

import jax
import jax.numpy as jnp
from jax import lax
from jax.experimental import pallas as pl
from jax.experimental.pallas import tpu as pltpu
from jax.sharding import Mesh, PartitionSpec as P

epsilon = 1e-06
LEAVES = 4
NODES = 16
LIMIT = 64 * 1024 * 1024 * 3 // 4
TOP = 16384.0
FLOOR = 1e-15

f32 = jnp.float32
bf16 = jnp.bfloat16
SMEM = pl.BlockSpec(memory_space=pltpu.SMEM)
VMEM = pl.BlockSpec(memory_space=pltpu.VMEM)


def call(kernel, out_shape, in_specs, flops=0, size=0, scratch=()):
    many = isinstance(out_shape, (list, tuple))
    return pl.pallas_call(
        kernel,
        out_shape=out_shape,
        in_specs=in_specs,
        out_specs=[VMEM] * len(out_shape) if many else VMEM,
        scratch_shapes=list(scratch),
        compiler_params=pltpu.CompilerParams(vmem_limit_bytes=LIMIT),
        cost_estimate=pl.CostEstimate(flops=flops, bytes_accessed=size, transcendentals=0),
    )


def from_everyone(array, axes):
    copies = jnp.broadcast_to(array, (lax.axis_size(axes), *array.shape))
    return lax.all_to_all(copies, axes, split_axis=0, concat_axis=0, tiled=True)


def deal_kernel(me_ref, pre_ref, *refs):
    out_refs, deal_ref = refs[:LEAVES], refs[LEAVES]
    width = pre_ref.shape[1]

    @pl.when(pl.program_id(0) == 0)
    def _():
        row = lax.broadcasted_iota(jnp.int32, (width, width), 0)
        col = lax.broadcasted_iota(jnp.int32, (width, width), 1)
        block = row >> 5
        place = (((block & 3) ^ me_ref[0]) << 7) + ((block >> 2) << 5) + (row & 31)
        deal_ref[...] = jnp.where(place == col, 1.0, 0.0).astype(bf16)

    part = jnp.maximum(pre_ref[...], jnp.zeros((), bf16))
    dealt = jnp.dot(part, deal_ref[...], preferred_element_type=f32).astype(bf16)
    for k in range(LEAVES):
        out_refs[k][...] = dealt[:, k * 128 : (k + 1) * 128]


def deal(me, pre_act):
    tokens, hidden = pre_act.shape
    group = 512
    return pl.pallas_call(
        deal_kernel,
        grid_spec=pltpu.PrefetchScalarGridSpec(
            num_scalar_prefetch=1,
            grid=(hidden // group,),
            in_specs=[pl.BlockSpec((tokens, group), lambda g, me: (0, g))],
            out_specs=[pl.BlockSpec((tokens, group // LEAVES), lambda g, me: (0, g))] * LEAVES,
            scratch_shapes=[pltpu.VMEM((group, group), bf16)],
        ),
        out_shape=[jax.ShapeDtypeStruct((tokens, hidden // LEAVES), bf16)] * LEAVES,
        compiler_params=pltpu.CompilerParams(vmem_limit_bytes=LIMIT),
        cost_estimate=pl.CostEstimate(
            flops=2 * tokens * hidden * group, bytes_accessed=4 * tokens * hidden, transcendentals=0
        ),
    )(me, pre_act)


def leaf_of(act_ref, grads_ref):
    peers, _, rows, width = grads_ref.shape
    out_grad = grads_ref[:, 0].reshape(peers * rows, width)
    return lax.dot_general(act_ref[...], out_grad, (((0,), (0,)), ((), ())), preferred_element_type=f32)


def leaf_kernel(me_ref, act_ref, grads_ref, out_ref):
    out_ref[...] = leaf_of(act_ref, grads_ref)


def with_leaf(kernel, k, me, act, grads, others, outs):
    peers, _, shard, width = grads.shape
    tokens, quarter = act.shape

    def whole(shape):
        return pl.BlockSpec(shape, lambda g, me: (0,) * len(shape))

    return pl.pallas_call(
        kernel,
        grid_spec=pltpu.PrefetchScalarGridSpec(
            num_scalar_prefetch=1,
            grid=(1,),
            in_specs=[
                whole(act.shape),
                pl.BlockSpec((peers, 1, shard, width), lambda g, me: (0, me[0] ^ k, 0, 0)),
            ]
            + [whole(other.shape) for other in others],
            out_specs=[whole(out.shape) for out in outs],
        ),
        out_shape=outs,
        compiler_params=pltpu.CompilerParams(vmem_limit_bytes=LIMIT),
        cost_estimate=pl.CostEstimate(
            flops=2 * tokens * quarter * width, bytes_accessed=4 * quarter * width, transcendentals=0
        ),
    )(me, act, grads, *others)


def project_kernel(pre_ref, weight_ref, late_ref, out_ref):
    act = jnp.maximum(pre_ref[...], jnp.zeros((), bf16))
    out_ref[...] = jnp.dot(act, weight_ref[...], preferred_element_type=f32)


def lanes_of(total):
    return total[:, :128] + total[:, 128:256] + total[:, 256:384] + total[:, 384:512]


def first_gram_kernel(order, me_ref, act_ref, grads_ref, *refs):
    count = LEAVES - 1
    other_refs, (leaf_ref, out_ref) = refs[:count], refs[count:]
    leaf_ref[...] = leaf_of(act_ref, grads_ref)
    held = dict(zip(order, (*other_refs, leaf_ref)))
    me = me_ref[0]
    lane = lax.broadcasted_iota(jnp.int32, (1, 128), 1)
    whole = jnp.zeros((1, 128), f32)
    for a in range(LEAVES):
        for b in range(a, LEAVES):
            lanes = lanes_of(jnp.sum(held[a][...] * held[b][...], axis=0, keepdims=True))
            value = jnp.sum(lanes, axis=1, keepdims=True)
            here = lane == LEAVES * (a ^ me) + (b ^ me)
            if a != b:
                here = here | (lane == LEAVES * (b ^ me) + (a ^ me))
            whole = jnp.where(here, value, whole)
    for copy in range(out_ref.shape[0]):
        out_ref[copy] = whole


def tree(gram, count):
    coef = [None] * count
    weight = [jnp.ones_like(gram[0][0])] * count
    size = 1
    while size < count:
        for low in range(0, count, 2 * size):
            first, second = range(low, low + size), range(low + size, low + 2 * size)

            def inner(left, right):
                return sum(weight[i] * weight[j] * gram[i][j] for i in left for j in right)

            cross = inner(first, second)
            first_sq = jnp.maximum(inner(first, first), 0.0)
            second_sq = jnp.maximum(inner(second, second), 0.0)
            first_coef = 1.0 - cross / (2.0 * (first_sq + epsilon))
            second_coef = 1.0 - cross / (2.0 * (second_sq + epsilon))
            for i in first:
                coef[i] = weight[i] * first_coef
            for i in second:
                coef[i] = weight[i] * second_coef
        weight = list(coef)
        size *= 2
    return weight


def first_merge_kernel(me_ref, sums_ref, *refs):
    leaf_refs, node_ref, inverse_ref = refs[:LEAVES], refs[LEAVES], refs[LEAVES + 1]
    me = me_ref[0]
    total = jnp.sum(sums_ref[...], axis=0)
    lane = lax.broadcasted_iota(jnp.int32, total.shape, 1)
    gram = [
        [
            jnp.sum(jnp.where(lane == LEAVES * i + j, total, 0.0), axis=1, keepdims=True)
            for j in range(LEAVES)
        ]
        for i in range(LEAVES)
    ]
    coef = tree(gram, LEAVES)
    bound = sum(jnp.abs(coef[i]) * jnp.sqrt(gram[i][i]) for i in range(LEAVES))
    bound = jnp.maximum(bound, FLOOR)
    scale = TOP / bound
    inverse_ref[...] = jnp.broadcast_to(bound * (1.0 / TOP), inverse_ref.shape)
    merged = None
    for k in range(LEAVES):
        mine = coef[k]
        for other in range(1, LEAVES):
            mine = jnp.where(me == other, coef[k ^ other], mine)
        term = (mine * scale) * leaf_refs[k][...]
        merged = term if merged is None else merged + term
    node_ref[...] = merged


def second_gram_kernel(copies, share, node_ref, nodes_ref, inverse_ref, late_ref, out_ref):
    node = node_ref[0]
    total, width = nodes_ref.shape
    rows = total // NODES
    held = nodes_ref[...]
    high = held.astype(bf16)
    low = (held - high.astype(f32)).astype(bf16)
    last = (((1,), (1,)), ((), ()))
    products = (
        lax.dot_general(high, high, last, preferred_element_type=f32)
        + lax.dot_general(high, low, last, preferred_element_type=f32)
        + lax.dot_general(low, high, last, preferred_element_type=f32)
        + lax.dot_general(low, low, last, preferred_element_type=f32)
    )
    row = lax.broadcasted_iota(jnp.int32, (total, total), 0)
    col = lax.broadcasted_iota(jnp.int32, (total, total), 1)
    products = jnp.where((row & (rows - 1)) == (col & (rows - 1)), products, 0.0)
    by_node = jnp.sum(products.reshape(NODES, rows, total), axis=1)
    source = lax.broadcasted_iota(jnp.int32, (total, 128), 0)
    lane = lax.broadcasted_iota(jnp.int32, (total, 128), 1)
    spread = jnp.where(source // rows == (lane & (NODES - 1)), 1.0, 0.0)
    gram = jnp.dot(by_node, spread, preferred_element_type=f32, precision=lax.Precision.HIGHEST)
    place = lax.broadcasted_iota(jnp.int32, (NODES, 128), 0)
    lane = lax.broadcasted_iota(jnp.int32, (NODES, 128), 1)
    packed = jnp.where(lane // NODES == (place & 7), gram, 0.0)
    lane = lane[:1]
    inverse = jnp.where(lane == node, inverse_ref[:1] * share, 0.0)
    whole = jnp.concatenate(
        [
            jnp.sum(packed[:8], axis=0, keepdims=True),
            jnp.sum(packed[8:], axis=0, keepdims=True),
            inverse,
            jnp.zeros_like(inverse),
        ],
        axis=0,
    )
    for copy in range(copies):
        out_ref[copy] = whole


def pass_on_kernel(sums_ref, out_ref):
    whole = jnp.sum(sums_ref[...], axis=0)
    for copy in range(out_ref.shape[0]):
        out_ref[copy] = whole


def second_merge_kernel(sums_ref, nodes_ref, out_ref):
    total = jnp.sum(sums_ref[...], axis=0)
    place = lax.broadcasted_iota(jnp.int32, (NODES, 128), 0)
    lane = lax.broadcasted_iota(jnp.int32, (NODES, 128), 1)
    gram = jnp.where(place < 8, total[0:1], total[1:2])
    gram = jnp.where(lane // NODES == (place & 7), gram, 0.0)
    inverse_row = jnp.where(lane[:1] < NODES, total[2:3], 0.0)
    for turn in (16, 32, 64):
        gram = gram + pltpu.roll(gram, turn, 1)
        inverse_row = inverse_row + pltpu.roll(inverse_row, turn, 1)
    other = lane & (NODES - 1)
    first = lane < NODES

    def column(row):
        return jnp.sum(jnp.where(lane == place, row, 0.0), axis=1, keepdims=True)

    inverse_col = column(inverse_row)
    gram = gram * inverse_row * inverse_col
    size, weight = 1, jnp.ones((NODES, 1), f32)
    while size < NODES:
        mine = (place // size) == (other // size)
        sibling = (place // size) == ((other // size) ^ 1)
        own_col = jnp.sum(jnp.where(mine, gram, 0.0), axis=0, keepdims=True)
        cross_col = jnp.sum(jnp.where(sibling, gram, 0.0), axis=0, keepdims=True)
        here = mine & first
        own = jnp.sum(jnp.where(here, own_col, 0.0), axis=1, keepdims=True)
        cross = jnp.sum(jnp.where(here, cross_col, 0.0), axis=1, keepdims=True)
        coef = 1.0 - cross / (2.0 * (jnp.maximum(own, 0.0) + epsilon))
        coef_row = jnp.sum(jnp.where(place == other, coef, 0.0), axis=0, keepdims=True)
        gram = gram * coef * coef_row
        weight = weight * coef
        size *= 2
    weight = weight * inverse_col
    combined = None
    for node in range(NODES):
        term = weight[node : node + 1, :] * nodes_ref[node]
        combined = term if combined is None else combined + term
    out_ref[...] = combined


def local(pre_act, out_weight, out_grad):
    tokens, hidden = pre_act.shape
    width = out_weight.shape[1]
    mp = ("x", "c")
    hi = ("y", "zh")
    peers = lax.axis_size(mp)
    me = lax.axis_index("zl").astype(jnp.int32).reshape(1)
    node = lax.axis_index(hi).astype(jnp.int32).reshape(1)
    quarter = hidden // LEAVES

    def from_neighbour(value, apart):
        return lax.ppermute(value, "zl", [(i, i ^ apart) for i in range(LEAVES)])

    shards = from_everyone(out_grad, "zl")
    grads = from_everyone(shards, mp)
    dealt = deal(me, pre_act)
    acts = [dealt[0]] + [from_neighbour(dealt[k], k) for k in range(1, LEAVES)]

    leaf_shape = jax.ShapeDtypeStruct((quarter, width), f32)
    order = (0, 1, 3, 2)
    leaves = {}
    for k in order[:-1]:
        (leaves[k],) = with_leaf(leaf_kernel, k, me, acts[k], grads, [], [leaf_shape])
    k = order[-1]
    group = ("zl", *mp)
    leaves[k], sums = with_leaf(
        functools.partial(first_gram_kernel, order),
        k,
        me,
        acts[k],
        grads,
        [leaves[other] for other in order[:-1]],
        [leaf_shape, jax.ShapeDtypeStruct((LEAVES * peers, 1, 128), f32)],
    )
    sums = lax.all_to_all(sums, group, split_axis=0, concat_axis=0, tiled=True)
    scaled, inverse = call(
        first_merge_kernel,
        [leaf_shape, jax.ShapeDtypeStruct((8, 128), f32)],
        [SMEM] + [VMEM] * (LEAVES + 1),
        flops=8 * quarter * width,
        size=20 * quarter * width,
    )(me, sums, *[leaves[k] for k in range(LEAVES)])

    partial_out = call(
        project_kernel,
        jax.ShapeDtypeStruct((tokens, width), f32),
        [VMEM, VMEM, pl.BlockSpec(memory_space=pl.ANY)],
        flops=2 * tokens * hidden * width,
        size=4 * tokens * hidden,
    )(pre_act, out_weight, inverse)
    projected = lax.psum_scatter(partial_out, mp, scatter_dimension=0, tiled=True).astype(bf16)

    rows = quarter // NODES
    sent = scaled.astype(jnp.float16).reshape(NODES, rows, width)
    nodes = lax.all_to_all(sent, hi, split_axis=0, concat_axis=0, tiled=True).astype(f32)
    share = 1.0 / (LEAVES * peers)
    sums = call(
        functools.partial(second_gram_kernel, LEAVES * peers, share),
        jax.ShapeDtypeStruct((LEAVES * peers, 4, 128), f32),
        [SMEM, VMEM, VMEM, pl.BlockSpec(memory_space=pl.ANY)],
        flops=8 * quarter * quarter * width,
        size=4 * quarter * width,
    )(node, nodes.reshape(quarter, width), inverse, partial_out)
    sums = lax.all_to_all(sums, group, split_axis=0, concat_axis=0, tiled=True)
    sums = call(pass_on_kernel, jax.ShapeDtypeStruct((NODES, 4, 128), f32), [VMEM])(sums)
    sums = lax.all_to_all(sums, hi, split_axis=0, concat_axis=0, tiled=True)
    combined = call(
        second_merge_kernel,
        jax.ShapeDtypeStruct((rows, width), f32),
        [VMEM, VMEM],
        flops=2 * quarter * width,
        size=4 * quarter * width,
    )(sums, nodes)
    return projected, combined


def solution(mesh):
    devices = mesh.devices.reshape(4, 4, LEAVES, 4, 2)
    finer = Mesh(devices, ("y", "zh", "zl", "x", "c"))
    dp, mp = ("y", "zh", "zl"), ("x", "c")
    return jax.shard_map(
        local,
        mesh=finer,
        in_specs=(P(dp, mp), P(mp, None), P((*dp, *mp), None)),
        out_specs=(P((*dp, *mp), None), P((*mp, *dp), None)),
        check_vma=False,
    )
```

```python
import functools

import jax
import jax.numpy as jnp
from jax import lax
from jax.experimental import pallas as pl
from jax.experimental.pallas import tpu as pltpu
from jax.sharding import Mesh, PartitionSpec as P

epsilon = 1e-06
LEAVES = 4
NODES = 16
LIMIT = 24 * 1024 * 1024
TOP = 16384.0
FLOOR = 1e-15

f32 = jnp.float32
bf16 = jnp.bfloat16
SMEM = pl.BlockSpec(memory_space=pltpu.SMEM)
VMEM = pl.BlockSpec(memory_space=pltpu.VMEM)
ANY = pl.BlockSpec(memory_space=pl.ANY)


def call(kernel, out_shape, in_specs, flops=0, size=0, scratch=()):
    many = isinstance(out_shape, (list, tuple))
    return pl.pallas_call(
        kernel,
        out_shape=out_shape,
        in_specs=in_specs,
        out_specs=[VMEM] * len(out_shape) if many else VMEM,
        scratch_shapes=list(scratch),
        compiler_params=pltpu.CompilerParams(vmem_limit_bytes=LIMIT),
        cost_estimate=pl.CostEstimate(flops=flops, bytes_accessed=size, transcendentals=0),
    )


def from_everyone(array, axes):
    copies = jnp.broadcast_to(array, (lax.axis_size(axes), *array.shape))
    return lax.all_to_all(copies, axes, split_axis=0, concat_axis=0, tiled=True)


def deal_kernel(me_ref, pre_ref, *refs):
    out_refs, deal_ref = refs[:LEAVES], refs[LEAVES]
    width = pre_ref.shape[1]

    @pl.when(pl.program_id(0) == 0)
    def _():
        row = lax.broadcasted_iota(jnp.int32, (width, width), 0)
        col = lax.broadcasted_iota(jnp.int32, (width, width), 1)
        block = row >> 5
        place = (((block & 3) ^ me_ref[0]) << 7) + ((block >> 2) << 5) + (row & 31)
        deal_ref[...] = jnp.where(place == col, 1.0, 0.0).astype(bf16)

    part = jnp.maximum(pre_ref[...], jnp.zeros((), bf16))
    dealt = jnp.dot(part, deal_ref[...], preferred_element_type=f32).astype(bf16)
    for k in range(LEAVES):
        out_refs[k][...] = dealt[:, k * 128 : (k + 1) * 128]


def deal(me, pre_act):
    tokens, hidden = pre_act.shape
    group = 512
    return pl.pallas_call(
        deal_kernel,
        grid_spec=pltpu.PrefetchScalarGridSpec(
            num_scalar_prefetch=1,
            grid=(hidden // group,),
            in_specs=[pl.BlockSpec((tokens, group), lambda g, me: (0, g))],
            out_specs=[pl.BlockSpec((tokens, group // LEAVES), lambda g, me: (0, g))] * LEAVES,
            scratch_shapes=[pltpu.VMEM((group, group), bf16)],
        ),
        out_shape=[jax.ShapeDtypeStruct((tokens, hidden // LEAVES), bf16)] * LEAVES,
        compiler_params=pltpu.CompilerParams(vmem_limit_bytes=LIMIT),
        cost_estimate=pl.CostEstimate(
            flops=2 * tokens * hidden * group, bytes_accessed=4 * tokens * hidden, transcendentals=0
        ),
    )(me, pre_act)


def arrived_kernel(*refs):
    refs[-1][...] = jnp.zeros_like(refs[-1])


def project_kernel(spot_ref, pre_ref, weight_ref, late_ref, mine_ref, theirs_ref, held_ref):
    count = mine_ref.shape[0]
    x, core = spot_ref[1], spot_ref[2]
    act = jnp.maximum(pre_ref[...], jnp.zeros((), bf16))
    total = jnp.dot(act, weight_ref[...], preferred_element_type=f32)
    held_ref[...] = total.reshape(held_ref.shape)
    for k in range(count):
        mine_ref[k] = held_ref[x ^ k, core]
        theirs_ref[k] = held_ref[x ^ k, 1 - core]


def lanes_of(total):
    return total[:, :128] + total[:, 128:256] + total[:, 256:384] + total[:, 384:512]


def first_gram_kernel(spot_ref, grads_ref, late_ref, *refs):
    act_refs, held, out_ref = refs[:LEAVES], refs[LEAVES:-1], refs[-1]
    peers, _, rows, width = grads_ref.shape
    me = spot_ref[0]
    for k in range(LEAVES):
        out_grad = grads_ref[:, me ^ k].reshape(peers * rows, width)
        held[k][...] = lax.dot_general(
            act_refs[k][...], out_grad, (((0,), (0,)), ((), ())), preferred_element_type=f32
        )
    lane = lax.broadcasted_iota(jnp.int32, (1, 128), 1)
    whole = jnp.zeros((1, 128), f32)
    for a in range(LEAVES):
        for b in range(a, LEAVES):
            lanes = lanes_of(jnp.sum(held[a][...] * held[b][...], axis=0, keepdims=True))
            value = jnp.sum(lanes, axis=1, keepdims=True)
            here = lane == LEAVES * (a ^ me) + (b ^ me)
            if a != b:
                here = here | (lane == LEAVES * (b ^ me) + (a ^ me))
            whole = jnp.where(here, value, whole)
    for copy in range(out_ref.shape[0]):
        out_ref[copy] = whole


def tree(gram, count):
    coef = [None] * count
    weight = [jnp.ones_like(gram[0][0])] * count
    size = 1
    while size < count:
        for low in range(0, count, 2 * size):
            first, second = range(low, low + size), range(low + size, low + 2 * size)

            def inner(left, right):
                return sum(weight[i] * weight[j] * gram[i][j] for i in left for j in right)

            cross = inner(first, second)
            first_sq = jnp.maximum(inner(first, first), 0.0)
            second_sq = jnp.maximum(inner(second, second), 0.0)
            first_coef = 1.0 - cross / (2.0 * (first_sq + epsilon))
            second_coef = 1.0 - cross / (2.0 * (second_sq + epsilon))
            for i in first:
                coef[i] = weight[i] * first_coef
            for i in second:
                coef[i] = weight[i] * second_coef
        weight = list(coef)
        size *= 2
    return weight


def first_merge_kernel(me_ref, sums_ref, *refs):
    leaf_refs, node_ref, inverse_ref = refs[:LEAVES], refs[LEAVES], refs[LEAVES + 1]
    me = me_ref[0]
    total = jnp.sum(sums_ref[...], axis=0)
    lane = lax.broadcasted_iota(jnp.int32, total.shape, 1)
    gram = [
        [
            jnp.sum(jnp.where(lane == LEAVES * i + j, total, 0.0), axis=1, keepdims=True)
            for j in range(LEAVES)
        ]
        for i in range(LEAVES)
    ]
    coef = tree(gram, LEAVES)
    bound = sum(jnp.abs(coef[i]) * jnp.sqrt(gram[i][i]) for i in range(LEAVES))
    bound = jnp.maximum(bound, FLOOR)
    scale = TOP / bound
    inverse_ref[...] = jnp.broadcast_to(bound * (1.0 / TOP), inverse_ref.shape)
    merged = None
    for k in range(LEAVES):
        mine = coef[k]
        for other in range(1, LEAVES):
            mine = jnp.where(me == other, coef[k ^ other], mine)
        term = (mine * scale) * leaf_refs[k][...]
        merged = term if merged is None else merged + term
    node_ref[...] = merged


def second_gram_kernel(copies, share, node_ref, nodes_ref, inverse_ref, late_ref, out_ref):
    node = node_ref[0]
    total, width = nodes_ref.shape
    rows = total // NODES
    held = nodes_ref[...]
    high = held.astype(bf16)
    low = (held - high.astype(f32)).astype(bf16)
    last = (((1,), (1,)), ((), ()))
    products = (
        lax.dot_general(high, high, last, preferred_element_type=f32)
        + lax.dot_general(high, low, last, preferred_element_type=f32)
        + lax.dot_general(low, high, last, preferred_element_type=f32)
        + lax.dot_general(low, low, last, preferred_element_type=f32)
    )
    row = lax.broadcasted_iota(jnp.int32, (total, total), 0)
    col = lax.broadcasted_iota(jnp.int32, (total, total), 1)
    products = jnp.where((row & (rows - 1)) == (col & (rows - 1)), products, 0.0)
    by_node = jnp.sum(products.reshape(NODES, rows, total), axis=1)
    source = lax.broadcasted_iota(jnp.int32, (total, 128), 0)
    lane = lax.broadcasted_iota(jnp.int32, (total, 128), 1)
    spread = jnp.where(source // rows == (lane & (NODES - 1)), 1.0, 0.0)
    gram = jnp.dot(by_node, spread, preferred_element_type=f32, precision=lax.Precision.HIGHEST)
    place = lax.broadcasted_iota(jnp.int32, (NODES, 128), 0)
    lane = lax.broadcasted_iota(jnp.int32, (NODES, 128), 1)
    packed = jnp.where(lane // NODES == (place & 7), gram, 0.0)
    lane = lane[:1]
    inverse = jnp.where(lane == node, inverse_ref[:1] * share, 0.0)
    whole = jnp.concatenate(
        [
            jnp.sum(packed[:8], axis=0, keepdims=True),
            jnp.sum(packed[8:], axis=0, keepdims=True),
            inverse,
            jnp.zeros_like(inverse),
        ],
        axis=0,
    )
    for copy in range(copies):
        out_ref[copy] = whole


def pass_on_kernel(sums_ref, out_ref):
    whole = jnp.sum(sums_ref[...], axis=0)
    for copy in range(out_ref.shape[0]):
        out_ref[copy] = whole


def second_merge_kernel(sums_ref, nodes_ref, out_ref):
    total = jnp.sum(sums_ref[...], axis=0)
    place = lax.broadcasted_iota(jnp.int32, (NODES, 128), 0)
    lane = lax.broadcasted_iota(jnp.int32, (NODES, 128), 1)
    gram = jnp.where(place < 8, total[0:1], total[1:2])
    gram = jnp.where(lane // NODES == (place & 7), gram, 0.0)
    inverse_row = jnp.where(lane[:1] < NODES, total[2:3], 0.0)
    for turn in (16, 32, 64):
        gram = gram + pltpu.roll(gram, turn, 1)
        inverse_row = inverse_row + pltpu.roll(inverse_row, turn, 1)
    other = lane & (NODES - 1)
    first = lane < NODES

    def column(row):
        return jnp.sum(jnp.where(lane == place, row, 0.0), axis=1, keepdims=True)

    inverse_col = column(inverse_row)
    gram = gram * inverse_row * inverse_col
    size, weight = 1, jnp.ones((NODES, 1), f32)
    while size < NODES:
        mine = (place // size) == (other // size)
        sibling = (place // size) == ((other // size) ^ 1)
        own_col = jnp.sum(jnp.where(mine, gram, 0.0), axis=0, keepdims=True)
        cross_col = jnp.sum(jnp.where(sibling, gram, 0.0), axis=0, keepdims=True)
        here = mine & first
        own = jnp.sum(jnp.where(here, own_col, 0.0), axis=1, keepdims=True)
        cross = jnp.sum(jnp.where(here, cross_col, 0.0), axis=1, keepdims=True)
        coef = 1.0 - cross / (2.0 * (jnp.maximum(own, 0.0) + epsilon))
        coef_row = jnp.sum(jnp.where(place == other, coef, 0.0), axis=0, keepdims=True)
        gram = gram * coef * coef_row
        weight = weight * coef
        size *= 2
    weight = weight * inverse_col
    combined = None
    for node in range(NODES):
        term = weight[node : node + 1, :] * nodes_ref[node]
        combined = term if combined is None else combined + term
    out_ref[...] = combined


def local(pre_act, out_weight, out_grad):
    tokens, hidden = pre_act.shape
    width = out_weight.shape[1]
    mp = ("x", "c")
    hi = ("y", "zh")
    peers = lax.axis_size(mp)
    spot = jnp.stack([lax.axis_index(axis) for axis in ("zl", "x", "c")]).astype(jnp.int32)
    me = spot[:1]
    node = lax.axis_index(hi).astype(jnp.int32).reshape(1)
    quarter = hidden // LEAVES
    along = lax.axis_size("x")

    def swapped(value, axis, apart):
        return lax.ppermute(value, axis, [(i, i ^ apart) for i in range(lax.axis_size(axis))])

    shards = from_everyone(out_grad, "zl")
    grads = from_everyone(shards, mp)
    dealt = deal(me, pre_act)
    acts = [dealt[0]] + [swapped(dealt[k], "zl", k) for k in range(1, LEAVES)]
    arrived = pl.pallas_call(
        arrived_kernel,
        out_shape=jax.ShapeDtypeStruct((8, 128), f32),
        in_specs=[ANY] * (LEAVES - 1),
        compiler_params=pltpu.CompilerParams(vmem_limit_bytes=1024 * 1024),
        cost_estimate=pl.CostEstimate(flops=10**11, bytes_accessed=0, transcendentals=0),
    )(*acts[1:])

    leaf_shape = jax.ShapeDtypeStruct((quarter, width), f32)
    group = ("zl", *mp)
    *leaves, sums = call(
        first_gram_kernel,
        [leaf_shape] * LEAVES + [jax.ShapeDtypeStruct((LEAVES * peers, 1, 128), f32)],
        [SMEM, VMEM, VMEM] + [VMEM] * LEAVES,
        flops=2 * tokens * hidden * width,
        size=16 * quarter * width,
    )(spot, grads, arrived, *acts)
    sums = lax.all_to_all(sums, group, split_axis=0, concat_axis=0, tiled=True)
    scaled, inverse = call(
        first_merge_kernel,
        [leaf_shape, jax.ShapeDtypeStruct((8, 128), f32)],
        [SMEM] + [VMEM] * (LEAVES + 1),
        flops=8 * quarter * width,
        size=20 * quarter * width,
    )(me, sums, *leaves)

    half = jax.ShapeDtypeStruct((along, tokens // peers, width), f32)
    mine, theirs = call(
        project_kernel,
        [half, half],
        [SMEM, VMEM, VMEM, VMEM],
        flops=2 * tokens * hidden * width,
        size=4 * tokens * hidden,
        scratch=[pltpu.VMEM((along, 2, tokens // peers, width), f32)],
    )(spot, pre_act, out_weight, inverse)
    both = mine + swapped(theirs, "c", 1)
    projected = both[0]
    for k in range(1, along):
        projected = projected + swapped(both[k], "x", k)
    projected = projected.astype(bf16)

    rows = quarter // NODES
    sent = scaled.astype(jnp.float16).reshape(NODES, rows, width)
    nodes = lax.all_to_all(sent, hi, split_axis=0, concat_axis=0, tiled=True).astype(f32)
    share = 1.0 / (LEAVES * peers)
    sums = call(
        functools.partial(second_gram_kernel, LEAVES * peers, share),
        jax.ShapeDtypeStruct((LEAVES * peers, 4, 128), f32),
        [SMEM, VMEM, VMEM, VMEM],
        flops=8 * quarter * quarter * width,
        size=4 * quarter * width,
    )(node, nodes.reshape(quarter, width), inverse, projected)
    sums = lax.all_to_all(sums, group, split_axis=0, concat_axis=0, tiled=True)
    sums = call(pass_on_kernel, jax.ShapeDtypeStruct((NODES, 4, 128), f32), [VMEM])(sums)
    sums = lax.all_to_all(sums, hi, split_axis=0, concat_axis=0, tiled=True)
    combined = call(
        second_merge_kernel,
        jax.ShapeDtypeStruct((rows, width), f32),
        [VMEM, VMEM],
        flops=2 * quarter * width,
        size=4 * quarter * width,
    )(sums, nodes)
    return projected, combined


def solution(mesh):
    devices = mesh.devices.reshape(4, 4, LEAVES, 4, 2)
    finer = Mesh(devices, ("y", "zh", "zl", "x", "c"))
    dp, mp = ("y", "zh", "zl"), ("x", "c")
    return jax.shard_map(
        local,
        mesh=finer,
        in_specs=(P(dp, mp), P(mp, None), P((*dp, *mp), None)),
        out_specs=(P((*dp, *mp), None), P((*mp, *dp), None)),
        check_vma=False,
    )
```

```python
import functools

import jax
import jax.numpy as jnp
from jax import lax
from jax.experimental import pallas as pl
from jax.experimental.pallas import tpu as pltpu
from jax.sharding import Mesh, PartitionSpec as P

epsilon = 1e-06
LEAVES = 4
NODES = 16
LIMIT = 24 * 1024 * 1024
TOP = 16384.0
FLOOR = 1e-15

f32 = jnp.float32
bf16 = jnp.bfloat16
SMEM = pl.BlockSpec(memory_space=pltpu.SMEM)
VMEM = pl.BlockSpec(memory_space=pltpu.VMEM)
ANY = pl.BlockSpec(memory_space=pl.ANY)


def call(kernel, out_shape, in_specs, flops=0, size=0, scratch=()):
    many = isinstance(out_shape, (list, tuple))
    return pl.pallas_call(
        kernel,
        out_shape=out_shape,
        in_specs=in_specs,
        out_specs=[VMEM] * len(out_shape) if many else VMEM,
        scratch_shapes=list(scratch),
        compiler_params=pltpu.CompilerParams(vmem_limit_bytes=LIMIT),
        cost_estimate=pl.CostEstimate(flops=flops, bytes_accessed=size, transcendentals=0),
    )


def from_everyone(array, axes):
    copies = jnp.broadcast_to(array, (lax.axis_size(axes), *array.shape))
    return lax.all_to_all(copies, axes, split_axis=0, concat_axis=0, tiled=True)


def deal_kernel(me_ref, pre_ref, grad_ref, copies_ref, *refs):
    out_refs, deal_ref = refs[:LEAVES], refs[LEAVES]
    width = pre_ref.shape[1]

    @pl.when(pl.program_id(0) == 0)
    def _():
        row = lax.broadcasted_iota(jnp.int32, (width, width), 0)
        col = lax.broadcasted_iota(jnp.int32, (width, width), 1)
        block = row >> 5
        place = (((block & 3) ^ me_ref[0]) << 7) + ((block >> 2) << 5) + (row & 31)
        deal_ref[...] = jnp.where(place == col, 1.0, 0.0).astype(bf16)
        for copy in range(LEAVES):
            copies_ref[copy] = grad_ref[...]

    part = jnp.maximum(pre_ref[...], jnp.zeros((), bf16))
    dealt = jnp.dot(part, deal_ref[...], preferred_element_type=f32).astype(bf16)
    for k in range(LEAVES):
        out_refs[k][...] = dealt[:, k * 128 : (k + 1) * 128]


def deal(me, pre_act, out_grad):
    tokens, hidden = pre_act.shape
    shard, width = out_grad.shape
    group = 512
    return pl.pallas_call(
        deal_kernel,
        grid_spec=pltpu.PrefetchScalarGridSpec(
            num_scalar_prefetch=1,
            grid=(hidden // group,),
            in_specs=[
                pl.BlockSpec((tokens, group), lambda g, me: (0, g)),
                pl.BlockSpec((shard, width), lambda g, me: (0, 0)),
            ],
            out_specs=[pl.BlockSpec((LEAVES, shard, width), lambda g, me: (0, 0, 0))]
            + [pl.BlockSpec((tokens, group // LEAVES), lambda g, me: (0, g))] * LEAVES,
            scratch_shapes=[pltpu.VMEM((group, group), bf16)],
        ),
        out_shape=[jax.ShapeDtypeStruct((LEAVES, shard, width), bf16)]
        + [jax.ShapeDtypeStruct((tokens, hidden // LEAVES), bf16)] * LEAVES,
        compiler_params=pltpu.CompilerParams(vmem_limit_bytes=63 * 1024 * 1024),
        cost_estimate=pl.CostEstimate(
            flops=2 * tokens * hidden * group, bytes_accessed=4 * tokens * hidden, transcendentals=0
        ),
    )(me, pre_act, out_grad)


def arrived_kernel(*refs):
    refs[-1][...] = jnp.zeros_like(refs[-1])


def project_kernel(spot_ref, pre_ref, weight_ref, late_ref, mine_ref, theirs_ref, held_ref):
    count = mine_ref.shape[0]
    x, core = spot_ref[1], spot_ref[2]
    act = jnp.maximum(pre_ref[...], jnp.zeros((), bf16))
    total = jnp.dot(act, weight_ref[...], preferred_element_type=f32)
    held_ref[...] = total.reshape(held_ref.shape)
    for k in range(count):
        mine_ref[k] = held_ref[x ^ k, core]
        theirs_ref[k] = held_ref[x ^ k, 1 - core]


def lanes_of(total):
    return total[:, :128] + total[:, 128:256] + total[:, 256:384] + total[:, 384:512]


def first_gram_kernel(spot_ref, grads_ref, late_ref, *refs):
    act_refs, held, out_ref = refs[:LEAVES], refs[LEAVES:-1], refs[-1]
    peers, _, rows, width = grads_ref.shape
    me = spot_ref[0]
    for k in range(LEAVES):
        out_grad = grads_ref[:, me ^ k].reshape(peers * rows, width)
        held[k][...] = lax.dot_general(
            act_refs[k][...], out_grad, (((0,), (0,)), ((), ())), preferred_element_type=f32
        )
    lane = lax.broadcasted_iota(jnp.int32, (1, 128), 1)
    whole = jnp.zeros((1, 128), f32)
    for a in range(LEAVES):
        for b in range(a, LEAVES):
            lanes = lanes_of(jnp.sum(held[a][...] * held[b][...], axis=0, keepdims=True))
            value = jnp.sum(lanes, axis=1, keepdims=True)
            here = lane == LEAVES * (a ^ me) + (b ^ me)
            if a != b:
                here = here | (lane == LEAVES * (b ^ me) + (a ^ me))
            whole = jnp.where(here, value, whole)
    for copy in range(out_ref.shape[0]):
        out_ref[copy] = whole


def tree(gram, count):
    coef = [None] * count
    weight = [jnp.ones_like(gram[0][0])] * count
    size = 1
    while size < count:
        for low in range(0, count, 2 * size):
            first, second = range(low, low + size), range(low + size, low + 2 * size)

            def inner(left, right):
                return sum(weight[i] * weight[j] * gram[i][j] for i in left for j in right)

            cross = inner(first, second)
            first_sq = jnp.maximum(inner(first, first), 0.0)
            second_sq = jnp.maximum(inner(second, second), 0.0)
            first_coef = 1.0 - cross / (2.0 * (first_sq + epsilon))
            second_coef = 1.0 - cross / (2.0 * (second_sq + epsilon))
            for i in first:
                coef[i] = weight[i] * first_coef
            for i in second:
                coef[i] = weight[i] * second_coef
        weight = list(coef)
        size *= 2
    return weight


def first_merge_kernel(me_ref, sums_ref, *refs):
    leaf_refs, node_ref, inverse_ref = refs[:LEAVES], refs[LEAVES], refs[LEAVES + 1]
    me = me_ref[0]
    total = jnp.sum(sums_ref[...], axis=0)
    lane = lax.broadcasted_iota(jnp.int32, total.shape, 1)
    gram = [
        [
            jnp.sum(jnp.where(lane == LEAVES * i + j, total, 0.0), axis=1, keepdims=True)
            for j in range(LEAVES)
        ]
        for i in range(LEAVES)
    ]
    coef = tree(gram, LEAVES)
    bound = sum(jnp.abs(coef[i]) * jnp.sqrt(gram[i][i]) for i in range(LEAVES))
    bound = jnp.maximum(bound, FLOOR)
    scale = TOP / bound
    inverse_ref[...] = jnp.broadcast_to(bound * (1.0 / TOP), inverse_ref.shape)
    merged = None
    for k in range(LEAVES):
        mine = coef[k]
        for other in range(1, LEAVES):
            mine = jnp.where(me == other, coef[k ^ other], mine)
        term = (mine * scale) * leaf_refs[k][...]
        merged = term if merged is None else merged + term
    node_ref[...] = merged


def second_gram_kernel(copies, share, node_ref, nodes_ref, inverse_ref, late_ref, out_ref):
    node = node_ref[0]
    total, width = nodes_ref.shape
    rows = total // NODES
    held = nodes_ref[...]
    high = held.astype(bf16)
    low = (held - high.astype(f32)).astype(bf16)
    last = (((1,), (1,)), ((), ()))
    products = (
        lax.dot_general(high, high, last, preferred_element_type=f32)
        + lax.dot_general(high, low, last, preferred_element_type=f32)
        + lax.dot_general(low, high, last, preferred_element_type=f32)
        + lax.dot_general(low, low, last, preferred_element_type=f32)
    )
    row = lax.broadcasted_iota(jnp.int32, (total, total), 0)
    col = lax.broadcasted_iota(jnp.int32, (total, total), 1)
    products = jnp.where((row & (rows - 1)) == (col & (rows - 1)), products, 0.0)
    by_node = jnp.sum(products.reshape(NODES, rows, total), axis=1)
    source = lax.broadcasted_iota(jnp.int32, (total, 128), 0)
    lane = lax.broadcasted_iota(jnp.int32, (total, 128), 1)
    spread = jnp.where(source // rows == (lane & (NODES - 1)), 1.0, 0.0)
    gram = jnp.dot(by_node, spread, preferred_element_type=f32, precision=lax.Precision.HIGHEST)
    place = lax.broadcasted_iota(jnp.int32, (NODES, 128), 0)
    lane = lax.broadcasted_iota(jnp.int32, (NODES, 128), 1)
    packed = jnp.where(lane // NODES == (place & 7), gram, 0.0)
    lane = lane[:1]
    upper = jnp.sum(packed[:8], axis=0, keepdims=True)
    lower = jnp.sum(packed[8:], axis=0, keepdims=True)
    inverse = jnp.where(lane == (node & 7) + 2 * (node & 8), inverse_ref[:1] * share, 0.0)
    lower = jnp.where((lane & (NODES - 1)) < 8, inverse, lower)
    whole = jnp.concatenate([upper, lower], axis=0)
    for copy in range(copies):
        out_ref[copy] = whole


def pass_on_kernel(sums_ref, out_ref):
    whole = jnp.sum(sums_ref[...], axis=0)
    for copy in range(out_ref.shape[0]):
        out_ref[copy] = whole


def second_merge_kernel(sums_ref, nodes_ref, out_ref):
    total = jnp.sum(sums_ref[...], axis=0)
    place = lax.broadcasted_iota(jnp.int32, (NODES, 128), 0)
    lane = lax.broadcasted_iota(jnp.int32, (NODES, 128), 1)
    gram = jnp.where(place < 8, total[0:1], total[1:2])
    gram = jnp.where(lane // NODES == (place & 7), gram, 0.0)
    free = (lane & 8) == 0
    gram = jnp.where((place >= 8) & free, 0.0, gram)
    inverse_row = jnp.where((lane[:1] < NODES) & free[:1], total[1:2], 0.0)
    second = jnp.where((lane[:1] >= NODES) & (lane[:1] < NODES + 8), total[1:2], 0.0)
    inverse_row = inverse_row + pltpu.roll(second, 128 - 8, 1)
    for turn in (16, 32, 64):
        gram = gram + pltpu.roll(gram, turn, 1)
        inverse_row = inverse_row + pltpu.roll(inverse_row, turn, 1)
    other = lane & (NODES - 1)
    first = lane < NODES
    corner = jnp.where((place < 8) & (other >= 8), gram, 0.0)
    unit = jnp.where(place == other, 1.0, 0.0)
    mirrored = lax.dot_general(
        corner,
        unit,
        (((0,), (0,)), ((), ())),
        preferred_element_type=f32,
        precision=lax.Precision.HIGHEST,
    )
    gram = gram + mirrored[:NODES]

    def column(row):
        return jnp.sum(jnp.where(lane == place, row, 0.0), axis=1, keepdims=True)

    inverse_col = column(inverse_row)
    gram = gram * inverse_row * inverse_col
    size, weight = 1, jnp.ones((NODES, 1), f32)
    while size < NODES:
        mine = (place // size) == (other // size)
        sibling = (place // size) == ((other // size) ^ 1)
        own_col = jnp.sum(jnp.where(mine, gram, 0.0), axis=0, keepdims=True)
        cross_col = jnp.sum(jnp.where(sibling, gram, 0.0), axis=0, keepdims=True)
        here = mine & first
        own = jnp.sum(jnp.where(here, own_col, 0.0), axis=1, keepdims=True)
        cross = jnp.sum(jnp.where(here, cross_col, 0.0), axis=1, keepdims=True)
        coef = 1.0 - cross / (2.0 * (jnp.maximum(own, 0.0) + epsilon))
        coef_row = jnp.sum(jnp.where(place == other, coef, 0.0), axis=0, keepdims=True)
        gram = gram * coef * coef_row
        weight = weight * coef
        size *= 2
    weight = weight * inverse_col
    combined = None
    for node in range(NODES):
        term = weight[node : node + 1, :] * nodes_ref[node]
        combined = term if combined is None else combined + term
    out_ref[...] = combined


def local(pre_act, out_weight, out_grad):
    tokens, hidden = pre_act.shape
    width = out_weight.shape[1]
    mp = ("x", "c")
    hi = ("y", "zh")
    peers = lax.axis_size(mp)
    spot = jnp.stack([lax.axis_index(axis) for axis in ("zl", "x", "c")]).astype(jnp.int32)
    me = spot[:1]
    node = lax.axis_index(hi).astype(jnp.int32).reshape(1)
    quarter = hidden // LEAVES
    along = lax.axis_size("x")

    def swapped(value, axis, apart):
        return lax.ppermute(value, axis, [(i, i ^ apart) for i in range(lax.axis_size(axis))])

    copies, *dealt = deal(me, pre_act, out_grad)
    acts = {0: dealt[0]}
    for k in (3, 2, 1):
        acts[k] = swapped(dealt[k], "zl", k)
    shards = lax.all_to_all(copies, "zl", split_axis=0, concat_axis=0, tiled=True)
    grads = from_everyone(shards, mp)
    arrived = pl.pallas_call(
        arrived_kernel,
        out_shape=jax.ShapeDtypeStruct((8, 128), f32),
        in_specs=[ANY] * (LEAVES - 1),
        compiler_params=pltpu.CompilerParams(vmem_limit_bytes=1024 * 1024),
        cost_estimate=pl.CostEstimate(flops=10**11, bytes_accessed=0, transcendentals=0),
    )(acts[3], acts[2], acts[1])

    leaf_shape = jax.ShapeDtypeStruct((quarter, width), f32)
    group = ("zl", *mp)
    *leaves, sums = call(
        first_gram_kernel,
        [leaf_shape] * LEAVES + [jax.ShapeDtypeStruct((LEAVES * peers, 1, 128), f32)],
        [SMEM, VMEM, VMEM] + [VMEM] * LEAVES,
        flops=2 * tokens * hidden * width,
        size=16 * quarter * width,
    )(spot, grads, arrived, *[acts[k] for k in range(LEAVES)])
    sums = lax.all_to_all(sums, group, split_axis=0, concat_axis=0, tiled=True)
    scaled, inverse = call(
        first_merge_kernel,
        [leaf_shape, jax.ShapeDtypeStruct((8, 128), f32)],
        [SMEM] + [VMEM] * (LEAVES + 1),
        flops=8 * quarter * width,
        size=20 * quarter * width,
    )(me, sums, *leaves)

    half = jax.ShapeDtypeStruct((along, tokens // peers, width), f32)
    mine, theirs = call(
        project_kernel,
        [half, half],
        [SMEM, VMEM, VMEM, VMEM],
        flops=2 * tokens * hidden * width,
        size=4 * tokens * hidden,
        scratch=[pltpu.VMEM((along, 2, tokens // peers, width), f32)],
    )(spot, pre_act, out_weight, inverse)
    both = mine + swapped(theirs, "c", 1)
    projected = both[0]
    for k in range(1, along):
        projected = projected + swapped(both[k], "x", k)
    projected = projected.astype(bf16)

    rows = quarter // NODES
    sent = scaled.astype(jnp.float16).reshape(NODES, rows, width)
    nodes = lax.all_to_all(sent, hi, split_axis=0, concat_axis=0, tiled=True).astype(f32)
    share = 1.0 / (LEAVES * peers)
    sums = call(
        functools.partial(second_gram_kernel, peers, share),
        jax.ShapeDtypeStruct((peers, 2, 128), f32),
        [SMEM, VMEM, VMEM, VMEM],
        flops=8 * quarter * quarter * width,
        size=4 * quarter * width,
    )(node, nodes.reshape(quarter, width), inverse, projected)
    sums = lax.all_to_all(sums, mp, split_axis=0, concat_axis=0, tiled=True)
    dp = ("y", "zh", "zl")
    sums = call(pass_on_kernel, jax.ShapeDtypeStruct((LEAVES * NODES, 2, 128), f32), [VMEM])(sums)
    sums = lax.all_to_all(sums, dp, split_axis=0, concat_axis=0, tiled=True)
    combined = call(
        second_merge_kernel,
        jax.ShapeDtypeStruct((rows, width), f32),
        [VMEM, VMEM],
        flops=2 * quarter * width,
        size=4 * quarter * width,
    )(sums, nodes)
    return projected, combined


def solution(mesh):
    devices = mesh.devices.reshape(4, 4, LEAVES, 4, 2)
    finer = Mesh(devices, ("y", "zh", "zl", "x", "c"))
    dp, mp = ("y", "zh", "zl"), ("x", "c")
    return jax.shard_map(
        local,
        mesh=finer,
        in_specs=(P(dp, mp), P(mp, None), P((*dp, *mp), None)),
        out_specs=(P((*dp, *mp), None), P((*mp, *dp), None)),
        check_vma=False,
    )
```

```python
import functools

import jax
import jax.numpy as jnp
from jax import lax
from jax.experimental import pallas as pl
from jax.experimental.pallas import tpu as pltpu
from jax.sharding import Mesh, PartitionSpec as P

epsilon = 1e-06
LEAVES = 4
NODES = 16
LIMIT = 24 * 1024 * 1024
TOP = 16384.0
FLOOR = 1e-15

f32 = jnp.float32
bf16 = jnp.bfloat16
SMEM = pl.BlockSpec(memory_space=pltpu.SMEM)
VMEM = pl.BlockSpec(memory_space=pltpu.VMEM)
ANY = pl.BlockSpec(memory_space=pl.ANY)


def call(kernel, out_shape, in_specs, flops=0, size=0, scratch=()):
    many = isinstance(out_shape, (list, tuple))
    return pl.pallas_call(
        kernel,
        out_shape=out_shape,
        in_specs=in_specs,
        out_specs=[VMEM] * len(out_shape) if many else VMEM,
        scratch_shapes=list(scratch),
        compiler_params=pltpu.CompilerParams(vmem_limit_bytes=LIMIT),
        cost_estimate=pl.CostEstimate(flops=flops, bytes_accessed=size, transcendentals=0),
    )


def from_everyone(array, axes):
    copies = jnp.broadcast_to(array, (lax.axis_size(axes), *array.shape))
    return lax.all_to_all(copies, axes, split_axis=0, concat_axis=0, tiled=True)


def deal_kernel(me_ref, pre_ref, *refs):
    out_refs, deal_ref = refs[:LEAVES], refs[LEAVES]
    width = pre_ref.shape[1]

    @pl.when(pl.program_id(0) == 0)
    def _():
        row = lax.broadcasted_iota(jnp.int32, (width, width), 0)
        col = lax.broadcasted_iota(jnp.int32, (width, width), 1)
        block = row >> 5
        place = (((block & 3) ^ me_ref[0]) << 7) + ((block >> 2) << 5) + (row & 31)
        deal_ref[...] = jnp.where(place == col, 1.0, 0.0).astype(bf16)

    part = jnp.maximum(pre_ref[...], jnp.zeros((), bf16))
    dealt = jnp.dot(part, deal_ref[...], preferred_element_type=f32).astype(bf16)
    for k in range(LEAVES):
        out_refs[k][...] = dealt[:, k * 128 : (k + 1) * 128]


def deal(me, pre_act):
    tokens, hidden = pre_act.shape
    group = 512
    return pl.pallas_call(
        deal_kernel,
        grid_spec=pltpu.PrefetchScalarGridSpec(
            num_scalar_prefetch=1,
            grid=(hidden // group,),
            in_specs=[pl.BlockSpec((tokens, group), lambda g, me: (0, g))],
            out_specs=[pl.BlockSpec((tokens, group // LEAVES), lambda g, me: (0, g))] * LEAVES,
            scratch_shapes=[pltpu.VMEM((group, group), bf16)],
        ),
        out_shape=[jax.ShapeDtypeStruct((tokens, hidden // LEAVES), bf16)] * LEAVES,
        compiler_params=pltpu.CompilerParams(vmem_limit_bytes=LIMIT),
        cost_estimate=pl.CostEstimate(
            flops=2 * tokens * hidden * group, bytes_accessed=4 * tokens * hidden, transcendentals=0
        ),
    )(me, pre_act)


def arrived_kernel(*refs):
    refs[-1][...] = jnp.zeros_like(refs[-1])


def project_kernel(spot_ref, pre_ref, weight_ref, late_ref, mine_ref, theirs_ref, held_ref):
    count = mine_ref.shape[0]
    x, core = spot_ref[1], spot_ref[2]
    act = jnp.maximum(pre_ref[...], jnp.zeros((), bf16))
    total = jnp.dot(act, weight_ref[...], preferred_element_type=f32)
    held_ref[...] = total.reshape(held_ref.shape)
    for k in range(count):
        mine_ref[k] = held_ref[x ^ k, core]
        theirs_ref[k] = held_ref[x ^ k, 1 - core]


def lanes_of(total):
    return total[:, :128] + total[:, 128:256] + total[:, 256:384] + total[:, 384:512]


def first_gram_kernel(spot_ref, grads_ref, late_ref, *refs):
    act_refs, held, out_ref = refs[:LEAVES], refs[LEAVES:-1], refs[-1]
    peers, _, rows, width = grads_ref.shape
    me = spot_ref[0]
    for k in range(LEAVES):
        out_grad = grads_ref[:, me ^ k].reshape(peers * rows, width)
        held[k][...] = lax.dot_general(
            act_refs[k][...], out_grad, (((0,), (0,)), ((), ())), preferred_element_type=f32
        )
    lane = lax.broadcasted_iota(jnp.int32, (1, 128), 1)
    whole = jnp.zeros((1, 128), f32)
    for a in range(LEAVES):
        for b in range(a, LEAVES):
            lanes = lanes_of(jnp.sum(held[a][...] * held[b][...], axis=0, keepdims=True))
            value = jnp.sum(lanes, axis=1, keepdims=True)
            here = lane == LEAVES * (a ^ me) + (b ^ me)
            if a != b:
                here = here | (lane == LEAVES * (b ^ me) + (a ^ me))
            whole = jnp.where(here, value, whole)
    for copy in range(out_ref.shape[0]):
        out_ref[copy] = whole


def tree(gram, count):
    coef = [None] * count
    weight = [jnp.ones_like(gram[0][0])] * count
    size = 1
    while size < count:
        for low in range(0, count, 2 * size):
            first, second = range(low, low + size), range(low + size, low + 2 * size)

            def inner(left, right):
                return sum(weight[i] * weight[j] * gram[i][j] for i in left for j in right)

            cross = inner(first, second)
            first_sq = jnp.maximum(inner(first, first), 0.0)
            second_sq = jnp.maximum(inner(second, second), 0.0)
            first_coef = 1.0 - cross / (2.0 * (first_sq + epsilon))
            second_coef = 1.0 - cross / (2.0 * (second_sq + epsilon))
            for i in first:
                coef[i] = weight[i] * first_coef
            for i in second:
                coef[i] = weight[i] * second_coef
        weight = list(coef)
        size *= 2
    return weight


def first_merge_kernel(me_ref, sums_ref, *refs):
    leaf_refs, node_ref, inverse_ref = refs[:LEAVES], refs[LEAVES], refs[LEAVES + 1]
    me = me_ref[0]
    total = jnp.sum(sums_ref[...], axis=0)
    lane = lax.broadcasted_iota(jnp.int32, total.shape, 1)
    gram = [
        [
            jnp.sum(jnp.where(lane == LEAVES * i + j, total, 0.0), axis=1, keepdims=True)
            for j in range(LEAVES)
        ]
        for i in range(LEAVES)
    ]
    coef = tree(gram, LEAVES)
    bound = sum(jnp.abs(coef[i]) * jnp.sqrt(gram[i][i]) for i in range(LEAVES))
    bound = jnp.maximum(bound, FLOOR)
    scale = TOP / bound
    inverse_ref[...] = jnp.broadcast_to(bound * (1.0 / TOP), inverse_ref.shape)
    merged = None
    for k in range(LEAVES):
        mine = coef[k]
        for other in range(1, LEAVES):
            mine = jnp.where(me == other, coef[k ^ other], mine)
        term = (mine * scale) * leaf_refs[k][...]
        merged = term if merged is None else merged + term
    node_ref[...] = merged


def second_gram_kernel(copies, share, node_ref, nodes_ref, inverse_ref, late_ref, out_ref):
    node = node_ref[0]
    total, width = nodes_ref.shape
    rows = total // NODES
    held = nodes_ref[...]
    high = held.astype(bf16)
    low = (held - high.astype(f32)).astype(bf16)
    last = (((1,), (1,)), ((), ()))
    products = (
        lax.dot_general(high, high, last, preferred_element_type=f32)
        + lax.dot_general(high, low, last, preferred_element_type=f32)
        + lax.dot_general(low, high, last, preferred_element_type=f32)
        + lax.dot_general(low, low, last, preferred_element_type=f32)
    )
    row = lax.broadcasted_iota(jnp.int32, (total, total), 0)
    col = lax.broadcasted_iota(jnp.int32, (total, total), 1)
    products = jnp.where((row & (rows - 1)) == (col & (rows - 1)), products, 0.0)
    by_node = jnp.sum(products.reshape(NODES, rows, total), axis=1)
    source = lax.broadcasted_iota(jnp.int32, (total, 128), 0)
    lane = lax.broadcasted_iota(jnp.int32, (total, 128), 1)
    spread = jnp.where(source // rows == (lane & (NODES - 1)), 1.0, 0.0)
    gram = jnp.dot(by_node, spread, preferred_element_type=f32, precision=lax.Precision.HIGHEST)
    place = lax.broadcasted_iota(jnp.int32, (NODES, 128), 0)
    lane = lax.broadcasted_iota(jnp.int32, (NODES, 128), 1)
    packed = jnp.where(lane // NODES == (place & 7), gram, 0.0)
    lane = lane[:1]
    upper = jnp.sum(packed[:8], axis=0, keepdims=True)
    lower = jnp.sum(packed[8:], axis=0, keepdims=True)
    inverse = jnp.where(lane == (node & 7) + 2 * (node & 8), inverse_ref[:1] * share, 0.0)
    lower = jnp.where((lane & (NODES - 1)) < 8, inverse, lower)
    whole = jnp.concatenate([upper, lower], axis=0)
    for copy in range(copies):
        out_ref[copy] = whole


def pass_on_kernel(sums_ref, out_ref):
    whole = jnp.sum(sums_ref[...], axis=0)
    for copy in range(out_ref.shape[0]):
        out_ref[copy] = whole


def second_merge_kernel(sums_ref, nodes_ref, out_ref):
    total = jnp.sum(sums_ref[...], axis=0)
    place = lax.broadcasted_iota(jnp.int32, (NODES, 128), 0)
    lane = lax.broadcasted_iota(jnp.int32, (NODES, 128), 1)
    gram = jnp.where(place < 8, total[0:1], total[1:2])
    gram = jnp.where(lane // NODES == (place & 7), gram, 0.0)
    free = (lane & 8) == 0
    gram = jnp.where((place >= 8) & free, 0.0, gram)
    inverse_row = jnp.where((lane[:1] < NODES) & free[:1], total[1:2], 0.0)
    second = jnp.where((lane[:1] >= NODES) & (lane[:1] < NODES + 8), total[1:2], 0.0)
    inverse_row = inverse_row + pltpu.roll(second, 128 - 8, 1)
    for turn in (16, 32, 64):
        gram = gram + pltpu.roll(gram, turn, 1)
        inverse_row = inverse_row + pltpu.roll(inverse_row, turn, 1)
    other = lane & (NODES - 1)
    first = lane < NODES
    corner = jnp.where((place < 8) & (other >= 8), gram, 0.0)
    unit = jnp.where(place == other, 1.0, 0.0)
    mirrored = lax.dot_general(
        corner,
        unit,
        (((0,), (0,)), ((), ())),
        preferred_element_type=f32,
        precision=lax.Precision.HIGHEST,
    )
    gram = gram + mirrored[:NODES]

    def column(row):
        return jnp.sum(jnp.where(lane == place, row, 0.0), axis=1, keepdims=True)

    inverse_col = column(inverse_row)
    gram = gram * inverse_row * inverse_col
    size, weight = 1, jnp.ones((NODES, 1), f32)
    while size < NODES:
        mine = (place // size) == (other // size)
        sibling = (place // size) == ((other // size) ^ 1)
        own_col = jnp.sum(jnp.where(mine, gram, 0.0), axis=0, keepdims=True)
        cross_col = jnp.sum(jnp.where(sibling, gram, 0.0), axis=0, keepdims=True)
        here = mine & first
        own = jnp.sum(jnp.where(here, own_col, 0.0), axis=1, keepdims=True)
        cross = jnp.sum(jnp.where(here, cross_col, 0.0), axis=1, keepdims=True)
        coef = 1.0 - cross / (2.0 * (jnp.maximum(own, 0.0) + epsilon))
        coef_row = jnp.sum(jnp.where(place == other, coef, 0.0), axis=0, keepdims=True)
        gram = gram * coef * coef_row
        weight = weight * coef
        size *= 2
    weight = weight * inverse_col
    combined = None
    for node in range(NODES):
        term = weight[node : node + 1, :] * nodes_ref[node]
        combined = term if combined is None else combined + term
    out_ref[...] = combined


def local(pre_act, out_weight, out_grad):
    tokens, hidden = pre_act.shape
    width = out_weight.shape[1]
    mp = ("x", "c")
    hi = ("y", "zh")
    peers = lax.axis_size(mp)
    spot = jnp.stack([lax.axis_index(axis) for axis in ("zl", "x", "c")]).astype(jnp.int32)
    me = spot[:1]
    node = lax.axis_index(hi).astype(jnp.int32).reshape(1)
    quarter = hidden // LEAVES
    along = lax.axis_size("x")

    def swapped(value, axis, apart):
        return lax.ppermute(value, axis, [(i, i ^ apart) for i in range(lax.axis_size(axis))])

    shards = from_everyone(out_grad, "zl")
    grads = from_everyone(shards, mp)
    dealt = deal(me, pre_act)
    acts = {0: dealt[0]}
    for k in (3, 2, 1):
        acts[k] = swapped(dealt[k], "zl", k)
    arrived = pl.pallas_call(
        arrived_kernel,
        out_shape=jax.ShapeDtypeStruct((8, 128), f32),
        in_specs=[ANY] * (LEAVES - 1),
        compiler_params=pltpu.CompilerParams(vmem_limit_bytes=1024 * 1024),
        cost_estimate=pl.CostEstimate(flops=10**11, bytes_accessed=0, transcendentals=0),
    )(acts[3], acts[2], acts[1])

    leaf_shape = jax.ShapeDtypeStruct((quarter, width), f32)
    group = ("zl", *mp)
    *leaves, sums = call(
        first_gram_kernel,
        [leaf_shape] * LEAVES + [jax.ShapeDtypeStruct((LEAVES * peers, 1, 128), f32)],
        [SMEM, VMEM, VMEM] + [VMEM] * LEAVES,
        flops=2 * tokens * hidden * width,
        size=16 * quarter * width,
    )(spot, grads, arrived, *[acts[k] for k in range(LEAVES)])
    sums = lax.all_to_all(sums, group, split_axis=0, concat_axis=0, tiled=True)
    scaled, inverse = call(
        first_merge_kernel,
        [leaf_shape, jax.ShapeDtypeStruct((8, 128), f32)],
        [SMEM] + [VMEM] * (LEAVES + 1),
        flops=8 * quarter * width,
        size=20 * quarter * width,
    )(me, sums, *leaves)

    half = jax.ShapeDtypeStruct((along, tokens // peers, width), f32)
    mine, theirs = call(
        project_kernel,
        [half, half],
        [SMEM, VMEM, VMEM, VMEM],
        flops=2 * tokens * hidden * width,
        size=4 * tokens * hidden,
        scratch=[pltpu.VMEM((along, 2, tokens // peers, width), f32)],
    )(spot, pre_act, out_weight, inverse)
    both = mine + swapped(theirs, "c", 1)
    projected = both[0]
    for k in range(1, along):
        projected = projected + swapped(both[k], "x", k)
    projected = projected.astype(bf16)

    rows = quarter // NODES
    sent = scaled.astype(jnp.float16).reshape(NODES, rows, width)
    nodes = lax.all_to_all(sent, hi, split_axis=0, concat_axis=0, tiled=True).astype(f32)
    share = 1.0 / (LEAVES * peers)
    sums = call(
        functools.partial(second_gram_kernel, peers, share),
        jax.ShapeDtypeStruct((peers, 2, 128), f32),
        [SMEM, VMEM, VMEM, VMEM],
        flops=8 * quarter * quarter * width,
        size=4 * quarter * width,
    )(node, nodes.reshape(quarter, width), inverse, projected)
    sums = lax.all_to_all(sums, mp, split_axis=0, concat_axis=0, tiled=True)
    dp = ("y", "zh", "zl")
    sums = call(pass_on_kernel, jax.ShapeDtypeStruct((LEAVES * NODES, 2, 128), f32), [VMEM])(sums)
    sums = lax.all_to_all(sums, dp, split_axis=0, concat_axis=0, tiled=True)
    combined = call(
        second_merge_kernel,
        jax.ShapeDtypeStruct((rows, width), f32),
        [VMEM, VMEM],
        flops=2 * quarter * width,
        size=4 * quarter * width,
    )(sums, nodes)
    return projected, combined


def solution(mesh):
    devices = mesh.devices.reshape(4, 4, LEAVES, 4, 2)
    finer = Mesh(devices, ("y", "zh", "zl", "x", "c"))
    dp, mp = ("y", "zh", "zl"), ("x", "c")
    return jax.shard_map(
        local,
        mesh=finer,
        in_specs=(P(dp, mp), P(mp, None), P((*dp, *mp), None)),
        out_specs=(P((*dp, *mp), None), P((*mp, *dp), None)),
        check_vma=False,
    )
```

```python
import functools

import jax
import jax.numpy as jnp
from jax import lax
from jax.experimental import pallas as pl
from jax.experimental.pallas import tpu as pltpu
from jax.sharding import Mesh, PartitionSpec as P

epsilon = 1e-06
LEAVES = 4
NODES = 16
LIMIT = 24 * 1024 * 1024
TOP = 16384.0
FLOOR = 1e-15

f32 = jnp.float32
bf16 = jnp.bfloat16
SMEM = pl.BlockSpec(memory_space=pltpu.SMEM)
VMEM = pl.BlockSpec(memory_space=pltpu.VMEM)
ANY = pl.BlockSpec(memory_space=pl.ANY)


def call(kernel, out_shape, in_specs, flops=0, size=0, scratch=()):
    many = isinstance(out_shape, (list, tuple))
    return pl.pallas_call(
        kernel,
        out_shape=out_shape,
        in_specs=in_specs,
        out_specs=[VMEM] * len(out_shape) if many else VMEM,
        scratch_shapes=list(scratch),
        compiler_params=pltpu.CompilerParams(vmem_limit_bytes=LIMIT),
        cost_estimate=pl.CostEstimate(flops=flops, bytes_accessed=size, transcendentals=0),
    )


def from_everyone(array, axes):
    copies = jnp.broadcast_to(array, (lax.axis_size(axes), *array.shape))
    return lax.all_to_all(copies, axes, split_axis=0, concat_axis=0, tiled=True)


def deal_kernel(me_ref, pre_ref, *refs):
    out_refs, deal_ref = refs[:LEAVES], refs[LEAVES]
    width = pre_ref.shape[1]

    @pl.when(pl.program_id(0) == 0)
    def _():
        row = lax.broadcasted_iota(jnp.int32, (width, width), 0)
        col = lax.broadcasted_iota(jnp.int32, (width, width), 1)
        block = row >> 5
        place = (((block & 3) ^ me_ref[0]) << 7) + ((block >> 2) << 5) + (row & 31)
        deal_ref[...] = jnp.where(place == col, 1.0, 0.0).astype(bf16)

    part = jnp.maximum(pre_ref[...], jnp.zeros((), bf16))
    dealt = jnp.dot(part, deal_ref[...], preferred_element_type=f32).astype(bf16)
    for k in range(LEAVES):
        out_refs[k][...] = dealt[:, k * 128 : (k + 1) * 128]


def deal(me, pre_act):
    tokens, hidden = pre_act.shape
    group = 512
    return pl.pallas_call(
        deal_kernel,
        grid_spec=pltpu.PrefetchScalarGridSpec(
            num_scalar_prefetch=1,
            grid=(hidden // group,),
            in_specs=[pl.BlockSpec((tokens, group), lambda g, me: (0, g))],
            out_specs=[pl.BlockSpec((tokens, group // LEAVES), lambda g, me: (0, g))] * LEAVES,
            scratch_shapes=[pltpu.VMEM((group, group), bf16)],
        ),
        out_shape=[jax.ShapeDtypeStruct((tokens, hidden // LEAVES), bf16)] * LEAVES,
        compiler_params=pltpu.CompilerParams(vmem_limit_bytes=LIMIT),
        cost_estimate=pl.CostEstimate(
            flops=2 * tokens * hidden * group, bytes_accessed=4 * tokens * hidden, transcendentals=0
        ),
    )(me, pre_act)


def arrived_kernel(*refs):
    refs[-1][...] = jnp.zeros_like(refs[-1])


def project_kernel(spot_ref, pre_ref, weight_ref, late_ref, mine_ref, theirs_ref, held_ref):
    count = mine_ref.shape[0]
    x, core = spot_ref[1], spot_ref[2]
    rows, width = mine_ref.shape[1:]

    def step(at, carry):
        here = pl.ds(pl.multiple_of(at * 2 * rows, 2 * rows), 2 * rows)
        act = jnp.maximum(pre_ref[here, :], jnp.zeros((), bf16))
        total = jnp.dot(act, weight_ref[...], preferred_element_type=f32)
        held_ref[at] = total.reshape(2, rows, width)
        return carry

    lax.fori_loop(0, count, step, 0)
    for k in range(count):
        mine_ref[k] = held_ref[x ^ k, core]
        theirs_ref[k] = held_ref[x ^ k, 1 - core]


def lanes_of(total):
    return total[:, :128] + total[:, 128:256] + total[:, 256:384] + total[:, 384:512]


def first_gram_kernel(spot_ref, grads_ref, late_ref, *refs):
    act_refs, leaf_refs, out_ref = refs[:LEAVES], refs[LEAVES:-1], refs[-1]
    peers, _, rows, width = grads_ref.shape
    me = spot_ref[0]
    block = 128
    pairs = [(a, b) for a in range(LEAVES) for b in range(a, LEAVES)]

    def step(at, totals):
        here = pl.ds(pl.multiple_of(at * block, block), block)
        leaves = []
        for k in range(LEAVES):
            out_grad = grads_ref[:, me ^ k].reshape(peers * rows, width)
            leaf = lax.dot_general(
                act_refs[k][:, here], out_grad, (((0,), (0,)), ((), ())), preferred_element_type=f32
            )
            leaf_refs[k][here, :] = leaf
            leaves.append(leaf)
        added = []
        for total, (a, b) in zip(totals, pairs):
            product = jnp.sum((leaves[a] * leaves[b]).reshape(-1, 8, width), axis=0)
            added.append(total + lanes_of(product))
        return tuple(added)

    totals = lax.fori_loop(
        0, leaf_refs[0].shape[0] // block, step, tuple(jnp.zeros((8, 128), f32) for _ in pairs)
    )
    lane = lax.broadcasted_iota(jnp.int32, (1, 128), 1)
    whole = jnp.zeros((1, 128), f32)
    for total, (a, b) in zip(totals, pairs):
        value = jnp.sum(jnp.sum(total, axis=0, keepdims=True), axis=1, keepdims=True)
        here = lane == LEAVES * (a ^ me) + (b ^ me)
        if a != b:
            here = here | (lane == LEAVES * (b ^ me) + (a ^ me))
        whole = jnp.where(here, value, whole)
    for copy in range(out_ref.shape[0]):
        out_ref[copy] = whole


def tree(gram, count):
    coef = [None] * count
    weight = [jnp.ones_like(gram[0][0])] * count
    size = 1
    while size < count:
        for low in range(0, count, 2 * size):
            first, second = range(low, low + size), range(low + size, low + 2 * size)

            def inner(left, right):
                return sum(weight[i] * weight[j] * gram[i][j] for i in left for j in right)

            cross = inner(first, second)
            first_sq = jnp.maximum(inner(first, first), 0.0)
            second_sq = jnp.maximum(inner(second, second), 0.0)
            first_coef = 1.0 - cross / (2.0 * (first_sq + epsilon))
            second_coef = 1.0 - cross / (2.0 * (second_sq + epsilon))
            for i in first:
                coef[i] = weight[i] * first_coef
            for i in second:
                coef[i] = weight[i] * second_coef
        weight = list(coef)
        size *= 2
    return weight


def first_merge_kernel(me_ref, sums_ref, *refs):
    leaf_refs, node_ref, inverse_ref = refs[:LEAVES], refs[LEAVES], refs[LEAVES + 1]
    me = me_ref[0]
    total = jnp.sum(sums_ref[...], axis=0)
    lane = lax.broadcasted_iota(jnp.int32, total.shape, 1)
    gram = [
        [
            jnp.sum(jnp.where(lane == LEAVES * i + j, total, 0.0), axis=1, keepdims=True)
            for j in range(LEAVES)
        ]
        for i in range(LEAVES)
    ]
    coef = tree(gram, LEAVES)
    bound = sum(jnp.abs(coef[i]) * jnp.sqrt(gram[i][i]) for i in range(LEAVES))
    bound = jnp.maximum(bound, FLOOR)
    scale = TOP / bound
    inverse_ref[...] = jnp.broadcast_to(bound * (1.0 / TOP), inverse_ref.shape)
    merged = None
    for k in range(LEAVES):
        mine = coef[k]
        for other in range(1, LEAVES):
            mine = jnp.where(me == other, coef[k ^ other], mine)
        term = (mine * scale) * leaf_refs[k][...]
        merged = term if merged is None else merged + term
    node_ref[...] = merged


def second_gram_kernel(copies, share, node_ref, nodes_ref, inverse_ref, late_ref, out_ref, by_node_ref):
    node = node_ref[0]
    total, width = nodes_ref.shape
    rows = total // NODES
    held = nodes_ref[...]
    high = held.astype(bf16)
    low = (held - high.astype(f32)).astype(bf16)
    last = (((1,), (1,)), ((), ()))
    some = 8 * rows

    def step(at, carry):
        here = pl.ds(pl.multiple_of(at * some, some), some)
        part = nodes_ref[here, :]
        part_high = part.astype(bf16)
        part_low = (part - part_high.astype(f32)).astype(bf16)
        products = (
            lax.dot_general(part_high, high, last, preferred_element_type=f32)
            + lax.dot_general(part_high, low, last, preferred_element_type=f32)
            + lax.dot_general(part_low, high, last, preferred_element_type=f32)
            + lax.dot_general(part_low, low, last, preferred_element_type=f32)
        )
        row = lax.broadcasted_iota(jnp.int32, (some, total), 0)
        col = lax.broadcasted_iota(jnp.int32, (some, total), 1)
        products = jnp.where((row & (rows - 1)) == (col & (rows - 1)), products, 0.0)
        found = jnp.sum(products.reshape(8, rows, total), axis=1)
        by_node_ref[pl.ds(pl.multiple_of(at * 8, 8), 8), :] = found
        return carry

    lax.fori_loop(0, total // some, step, 0)
    by_node = by_node_ref[...]
    source = lax.broadcasted_iota(jnp.int32, (total, 128), 0)
    lane = lax.broadcasted_iota(jnp.int32, (total, 128), 1)
    spread = jnp.where(source // rows == (lane & (NODES - 1)), 1.0, 0.0)
    gram = jnp.dot(by_node, spread, preferred_element_type=f32, precision=lax.Precision.HIGHEST)
    place = lax.broadcasted_iota(jnp.int32, (NODES, 128), 0)
    lane = lax.broadcasted_iota(jnp.int32, (NODES, 128), 1)
    packed = jnp.where(lane // NODES == (place & 7), gram, 0.0)
    lane = lane[:1]
    upper = jnp.sum(packed[:8], axis=0, keepdims=True)
    lower = jnp.sum(packed[8:], axis=0, keepdims=True)
    inverse = jnp.where(lane == (node & 7) + 2 * (node & 8), inverse_ref[:1] * share, 0.0)
    lower = jnp.where((lane & (NODES - 1)) < 8, inverse, lower)
    whole = jnp.concatenate([upper, lower], axis=0)
    for copy in range(copies):
        out_ref[copy] = whole


def pass_on_kernel(sums_ref, out_ref):
    whole = jnp.sum(sums_ref[...], axis=0)
    for copy in range(out_ref.shape[0]):
        out_ref[copy] = whole


def second_merge_kernel(sums_ref, nodes_ref, out_ref):
    total = jnp.sum(sums_ref[...], axis=0)
    place = lax.broadcasted_iota(jnp.int32, (NODES, 128), 0)
    lane = lax.broadcasted_iota(jnp.int32, (NODES, 128), 1)
    gram = jnp.where(place < 8, total[0:1], total[1:2])
    gram = jnp.where(lane // NODES == (place & 7), gram, 0.0)
    free = (lane & 8) == 0
    gram = jnp.where((place >= 8) & free, 0.0, gram)
    inverse_row = jnp.where((lane[:1] < NODES) & free[:1], total[1:2], 0.0)
    second = jnp.where((lane[:1] >= NODES) & (lane[:1] < NODES + 8), total[1:2], 0.0)
    inverse_row = inverse_row + pltpu.roll(second, 128 - 8, 1)
    for turn in (16, 32, 64):
        gram = gram + pltpu.roll(gram, turn, 1)
        inverse_row = inverse_row + pltpu.roll(inverse_row, turn, 1)
    other = lane & (NODES - 1)
    first = lane < NODES
    corner = jnp.where((place < 8) & (other >= 8), gram, 0.0)
    unit = jnp.where(place == other, 1.0, 0.0)
    mirrored = lax.dot_general(
        corner,
        unit,
        (((0,), (0,)), ((), ())),
        preferred_element_type=f32,
        precision=lax.Precision.HIGHEST,
    )
    gram = gram + mirrored[:NODES]

    def column(row):
        return jnp.sum(jnp.where(lane == place, row, 0.0), axis=1, keepdims=True)

    inverse_col = column(inverse_row)
    gram = gram * inverse_row * inverse_col
    size, weight = 1, jnp.ones((NODES, 1), f32)
    while size < NODES:
        mine = (place // size) == (other // size)
        sibling = (place // size) == ((other // size) ^ 1)
        own_col = jnp.sum(jnp.where(mine, gram, 0.0), axis=0, keepdims=True)
        cross_col = jnp.sum(jnp.where(sibling, gram, 0.0), axis=0, keepdims=True)
        here = mine & first
        own = jnp.sum(jnp.where(here, own_col, 0.0), axis=1, keepdims=True)
        cross = jnp.sum(jnp.where(here, cross_col, 0.0), axis=1, keepdims=True)
        coef = 1.0 - cross / (2.0 * (jnp.maximum(own, 0.0) + epsilon))
        coef_row = jnp.sum(jnp.where(place == other, coef, 0.0), axis=0, keepdims=True)
        gram = gram * coef * coef_row
        weight = weight * coef
        size *= 2
    weight = weight * inverse_col
    combined = None
    for node in range(NODES):
        term = weight[node : node + 1, :] * nodes_ref[node]
        combined = term if combined is None else combined + term
    out_ref[...] = combined


def local(pre_act, out_weight, out_grad):
    tokens, hidden = pre_act.shape
    width = out_weight.shape[1]
    mp = ("x", "c")
    hi = ("y", "zh")
    peers = lax.axis_size(mp)
    spot = jnp.stack([lax.axis_index(axis) for axis in ("zl", "x", "c")]).astype(jnp.int32)
    me = spot[:1]
    node = lax.axis_index(hi).astype(jnp.int32).reshape(1)
    quarter = hidden // LEAVES
    along = lax.axis_size("x")

    def swapped(value, axis, apart):
        return lax.ppermute(value, axis, [(i, i ^ apart) for i in range(lax.axis_size(axis))])

    shards = from_everyone(out_grad, "zl")
    grads = from_everyone(shards, mp)
    dealt = deal(me, pre_act)
    acts = {0: dealt[0]}
    for k in (2, 3, 1):
        acts[k] = swapped(dealt[k], "zl", k)
    arrived = pl.pallas_call(
        arrived_kernel,
        out_shape=jax.ShapeDtypeStruct((8, 128), f32),
        in_specs=[ANY] * (LEAVES - 1),
        compiler_params=pltpu.CompilerParams(vmem_limit_bytes=1024 * 1024),
        cost_estimate=pl.CostEstimate(flops=10**11, bytes_accessed=0, transcendentals=0),
    )(acts[2], acts[3], acts[1])

    leaf_shape = jax.ShapeDtypeStruct((quarter, width), f32)
    group = ("zl", *mp)
    *leaves, sums = call(
        first_gram_kernel,
        [leaf_shape] * LEAVES + [jax.ShapeDtypeStruct((LEAVES * peers, 1, 128), f32)],
        [SMEM, VMEM, VMEM] + [VMEM] * LEAVES,
        flops=2 * tokens * hidden * width,
        size=16 * quarter * width,
    )(spot, grads, arrived, *[acts[k] for k in range(LEAVES)])
    sums = lax.all_to_all(sums, group, split_axis=0, concat_axis=0, tiled=True)
    scaled, inverse = call(
        first_merge_kernel,
        [leaf_shape, jax.ShapeDtypeStruct((8, 128), f32)],
        [SMEM] + [VMEM] * (LEAVES + 1),
        flops=8 * quarter * width,
        size=20 * quarter * width,
    )(me, sums, *leaves)

    half = jax.ShapeDtypeStruct((along, tokens // peers, width), f32)
    mine, theirs = call(
        project_kernel,
        [half, half],
        [SMEM, VMEM, VMEM, VMEM],
        flops=2 * tokens * hidden * width,
        size=4 * tokens * hidden,
        scratch=[pltpu.VMEM((along, 2, tokens // peers, width), f32)],
    )(spot, pre_act, out_weight, inverse)
    both = mine + swapped(theirs, "c", 1)
    projected = both[0]
    for k in range(1, along):
        projected = projected + swapped(both[k], "x", k)
    projected = projected.astype(bf16)

    rows = quarter // NODES
    sent = scaled.astype(jnp.float16).reshape(NODES, rows, width)
    nodes = lax.all_to_all(sent, hi, split_axis=0, concat_axis=0, tiled=True).astype(f32)
    share = 1.0 / (LEAVES * peers)
    sums = call(
        functools.partial(second_gram_kernel, peers * along, share),
        jax.ShapeDtypeStruct((peers * along, 2, 128), f32),
        [SMEM, VMEM, VMEM, VMEM],
        flops=8 * quarter * quarter * width,
        size=4 * quarter * width,
        scratch=[pltpu.VMEM((NODES, quarter), f32)],
    )(node, nodes.reshape(quarter, width), inverse, projected)
    sums = lax.all_to_all(sums, ("y", *mp), split_axis=0, concat_axis=0, tiled=True)
    sums = call(pass_on_kernel, jax.ShapeDtypeStruct((NODES, 2, 128), f32), [VMEM])(sums)
    sums = lax.all_to_all(sums, ("zh", "zl"), split_axis=0, concat_axis=0, tiled=True)
    combined = call(
        second_merge_kernel,
        jax.ShapeDtypeStruct((rows, width), f32),
        [VMEM, VMEM],
        flops=2 * quarter * width,
        size=4 * quarter * width,
    )(sums, nodes)
    return projected, combined


def solution(mesh):
    devices = mesh.devices.reshape(4, 4, LEAVES, 4, 2)
    finer = Mesh(devices, ("y", "zh", "zl", "x", "c"))
    dp, mp = ("y", "zh", "zl"), ("x", "c")
    return jax.shard_map(
        local,
        mesh=finer,
        in_specs=(P(dp, mp), P(mp, None), P((*dp, *mp), None)),
        out_specs=(P((*dp, *mp), None), P((*mp, *dp), None)),
        check_vma=False,
    )
```

```python
import functools

import jax
import jax.numpy as jnp
from jax import lax
from jax.experimental import pallas as pl
from jax.experimental.pallas import tpu as pltpu
from jax.sharding import Mesh, PartitionSpec as P

epsilon = 1e-06
LEAVES = 4
NODES = 16
LIMIT = 24 * 1024 * 1024
TOP = 16384.0
FLOOR = 1e-15

f32 = jnp.float32
bf16 = jnp.bfloat16
SMEM = pl.BlockSpec(memory_space=pltpu.SMEM)
VMEM = pl.BlockSpec(memory_space=pltpu.VMEM)
ANY = pl.BlockSpec(memory_space=pl.ANY)


def call(kernel, out_shape, in_specs, flops=0, size=0, scratch=()):
    many = isinstance(out_shape, (list, tuple))
    return pl.pallas_call(
        kernel,
        out_shape=out_shape,
        in_specs=in_specs,
        out_specs=[VMEM] * len(out_shape) if many else VMEM,
        scratch_shapes=list(scratch),
        compiler_params=pltpu.CompilerParams(vmem_limit_bytes=LIMIT),
        cost_estimate=pl.CostEstimate(flops=flops, bytes_accessed=size, transcendentals=0),
    )


def from_everyone(array, axes):
    copies = jnp.broadcast_to(array, (lax.axis_size(axes), *array.shape))
    return lax.all_to_all(copies, axes, split_axis=0, concat_axis=0, tiled=True)


def deal_kernel(me_ref, pre_ref, *refs):
    out_refs, deal_ref = refs[:LEAVES], refs[LEAVES]
    width = pre_ref.shape[1]

    @pl.when(pl.program_id(0) == 0)
    def _():
        row = lax.broadcasted_iota(jnp.int32, (width, width), 0)
        col = lax.broadcasted_iota(jnp.int32, (width, width), 1)
        block = row >> 5
        place = (((block & 3) ^ me_ref[0]) << 7) + ((block >> 2) << 5) + (row & 31)
        deal_ref[...] = jnp.where(place == col, 1.0, 0.0).astype(bf16)

    part = jnp.maximum(pre_ref[...], jnp.zeros((), bf16))
    dealt = jnp.dot(part, deal_ref[...], preferred_element_type=f32).astype(bf16)
    for k in range(LEAVES):
        out_refs[k][...] = dealt[:, k * 128 : (k + 1) * 128]


def deal(me, pre_act):
    tokens, hidden = pre_act.shape
    group = 512
    return pl.pallas_call(
        deal_kernel,
        grid_spec=pltpu.PrefetchScalarGridSpec(
            num_scalar_prefetch=1,
            grid=(hidden // group,),
            in_specs=[pl.BlockSpec((tokens, group), lambda g, me: (0, g))],
            out_specs=[pl.BlockSpec((tokens, group // LEAVES), lambda g, me: (0, g))] * LEAVES,
            scratch_shapes=[pltpu.VMEM((group, group), bf16)],
        ),
        out_shape=[jax.ShapeDtypeStruct((tokens, hidden // LEAVES), bf16)] * LEAVES,
        compiler_params=pltpu.CompilerParams(vmem_limit_bytes=LIMIT),
        cost_estimate=pl.CostEstimate(
            flops=2 * tokens * hidden * group, bytes_accessed=4 * tokens * hidden, transcendentals=0
        ),
    )(me, pre_act)


def arrived_kernel(*refs):
    refs[-1][...] = jnp.zeros_like(refs[-1])


def project_kernel(spot_ref, weight_ref, late_ref, *refs):
    act_refs, (mine_ref, theirs_ref, held_ref) = refs[:LEAVES], refs[LEAVES:]
    count = mine_ref.shape[0]
    me, x, core = spot_ref[0], spot_ref[1], spot_ref[2]
    total = None
    for k in range(LEAVES):
        weight = weight_ref[:, me ^ k].reshape(act_refs[k].shape[1], -1)
        part = jnp.dot(act_refs[k][...], weight, preferred_element_type=f32)
        total = part if total is None else total + part
    held_ref[...] = total.reshape(held_ref.shape)
    for k in range(count):
        mine_ref[k] = held_ref[x ^ k, core]
        theirs_ref[k] = held_ref[x ^ k, 1 - core]


def lanes_of(total):
    return total[:, :128] + total[:, 128:256] + total[:, 256:384] + total[:, 384:512]


def first_gram_kernel(spot_ref, grads_ref, late_ref, *refs):
    act_refs, held, out_ref = refs[:LEAVES], refs[LEAVES:-1], refs[-1]
    peers, _, rows, width = grads_ref.shape
    me = spot_ref[0]
    for k in range(LEAVES):
        out_grad = grads_ref[:, me ^ k].reshape(peers * rows, width)
        held[k][...] = lax.dot_general(
            act_refs[k][...], out_grad, (((0,), (0,)), ((), ())), preferred_element_type=f32
        )
    lane = lax.broadcasted_iota(jnp.int32, (1, 128), 1)
    whole = jnp.zeros((1, 128), f32)
    for a in range(LEAVES):
        for b in range(a, LEAVES):
            lanes = lanes_of(jnp.sum(held[a][...] * held[b][...], axis=0, keepdims=True))
            value = jnp.sum(lanes, axis=1, keepdims=True)
            here = lane == LEAVES * (a ^ me) + (b ^ me)
            if a != b:
                here = here | (lane == LEAVES * (b ^ me) + (a ^ me))
            whole = jnp.where(here, value, whole)
    for copy in range(out_ref.shape[0]):
        out_ref[copy] = whole


def tree(gram, count):
    coef = [None] * count
    weight = [jnp.ones_like(gram[0][0])] * count
    size = 1
    while size < count:
        for low in range(0, count, 2 * size):
            first, second = range(low, low + size), range(low + size, low + 2 * size)

            def inner(left, right):
                return sum(weight[i] * weight[j] * gram[i][j] for i in left for j in right)

            cross = inner(first, second)
            first_sq = jnp.maximum(inner(first, first), 0.0)
            second_sq = jnp.maximum(inner(second, second), 0.0)
            first_coef = 1.0 - cross / (2.0 * (first_sq + epsilon))
            second_coef = 1.0 - cross / (2.0 * (second_sq + epsilon))
            for i in first:
                coef[i] = weight[i] * first_coef
            for i in second:
                coef[i] = weight[i] * second_coef
        weight = list(coef)
        size *= 2
    return weight


def first_merge_kernel(me_ref, sums_ref, *refs):
    leaf_refs, node_ref, inverse_ref = refs[:LEAVES], refs[LEAVES], refs[LEAVES + 1]
    me = me_ref[0]
    total = jnp.sum(sums_ref[...], axis=0)
    lane = lax.broadcasted_iota(jnp.int32, total.shape, 1)
    gram = [
        [
            jnp.sum(jnp.where(lane == LEAVES * i + j, total, 0.0), axis=1, keepdims=True)
            for j in range(LEAVES)
        ]
        for i in range(LEAVES)
    ]
    coef = tree(gram, LEAVES)
    bound = sum(jnp.abs(coef[i]) * jnp.sqrt(gram[i][i]) for i in range(LEAVES))
    bound = jnp.maximum(bound, FLOOR)
    scale = TOP / bound
    inverse_ref[...] = jnp.broadcast_to(bound * (1.0 / TOP), inverse_ref.shape)
    merged = None
    for k in range(LEAVES):
        mine = coef[k]
        for other in range(1, LEAVES):
            mine = jnp.where(me == other, coef[k ^ other], mine)
        term = (mine * scale) * leaf_refs[k][...]
        merged = term if merged is None else merged + term
    node_ref[...] = merged


def second_gram_kernel(copies, share, node_ref, nodes_ref, inverse_ref, late_ref, out_ref):
    node = node_ref[0]
    total, width = nodes_ref.shape
    rows = total // NODES
    held = nodes_ref[...]
    high = held.astype(bf16)
    low = (held - high.astype(f32)).astype(bf16)
    last = (((1,), (1,)), ((), ()))
    products = (
        lax.dot_general(high, high, last, preferred_element_type=f32)
        + lax.dot_general(high, low, last, preferred_element_type=f32)
        + lax.dot_general(low, high, last, preferred_element_type=f32)
        + lax.dot_general(low, low, last, preferred_element_type=f32)
    )
    row = lax.broadcasted_iota(jnp.int32, (total, total), 0)
    col = lax.broadcasted_iota(jnp.int32, (total, total), 1)
    products = jnp.where((row & (rows - 1)) == (col & (rows - 1)), products, 0.0)
    by_node = jnp.sum(products.reshape(NODES, rows, total), axis=1)
    source = lax.broadcasted_iota(jnp.int32, (total, 128), 0)
    lane = lax.broadcasted_iota(jnp.int32, (total, 128), 1)
    spread = jnp.where(source // rows == (lane & (NODES - 1)), 1.0, 0.0)
    gram = jnp.dot(by_node, spread, preferred_element_type=f32, precision=lax.Precision.HIGHEST)
    place = lax.broadcasted_iota(jnp.int32, (NODES, 128), 0)
    lane = lax.broadcasted_iota(jnp.int32, (NODES, 128), 1)
    packed = jnp.where(lane // NODES == (place & 7), gram, 0.0)
    lane = lane[:1]
    upper = jnp.sum(packed[:8], axis=0, keepdims=True)
    lower = jnp.sum(packed[8:], axis=0, keepdims=True)
    inverse = jnp.where(lane == (node & 7) + 2 * (node & 8), inverse_ref[:1] * share, 0.0)
    lower = jnp.where((lane & (NODES - 1)) < 8, inverse, lower)
    whole = jnp.concatenate([upper, lower], axis=0)
    for copy in range(copies):
        out_ref[copy] = whole


def pass_on_kernel(sums_ref, out_ref):
    whole = jnp.sum(sums_ref[...], axis=0)
    for copy in range(out_ref.shape[0]):
        out_ref[copy] = whole


def second_merge_kernel(sums_ref, nodes_ref, out_ref):
    total = jnp.sum(sums_ref[...], axis=0)
    place = lax.broadcasted_iota(jnp.int32, (NODES, 128), 0)
    lane = lax.broadcasted_iota(jnp.int32, (NODES, 128), 1)
    gram = jnp.where(place < 8, total[0:1], total[1:2])
    gram = jnp.where(lane // NODES == (place & 7), gram, 0.0)
    free = (lane & 8) == 0
    gram = jnp.where((place >= 8) & free, 0.0, gram)
    inverse_row = jnp.where((lane[:1] < NODES) & free[:1], total[1:2], 0.0)
    second = jnp.where((lane[:1] >= NODES) & (lane[:1] < NODES + 8), total[1:2], 0.0)
    inverse_row = inverse_row + pltpu.roll(second, 128 - 8, 1)
    for turn in (16, 32, 64):
        gram = gram + pltpu.roll(gram, turn, 1)
        inverse_row = inverse_row + pltpu.roll(inverse_row, turn, 1)
    other = lane & (NODES - 1)
    first = lane < NODES
    corner = jnp.where((place < 8) & (other >= 8), gram, 0.0)
    unit = jnp.where(place == other, 1.0, 0.0)
    mirrored = lax.dot_general(
        corner,
        unit,
        (((0,), (0,)), ((), ())),
        preferred_element_type=f32,
        precision=lax.Precision.HIGHEST,
    )
    gram = gram + mirrored[:NODES]

    def column(row):
        return jnp.sum(jnp.where(lane == place, row, 0.0), axis=1, keepdims=True)

    inverse_col = column(inverse_row)
    gram = gram * inverse_row * inverse_col
    size, weight = 1, jnp.ones((NODES, 1), f32)
    while size < NODES:
        mine = (place // size) == (other // size)
        sibling = (place // size) == ((other // size) ^ 1)
        own_col = jnp.sum(jnp.where(mine, gram, 0.0), axis=0, keepdims=True)
        cross_col = jnp.sum(jnp.where(sibling, gram, 0.0), axis=0, keepdims=True)
        here = mine & first
        own = jnp.sum(jnp.where(here, own_col, 0.0), axis=1, keepdims=True)
        cross = jnp.sum(jnp.where(here, cross_col, 0.0), axis=1, keepdims=True)
        coef = 1.0 - cross / (2.0 * (jnp.maximum(own, 0.0) + epsilon))
        coef_row = jnp.sum(jnp.where(place == other, coef, 0.0), axis=0, keepdims=True)
        gram = gram * coef * coef_row
        weight = weight * coef
        size *= 2
    weight = weight * inverse_col
    combined = None
    for node in range(NODES):
        term = weight[node : node + 1, :] * nodes_ref[node]
        combined = term if combined is None else combined + term
    out_ref[...] = combined


def local(pre_act, out_weight, out_grad):
    tokens, hidden = pre_act.shape
    width = out_weight.shape[1]
    mp = ("x", "c")
    hi = ("y", "zh")
    peers = lax.axis_size(mp)
    spot = jnp.stack([lax.axis_index(axis) for axis in ("zl", "x", "c")]).astype(jnp.int32)
    me = spot[:1]
    node = lax.axis_index(hi).astype(jnp.int32).reshape(1)
    quarter = hidden // LEAVES
    along = lax.axis_size("x")

    def swapped(value, axis, apart):
        return lax.ppermute(value, axis, [(i, i ^ apart) for i in range(lax.axis_size(axis))])

    shards = from_everyone(out_grad, "zl")
    grads = from_everyone(shards, mp)
    dealt = deal(me, pre_act)
    acts = {0: dealt[0]}
    for k in (2, 3, 1):
        acts[k] = swapped(dealt[k], "zl", k)
    arrived = pl.pallas_call(
        arrived_kernel,
        out_shape=jax.ShapeDtypeStruct((8, 128), f32),
        in_specs=[ANY] * (LEAVES - 1),
        compiler_params=pltpu.CompilerParams(vmem_limit_bytes=1024 * 1024),
        cost_estimate=pl.CostEstimate(flops=10**11, bytes_accessed=0, transcendentals=0),
    )(acts[2], acts[3], acts[1])

    leaf_shape = jax.ShapeDtypeStruct((quarter, width), f32)
    group = ("zl", *mp)
    *leaves, sums = call(
        first_gram_kernel,
        [leaf_shape] * LEAVES + [jax.ShapeDtypeStruct((LEAVES * peers, 1, 128), f32)],
        [SMEM, VMEM, VMEM] + [VMEM] * LEAVES,
        flops=2 * tokens * hidden * width,
        size=16 * quarter * width,
    )(spot, grads, arrived, *[acts[k] for k in range(LEAVES)])
    sums = lax.all_to_all(sums, group, split_axis=0, concat_axis=0, tiled=True)
    scaled, inverse = call(
        first_merge_kernel,
        [leaf_shape, jax.ShapeDtypeStruct((8, 128), f32)],
        [SMEM] + [VMEM] * (LEAVES + 1),
        flops=8 * quarter * width,
        size=20 * quarter * width,
    )(me, sums, *leaves)

    half = jax.ShapeDtypeStruct((along, tokens // peers, width), f32)
    mine, theirs = call(
        project_kernel,
        [half, half],
        [SMEM] + [VMEM] * (LEAVES + 2),
        flops=2 * tokens * hidden * width,
        size=4 * tokens * hidden,
        scratch=[pltpu.VMEM((along, 2, tokens // peers, width), f32)],
    )(spot, out_weight.reshape(NODES, LEAVES, -1, width), inverse, *dealt)
    both = mine + swapped(theirs, "c", 1)
    projected = both[0]
    for k in range(1, along):
        projected = projected + swapped(both[k], "x", k)
    projected = projected.astype(bf16)

    rows = quarter // NODES
    sent = scaled.astype(jnp.float16).reshape(NODES, rows, width)
    nodes = lax.all_to_all(sent, hi, split_axis=0, concat_axis=0, tiled=True).astype(f32)
    share = 1.0 / (LEAVES * peers)
    sums = call(
        functools.partial(second_gram_kernel, peers * along, share),
        jax.ShapeDtypeStruct((peers * along, 2, 128), f32),
        [SMEM, VMEM, VMEM, VMEM],
        flops=8 * quarter * quarter * width,
        size=4 * quarter * width,
    )(node, nodes.reshape(quarter, width), inverse, projected)
    sums = lax.all_to_all(sums, ("y", *mp), split_axis=0, concat_axis=0, tiled=True)
    sums = call(pass_on_kernel, jax.ShapeDtypeStruct((NODES, 2, 128), f32), [VMEM])(sums)
    sums = lax.all_to_all(sums, ("zh", "zl"), split_axis=0, concat_axis=0, tiled=True)
    combined = call(
        second_merge_kernel,
        jax.ShapeDtypeStruct((rows, width), f32),
        [VMEM, VMEM],
        flops=2 * quarter * width,
        size=4 * quarter * width,
    )(sums, nodes)
    return projected, combined


def solution(mesh):
    devices = mesh.devices.reshape(4, 4, LEAVES, 4, 2)
    finer = Mesh(devices, ("y", "zh", "zl", "x", "c"))
    dp, mp = ("y", "zh", "zl"), ("x", "c")
    return jax.shard_map(
        local,
        mesh=finer,
        in_specs=(P(dp, mp), P(mp, None), P((*dp, *mp), None)),
        out_specs=(P((*dp, *mp), None), P((*mp, *dp), None)),
        check_vma=False,
    )
```

```python
import functools

import jax
import jax.numpy as jnp
from jax import lax
from jax.experimental import pallas as pl
from jax.experimental.pallas import tpu as pltpu
from jax.sharding import Mesh, PartitionSpec as P

epsilon = 1e-06
LEAVES = 4
NODES = 16
LIMIT = 24 * 1024 * 1024
TOP = 16384.0
FLOOR = 1e-15

f32 = jnp.float32
bf16 = jnp.bfloat16
SMEM = pl.BlockSpec(memory_space=pltpu.SMEM)
VMEM = pl.BlockSpec(memory_space=pltpu.VMEM)
ANY = pl.BlockSpec(memory_space=pl.ANY)


def call(kernel, out_shape, in_specs, flops=0, size=0, scratch=()):
    many = isinstance(out_shape, (list, tuple))
    return pl.pallas_call(
        kernel,
        out_shape=out_shape,
        in_specs=in_specs,
        out_specs=[VMEM] * len(out_shape) if many else VMEM,
        scratch_shapes=list(scratch),
        compiler_params=pltpu.CompilerParams(vmem_limit_bytes=LIMIT),
        cost_estimate=pl.CostEstimate(flops=flops, bytes_accessed=size, transcendentals=0),
    )


def from_everyone(array, axes):
    copies = jnp.broadcast_to(array, (lax.axis_size(axes), *array.shape))
    return lax.all_to_all(copies, axes, split_axis=0, concat_axis=0, tiled=True)


def deal_kernel(me_ref, pre_ref, grad_ref, copies_ref, *refs):
    out_refs, deal_ref = refs[:LEAVES], refs[LEAVES]
    width = pre_ref.shape[1]

    @pl.when(pl.program_id(0) == 0)
    def _():
        row = lax.broadcasted_iota(jnp.int32, (width, width), 0)
        col = lax.broadcasted_iota(jnp.int32, (width, width), 1)
        block = col >> 5
        place = (((block & 3) ^ me_ref[0]) << 7) + ((block >> 2) << 5) + (col & 31)
        deal_ref[...] = jnp.where(place == row, 1.0, 0.0).astype(bf16)
        for copy in range(LEAVES):
            copies_ref[copy] = grad_ref[...]

    part = jnp.maximum(pre_ref[...], jnp.zeros((), bf16))
    dealt = lax.dot_general(
        deal_ref[...], part, (((1,), (1,)), ((), ())), preferred_element_type=f32
    ).astype(bf16)
    for k in range(LEAVES):
        out_refs[k][...] = dealt[k * 128 : (k + 1) * 128, :]


def deal(me, pre_act, out_grad):
    tokens, hidden = pre_act.shape
    shard, width = out_grad.shape
    group = 512
    return pl.pallas_call(
        deal_kernel,
        grid_spec=pltpu.PrefetchScalarGridSpec(
            num_scalar_prefetch=1,
            grid=(hidden // group,),
            in_specs=[
                pl.BlockSpec((tokens, group), lambda g, me: (0, g)),
                pl.BlockSpec((shard, width), lambda g, me: (0, 0)),
            ],
            out_specs=[pl.BlockSpec((LEAVES, shard, width), lambda g, me: (0, 0, 0))]
            + [pl.BlockSpec((group // LEAVES, tokens), lambda g, me: (g, 0))] * LEAVES,
            scratch_shapes=[pltpu.VMEM((group, group), bf16)],
        ),
        out_shape=[jax.ShapeDtypeStruct((LEAVES, shard, width), bf16)]
        + [jax.ShapeDtypeStruct((hidden // LEAVES, tokens), bf16)] * LEAVES,
        compiler_params=pltpu.CompilerParams(vmem_limit_bytes=63 * 1024 * 1024),
        cost_estimate=pl.CostEstimate(
            flops=2 * tokens * hidden * group, bytes_accessed=4 * tokens * hidden, transcendentals=0
        ),
    )(me, pre_act, out_grad)


def arrived_kernel(*refs):
    refs[-1][...] = jnp.zeros_like(refs[-1])


def project_kernel(spot_ref, weight_ref, late_ref, *refs):
    act_refs, (mine_ref, theirs_ref, held_ref) = refs[:LEAVES], refs[LEAVES:]
    count = mine_ref.shape[0]
    me, x, core = spot_ref[0], spot_ref[1], spot_ref[2]
    total = None
    for k in range(LEAVES):
        weight = weight_ref[:, me ^ k].reshape(act_refs[k].shape[0], -1)
        part = lax.dot_general(
            act_refs[k][...], weight, (((0,), (0,)), ((), ())), preferred_element_type=f32
        )
        total = part if total is None else total + part
    held_ref[...] = total.reshape(held_ref.shape)
    for k in range(count):
        mine_ref[k] = held_ref[x ^ k, core]
        theirs_ref[k] = held_ref[x ^ k, 1 - core]


def lanes_of(total):
    return total[:, :128] + total[:, 128:256] + total[:, 256:384] + total[:, 384:512]


def first_gram_kernel(spot_ref, grads_ref, late_ref, *refs):
    act_refs, held, out_ref = refs[:LEAVES], refs[LEAVES:-1], refs[-1]
    peers, _, rows, width = grads_ref.shape
    me = spot_ref[0]
    for k in range(LEAVES):
        out_grad = grads_ref[:, me ^ k].reshape(peers * rows, width)
        held[k][...] = jnp.dot(act_refs[k][...], out_grad, preferred_element_type=f32)
    lane = lax.broadcasted_iota(jnp.int32, (1, 128), 1)
    whole = jnp.zeros((1, 128), f32)
    for a in range(LEAVES):
        for b in range(a, LEAVES):
            lanes = lanes_of(jnp.sum(held[a][...] * held[b][...], axis=0, keepdims=True))
            value = jnp.sum(lanes, axis=1, keepdims=True)
            here = lane == LEAVES * (a ^ me) + (b ^ me)
            if a != b:
                here = here | (lane == LEAVES * (b ^ me) + (a ^ me))
            whole = jnp.where(here, value, whole)
    for copy in range(out_ref.shape[0]):
        out_ref[copy] = whole


def tree(gram, count):
    coef = [None] * count
    weight = [jnp.ones_like(gram[0][0])] * count
    size = 1
    while size < count:
        for low in range(0, count, 2 * size):
            first, second = range(low, low + size), range(low + size, low + 2 * size)

            def inner(left, right):
                return sum(weight[i] * weight[j] * gram[i][j] for i in left for j in right)

            cross = inner(first, second)
            first_sq = jnp.maximum(inner(first, first), 0.0)
            second_sq = jnp.maximum(inner(second, second), 0.0)
            first_coef = 1.0 - cross / (2.0 * (first_sq + epsilon))
            second_coef = 1.0 - cross / (2.0 * (second_sq + epsilon))
            for i in first:
                coef[i] = weight[i] * first_coef
            for i in second:
                coef[i] = weight[i] * second_coef
        weight = list(coef)
        size *= 2
    return weight


def first_merge_kernel(me_ref, sums_ref, *refs):
    leaf_refs, node_ref, inverse_ref = refs[:LEAVES], refs[LEAVES], refs[LEAVES + 1]
    me = me_ref[0]
    total = jnp.sum(sums_ref[...], axis=0)
    lane = lax.broadcasted_iota(jnp.int32, total.shape, 1)
    gram = [
        [
            jnp.sum(jnp.where(lane == LEAVES * i + j, total, 0.0), axis=1, keepdims=True)
            for j in range(LEAVES)
        ]
        for i in range(LEAVES)
    ]
    coef = tree(gram, LEAVES)
    bound = sum(jnp.abs(coef[i]) * jnp.sqrt(gram[i][i]) for i in range(LEAVES))
    bound = jnp.maximum(bound, FLOOR)
    scale = TOP / bound
    inverse_ref[...] = jnp.broadcast_to(bound * (1.0 / TOP), inverse_ref.shape)
    merged = None
    for k in range(LEAVES):
        mine = coef[k]
        for other in range(1, LEAVES):
            mine = jnp.where(me == other, coef[k ^ other], mine)
        term = (mine * scale) * leaf_refs[k][...]
        merged = term if merged is None else merged + term
    node_ref[...] = merged


def second_gram_kernel(copies, share, node_ref, nodes_ref, inverse_ref, late_ref, out_ref):
    node = node_ref[0]
    total, width = nodes_ref.shape
    rows = total // NODES
    held = nodes_ref[...]
    high = held.astype(bf16)
    low = (held - high.astype(f32)).astype(bf16)
    last = (((1,), (1,)), ((), ()))
    products = (
        lax.dot_general(high, high, last, preferred_element_type=f32)
        + lax.dot_general(high, low, last, preferred_element_type=f32)
        + lax.dot_general(low, high, last, preferred_element_type=f32)
        + lax.dot_general(low, low, last, preferred_element_type=f32)
    )
    row = lax.broadcasted_iota(jnp.int32, (total, total), 0)
    col = lax.broadcasted_iota(jnp.int32, (total, total), 1)
    products = jnp.where((row & (rows - 1)) == (col & (rows - 1)), products, 0.0)
    by_node = jnp.sum(products.reshape(NODES, rows, total), axis=1)
    source = lax.broadcasted_iota(jnp.int32, (total, 128), 0)
    lane = lax.broadcasted_iota(jnp.int32, (total, 128), 1)
    spread = jnp.where(source // rows == (lane & (NODES - 1)), 1.0, 0.0)
    gram = jnp.dot(by_node, spread, preferred_element_type=f32, precision=lax.Precision.HIGHEST)
    place = lax.broadcasted_iota(jnp.int32, (NODES, 128), 0)
    lane = lax.broadcasted_iota(jnp.int32, (NODES, 128), 1)
    packed = jnp.where(lane // NODES == (place & 7), gram, 0.0)
    lane = lane[:1]
    upper = jnp.sum(packed[:8], axis=0, keepdims=True)
    lower = jnp.sum(packed[8:], axis=0, keepdims=True)
    inverse = jnp.where(lane == (node & 7) + 2 * (node & 8), inverse_ref[:1] * share, 0.0)
    lower = jnp.where((lane & (NODES - 1)) < 8, inverse, lower)
    whole = jnp.concatenate([upper, lower], axis=0)
    for copy in range(copies):
        out_ref[copy] = whole


def pass_on_kernel(sums_ref, out_ref):
    whole = jnp.sum(sums_ref[...], axis=0)
    for copy in range(out_ref.shape[0]):
        out_ref[copy] = whole


def second_merge_kernel(sums_ref, nodes_ref, out_ref):
    total = jnp.sum(sums_ref[...], axis=0)
    place = lax.broadcasted_iota(jnp.int32, (NODES, 128), 0)
    lane = lax.broadcasted_iota(jnp.int32, (NODES, 128), 1)
    gram = jnp.where(place < 8, total[0:1], total[1:2])
    gram = jnp.where(lane // NODES == (place & 7), gram, 0.0)
    free = (lane & 8) == 0
    gram = jnp.where((place >= 8) & free, 0.0, gram)
    inverse_row = jnp.where((lane[:1] < NODES) & free[:1], total[1:2], 0.0)
    second = jnp.where((lane[:1] >= NODES) & (lane[:1] < NODES + 8), total[1:2], 0.0)
    inverse_row = inverse_row + pltpu.roll(second, 128 - 8, 1)
    for turn in (16, 32, 64):
        gram = gram + pltpu.roll(gram, turn, 1)
        inverse_row = inverse_row + pltpu.roll(inverse_row, turn, 1)
    other = lane & (NODES - 1)
    first = lane < NODES
    corner = jnp.where((place < 8) & (other >= 8), gram, 0.0)
    unit = jnp.where(place == other, 1.0, 0.0)
    mirrored = lax.dot_general(
        corner,
        unit,
        (((0,), (0,)), ((), ())),
        preferred_element_type=f32,
        precision=lax.Precision.HIGHEST,
    )
    gram = gram + mirrored[:NODES]

    def column(row):
        return jnp.sum(jnp.where(lane == place, row, 0.0), axis=1, keepdims=True)

    inverse_col = column(inverse_row)
    gram = gram * inverse_row * inverse_col
    size, weight = 1, jnp.ones((NODES, 1), f32)
    while size < NODES:
        mine = (place // size) == (other // size)
        sibling = (place // size) == ((other // size) ^ 1)
        own_col = jnp.sum(jnp.where(mine, gram, 0.0), axis=0, keepdims=True)
        cross_col = jnp.sum(jnp.where(sibling, gram, 0.0), axis=0, keepdims=True)
        here = mine & first
        own = jnp.sum(jnp.where(here, own_col, 0.0), axis=1, keepdims=True)
        cross = jnp.sum(jnp.where(here, cross_col, 0.0), axis=1, keepdims=True)
        coef = 1.0 - cross / (2.0 * (jnp.maximum(own, 0.0) + epsilon))
        coef_row = jnp.sum(jnp.where(place == other, coef, 0.0), axis=0, keepdims=True)
        gram = gram * coef * coef_row
        weight = weight * coef
        size *= 2
    weight = weight * inverse_col
    combined = None
    for node in range(NODES):
        term = weight[node : node + 1, :] * nodes_ref[node]
        combined = term if combined is None else combined + term
    out_ref[...] = combined


def local(pre_act, out_weight, out_grad):
    tokens, hidden = pre_act.shape
    width = out_weight.shape[1]
    mp = ("x", "c")
    hi = ("y", "zh")
    peers = lax.axis_size(mp)
    spot = jnp.stack([lax.axis_index(axis) for axis in ("zl", "x", "c")]).astype(jnp.int32)
    me = spot[:1]
    node = lax.axis_index(hi).astype(jnp.int32).reshape(1)
    quarter = hidden // LEAVES
    along = lax.axis_size("x")

    def swapped(value, axis, apart):
        return lax.ppermute(value, axis, [(i, i ^ apart) for i in range(lax.axis_size(axis))])

    copies, *dealt = deal(me, pre_act, out_grad)
    acts = {0: dealt[0]}
    for k in (2, 1, 3):
        acts[k] = swapped(dealt[k], "zl", k)
    shards = lax.all_to_all(copies, "zl", split_axis=0, concat_axis=0, tiled=True)
    grads = from_everyone(shards, mp)
    arrived = pl.pallas_call(
        arrived_kernel,
        out_shape=jax.ShapeDtypeStruct((8, 128), f32),
        in_specs=[ANY] * (LEAVES - 1),
        compiler_params=pltpu.CompilerParams(vmem_limit_bytes=1024 * 1024),
        cost_estimate=pl.CostEstimate(flops=10**11, bytes_accessed=0, transcendentals=0),
    )(acts[2], acts[1], acts[3])

    leaf_shape = jax.ShapeDtypeStruct((quarter, width), f32)
    group = ("zl", *mp)
    *leaves, sums = call(
        first_gram_kernel,
        [leaf_shape] * LEAVES + [jax.ShapeDtypeStruct((LEAVES * peers, 1, 128), f32)],
        [SMEM, VMEM, VMEM] + [VMEM] * LEAVES,
        flops=2 * tokens * hidden * width,
        size=16 * quarter * width,
    )(spot, grads, arrived, *[acts[k] for k in range(LEAVES)])
    sums = lax.all_to_all(sums, group, split_axis=0, concat_axis=0, tiled=True)
    scaled, inverse = call(
        first_merge_kernel,
        [leaf_shape, jax.ShapeDtypeStruct((8, 128), f32)],
        [SMEM] + [VMEM] * (LEAVES + 1),
        flops=8 * quarter * width,
        size=20 * quarter * width,
    )(me, sums, *leaves)

    half = jax.ShapeDtypeStruct((along, tokens // peers, width), f32)
    mine, theirs = call(
        project_kernel,
        [half, half],
        [SMEM] + [VMEM] * (LEAVES + 2),
        flops=2 * tokens * hidden * width,
        size=4 * tokens * hidden,
        scratch=[pltpu.VMEM((along, 2, tokens // peers, width), f32)],
    )(spot, out_weight.reshape(NODES, LEAVES, -1, width), inverse, *dealt)
    both = mine + swapped(theirs, "c", 1)
    projected = both[0]
    for k in range(1, along):
        projected = projected + swapped(both[k], "x", k)
    projected = projected.astype(bf16)

    rows = quarter // NODES
    sent = scaled.astype(jnp.float16).reshape(NODES, rows, width)
    nodes = lax.all_to_all(sent, hi, split_axis=0, concat_axis=0, tiled=True).astype(f32)
    share = 1.0 / (LEAVES * peers)
    sums = call(
        functools.partial(second_gram_kernel, peers * along, share),
        jax.ShapeDtypeStruct((peers * along, 2, 128), f32),
        [SMEM, VMEM, VMEM, VMEM],
        flops=8 * quarter * quarter * width,
        size=4 * quarter * width,
    )(node, nodes.reshape(quarter, width), inverse, projected)
    sums = lax.all_to_all(sums, ("y", *mp), split_axis=0, concat_axis=0, tiled=True)
    sums = call(pass_on_kernel, jax.ShapeDtypeStruct((NODES, 2, 128), f32), [VMEM])(sums)
    sums = lax.all_to_all(sums, ("zh", "zl"), split_axis=0, concat_axis=0, tiled=True)
    combined = call(
        second_merge_kernel,
        jax.ShapeDtypeStruct((rows, width), f32),
        [VMEM, VMEM],
        flops=2 * quarter * width,
        size=4 * quarter * width,
    )(sums, nodes)
    return projected, combined


def solution(mesh):
    devices = mesh.devices.reshape(4, 4, LEAVES, 4, 2)
    finer = Mesh(devices, ("y", "zh", "zl", "x", "c"))
    dp, mp = ("y", "zh", "zl"), ("x", "c")
    return jax.shard_map(
        local,
        mesh=finer,
        in_specs=(P(dp, mp), P(mp, None), P((*dp, *mp), None)),
        out_specs=(P((*dp, *mp), None), P((*mp, *dp), None)),
        check_vma=False,
    )
```

```python
import functools

import jax
import jax.numpy as jnp
from jax import lax
from jax.experimental import pallas as pl
from jax.experimental.pallas import tpu as pltpu
from jax.sharding import Mesh, PartitionSpec as P

epsilon = 1e-06
LEAVES = 4
NODES = 16
LIMIT = 24 * 1024 * 1024
TOP = 16384.0
FLOOR = 1e-15

f32 = jnp.float32
bf16 = jnp.bfloat16
SMEM = pl.BlockSpec(memory_space=pltpu.SMEM)
VMEM = pl.BlockSpec(memory_space=pltpu.VMEM)
ANY = pl.BlockSpec(memory_space=pl.ANY)


def call(kernel, out_shape, in_specs, flops=0, size=0, scratch=()):
    many = isinstance(out_shape, (list, tuple))
    return pl.pallas_call(
        kernel,
        out_shape=out_shape,
        in_specs=in_specs,
        out_specs=[VMEM] * len(out_shape) if many else VMEM,
        scratch_shapes=list(scratch),
        compiler_params=pltpu.CompilerParams(vmem_limit_bytes=LIMIT),
        cost_estimate=pl.CostEstimate(flops=flops, bytes_accessed=size, transcendentals=0),
    )


def from_everyone(array, axes):
    copies = jnp.broadcast_to(array, (lax.axis_size(axes), *array.shape))
    return lax.all_to_all(copies, axes, split_axis=0, concat_axis=0, tiled=True)


def deal_kernel(me_ref, pre_ref, *refs):
    out_refs, deal_ref = refs[:LEAVES], refs[LEAVES]
    width = pre_ref.shape[1]

    @pl.when(pl.program_id(0) == 0)
    def _():
        row = lax.broadcasted_iota(jnp.int32, (width, width), 0)
        col = lax.broadcasted_iota(jnp.int32, (width, width), 1)
        block = row >> 5
        place = (((block & 3) ^ me_ref[0]) << 7) + ((block >> 2) << 5) + (row & 31)
        deal_ref[...] = jnp.where(place == col, 1.0, 0.0).astype(bf16)

    part = jnp.maximum(pre_ref[...], jnp.zeros((), bf16))
    dealt = jnp.dot(part, deal_ref[...], preferred_element_type=f32).astype(bf16)
    for k in range(LEAVES):
        out_refs[k][...] = dealt[:, k * 128 : (k + 1) * 128]


def deal(me, pre_act):
    tokens, hidden = pre_act.shape
    group = 512
    return pl.pallas_call(
        deal_kernel,
        grid_spec=pltpu.PrefetchScalarGridSpec(
            num_scalar_prefetch=1,
            grid=(hidden // group,),
            in_specs=[pl.BlockSpec((tokens, group), lambda g, me: (0, g))],
            out_specs=[pl.BlockSpec((tokens, group // LEAVES), lambda g, me: (0, g))] * LEAVES,
            scratch_shapes=[pltpu.VMEM((group, group), bf16)],
        ),
        out_shape=[jax.ShapeDtypeStruct((tokens, hidden // LEAVES), bf16)] * LEAVES,
        compiler_params=pltpu.CompilerParams(vmem_limit_bytes=LIMIT),
        cost_estimate=pl.CostEstimate(
            flops=2 * tokens * hidden * group, bytes_accessed=4 * tokens * hidden, transcendentals=0
        ),
    )(me, pre_act)


def arrived_kernel(*refs):
    refs[-1][...] = jnp.zeros_like(refs[-1])


def project_kernel(spot_ref, weight_ref, late_ref, *refs):
    act_refs, (mine_ref, theirs_ref, held_ref) = refs[:LEAVES], refs[LEAVES:]
    count = mine_ref.shape[0]
    me, x, core = spot_ref[0], spot_ref[1], spot_ref[2]
    total = None
    for k in range(LEAVES):
        weight = weight_ref[:, me ^ k].reshape(act_refs[k].shape[1], -1)
        part = jnp.dot(act_refs[k][...], weight, preferred_element_type=f32)
        total = part if total is None else total + part
    held_ref[...] = total.reshape(held_ref.shape)
    for k in range(count):
        mine_ref[k] = held_ref[x ^ k, core]
        theirs_ref[k] = held_ref[x ^ k, 1 - core]


def lanes_of(total):
    return total[:, :128] + total[:, 128:256] + total[:, 256:384] + total[:, 384:512]


def first_gram_kernel(spot_ref, grads_ref, late_ref, *refs):
    act_refs, held, out_ref = refs[:LEAVES], refs[LEAVES:-1], refs[-1]
    peers, _, rows, width = grads_ref.shape
    me = spot_ref[0]
    for k in range(LEAVES):
        out_grad = grads_ref[:, me ^ k].reshape(peers * rows, width)
        held[k][...] = lax.dot_general(
            act_refs[k][...], out_grad, (((0,), (0,)), ((), ())), preferred_element_type=f32
        )
    pairs = [(a, b) for a in range(LEAVES) for b in range(a, LEAVES)]
    totals = [jnp.zeros((8, 128), f32) for _ in pairs]
    for row in range(0, held[0].shape[0], 8):
        strip = [leaf_ref[row : row + 8, :] for leaf_ref in held]
        totals = [total + lanes_of(strip[a] * strip[b]) for total, (a, b) in zip(totals, pairs)]
    lane = lax.broadcasted_iota(jnp.int32, (1, 128), 1)
    whole = jnp.zeros((1, 128), f32)
    for total, (a, b) in zip(totals, pairs):
        value = jnp.sum(jnp.sum(total, axis=0, keepdims=True), axis=1, keepdims=True)
        here = lane == LEAVES * (a ^ me) + (b ^ me)
        if a != b:
            here = here | (lane == LEAVES * (b ^ me) + (a ^ me))
        whole = jnp.where(here, value, whole)
    for copy in range(out_ref.shape[0]):
        out_ref[copy] = whole


def tree(gram, count):
    coef = [None] * count
    weight = [jnp.ones_like(gram[0][0])] * count
    size = 1
    while size < count:
        for low in range(0, count, 2 * size):
            first, second = range(low, low + size), range(low + size, low + 2 * size)

            def inner(left, right):
                return sum(weight[i] * weight[j] * gram[i][j] for i in left for j in right)

            cross = inner(first, second)
            first_sq = jnp.maximum(inner(first, first), 0.0)
            second_sq = jnp.maximum(inner(second, second), 0.0)
            first_coef = 1.0 - cross / (2.0 * (first_sq + epsilon))
            second_coef = 1.0 - cross / (2.0 * (second_sq + epsilon))
            for i in first:
                coef[i] = weight[i] * first_coef
            for i in second:
                coef[i] = weight[i] * second_coef
        weight = list(coef)
        size *= 2
    return weight


def first_merge_kernel(me_ref, sums_ref, *refs):
    leaf_refs, node_ref, inverse_ref = refs[:LEAVES], refs[LEAVES], refs[LEAVES + 1]
    me = me_ref[0]
    total = jnp.sum(sums_ref[...], axis=0)
    lane = lax.broadcasted_iota(jnp.int32, total.shape, 1)
    gram = [
        [
            jnp.sum(jnp.where(lane == LEAVES * i + j, total, 0.0), axis=1, keepdims=True)
            for j in range(LEAVES)
        ]
        for i in range(LEAVES)
    ]
    coef = tree(gram, LEAVES)
    bound = sum(jnp.abs(coef[i]) * jnp.sqrt(gram[i][i]) for i in range(LEAVES))
    bound = jnp.maximum(bound, FLOOR)
    scale = TOP / bound
    inverse_ref[...] = jnp.broadcast_to(bound * (1.0 / TOP), inverse_ref.shape)
    merged = None
    for k in range(LEAVES):
        mine = coef[k]
        for other in range(1, LEAVES):
            mine = jnp.where(me == other, coef[k ^ other], mine)
        term = (mine * scale) * leaf_refs[k][...]
        merged = term if merged is None else merged + term
    node_ref[...] = merged


def second_gram_kernel(copies, share, node_ref, nodes_ref, inverse_ref, late_ref, out_ref):
    node = node_ref[0]
    total, width = nodes_ref.shape
    rows = total // NODES
    held = nodes_ref[...]
    high = held.astype(bf16)
    low = (held - high.astype(f32)).astype(bf16)
    last = (((1,), (1,)), ((), ()))
    products = (
        lax.dot_general(high, high, last, preferred_element_type=f32)
        + lax.dot_general(high, low, last, preferred_element_type=f32)
        + lax.dot_general(low, high, last, preferred_element_type=f32)
        + lax.dot_general(low, low, last, preferred_element_type=f32)
    )
    row = lax.broadcasted_iota(jnp.int32, (total, total), 0)
    col = lax.broadcasted_iota(jnp.int32, (total, total), 1)
    products = jnp.where((row & (rows - 1)) == (col & (rows - 1)), products, 0.0)
    by_node = jnp.sum(products.reshape(NODES, rows, total), axis=1)
    source = lax.broadcasted_iota(jnp.int32, (total, 128), 0)
    lane = lax.broadcasted_iota(jnp.int32, (total, 128), 1)
    spread = jnp.where(source // rows == (lane & (NODES - 1)), 1.0, 0.0)
    gram = jnp.dot(by_node, spread, preferred_element_type=f32, precision=lax.Precision.HIGHEST)
    place = lax.broadcasted_iota(jnp.int32, (NODES, 128), 0)
    lane = lax.broadcasted_iota(jnp.int32, (NODES, 128), 1)
    packed = jnp.where(lane // NODES == (place & 7), gram, 0.0)
    lane = lane[:1]
    upper = jnp.sum(packed[:8], axis=0, keepdims=True)
    lower = jnp.sum(packed[8:], axis=0, keepdims=True)
    inverse = jnp.where(lane == (node & 7) + 2 * (node & 8), inverse_ref[:1] * share, 0.0)
    lower = jnp.where((lane & (NODES - 1)) < 8, inverse, lower)
    whole = jnp.concatenate([upper, lower], axis=0)
    for copy in range(copies):
        out_ref[copy] = whole


def pass_on_kernel(sums_ref, out_ref):
    whole = jnp.sum(sums_ref[...], axis=0)
    for copy in range(out_ref.shape[0]):
        out_ref[copy] = whole


def second_merge_kernel(sums_ref, nodes_ref, out_ref):
    total = jnp.sum(sums_ref[...], axis=0)
    place = lax.broadcasted_iota(jnp.int32, (NODES, 128), 0)
    lane = lax.broadcasted_iota(jnp.int32, (NODES, 128), 1)
    gram = jnp.where(place < 8, total[0:1], total[1:2])
    gram = jnp.where(lane // NODES == (place & 7), gram, 0.0)
    free = (lane & 8) == 0
    gram = jnp.where((place >= 8) & free, 0.0, gram)
    inverse_row = jnp.where((lane[:1] < NODES) & free[:1], total[1:2], 0.0)
    second = jnp.where((lane[:1] >= NODES) & (lane[:1] < NODES + 8), total[1:2], 0.0)
    inverse_row = inverse_row + pltpu.roll(second, 128 - 8, 1)
    for turn in (16, 32, 64):
        gram = gram + pltpu.roll(gram, turn, 1)
        inverse_row = inverse_row + pltpu.roll(inverse_row, turn, 1)
    other = lane & (NODES - 1)
    first = lane < NODES
    corner = jnp.where((place < 8) & (other >= 8), gram, 0.0)
    unit = jnp.where(place == other, 1.0, 0.0)
    mirrored = lax.dot_general(
        corner,
        unit,
        (((0,), (0,)), ((), ())),
        preferred_element_type=f32,
        precision=lax.Precision.HIGHEST,
    )
    gram = gram + mirrored[:NODES]

    def column(row):
        return jnp.sum(jnp.where(lane == place, row, 0.0), axis=1, keepdims=True)

    inverse_col = column(inverse_row)
    gram = gram * inverse_row * inverse_col
    size, weight = 1, jnp.ones((NODES, 1), f32)
    while size < NODES:
        mine = (place // size) == (other // size)
        sibling = (place // size) == ((other // size) ^ 1)
        own_col = jnp.sum(jnp.where(mine, gram, 0.0), axis=0, keepdims=True)
        cross_col = jnp.sum(jnp.where(sibling, gram, 0.0), axis=0, keepdims=True)
        here = mine & first
        own = jnp.sum(jnp.where(here, own_col, 0.0), axis=1, keepdims=True)
        cross = jnp.sum(jnp.where(here, cross_col, 0.0), axis=1, keepdims=True)
        coef = 1.0 - cross / (2.0 * (jnp.maximum(own, 0.0) + epsilon))
        coef_row = jnp.sum(jnp.where(place == other, coef, 0.0), axis=0, keepdims=True)
        gram = gram * coef * coef_row
        weight = weight * coef
        size *= 2
    weight = weight * inverse_col
    combined = None
    for node in range(NODES):
        term = weight[node : node + 1, :] * nodes_ref[node]
        combined = term if combined is None else combined + term
    out_ref[...] = combined


def local(pre_act, out_weight, out_grad):
    tokens, hidden = pre_act.shape
    width = out_weight.shape[1]
    mp = ("x", "c")
    hi = ("y", "zh")
    peers = lax.axis_size(mp)
    spot = jnp.stack([lax.axis_index(axis) for axis in ("zl", "x", "c")]).astype(jnp.int32)
    me = spot[:1]
    node = lax.axis_index(hi).astype(jnp.int32).reshape(1)
    quarter = hidden // LEAVES
    along = lax.axis_size("x")

    def swapped(value, axis, apart):
        return lax.ppermute(value, axis, [(i, i ^ apart) for i in range(lax.axis_size(axis))])

    shards = from_everyone(out_grad, "zl")
    grads = from_everyone(shards, mp)
    dealt = deal(me, pre_act)
    acts = {0: dealt[0]}
    for k in (3, 2, 1):
        acts[k] = swapped(dealt[k], "zl", k)
    arrived = pl.pallas_call(
        arrived_kernel,
        out_shape=jax.ShapeDtypeStruct((8, 128), f32),
        in_specs=[ANY] * (LEAVES - 1),
        compiler_params=pltpu.CompilerParams(vmem_limit_bytes=1024 * 1024),
        cost_estimate=pl.CostEstimate(flops=10**11, bytes_accessed=0, transcendentals=0),
    )(acts[3], acts[2], acts[1])

    leaf_shape = jax.ShapeDtypeStruct((quarter, width), f32)
    group = ("zl", *mp)
    *leaves, sums = call(
        first_gram_kernel,
        [leaf_shape] * LEAVES + [jax.ShapeDtypeStruct((LEAVES * peers, 1, 128), f32)],
        [SMEM, VMEM, VMEM] + [VMEM] * LEAVES,
        flops=2 * tokens * hidden * width,
        size=16 * quarter * width,
    )(spot, grads, arrived, *[acts[k] for k in range(LEAVES)])
    sums = lax.all_to_all(sums, group, split_axis=0, concat_axis=0, tiled=True)
    scaled, inverse = call(
        first_merge_kernel,
        [leaf_shape, jax.ShapeDtypeStruct((8, 128), f32)],
        [SMEM] + [VMEM] * (LEAVES + 1),
        flops=8 * quarter * width,
        size=20 * quarter * width,
    )(me, sums, *leaves)

    half = jax.ShapeDtypeStruct((along, tokens // peers, width), f32)
    mine, theirs = call(
        project_kernel,
        [half, half],
        [SMEM] + [VMEM] * (LEAVES + 2),
        flops=2 * tokens * hidden * width,
        size=4 * tokens * hidden,
        scratch=[pltpu.VMEM((along, 2, tokens // peers, width), f32)],
    )(spot, out_weight.reshape(NODES, LEAVES, -1, width), inverse, *dealt)
    both = mine + swapped(theirs, "c", 1)
    projected = both[0]
    for k in range(1, along):
        projected = projected + swapped(both[k], "x", k)
    projected = projected.astype(bf16)

    rows = quarter // NODES
    sent = scaled.astype(jnp.float16).reshape(NODES, rows, width)
    nodes = lax.all_to_all(sent, hi, split_axis=0, concat_axis=0, tiled=True).astype(f32)
    share = 1.0 / (LEAVES * peers)
    sums = call(
        functools.partial(second_gram_kernel, peers * along, share),
        jax.ShapeDtypeStruct((peers * along, 2, 128), f32),
        [SMEM, VMEM, VMEM, VMEM],
        flops=8 * quarter * quarter * width,
        size=4 * quarter * width,
    )(node, nodes.reshape(quarter, width), inverse, projected)
    sums = lax.all_to_all(sums, ("y", *mp), split_axis=0, concat_axis=0, tiled=True)
    sums = call(pass_on_kernel, jax.ShapeDtypeStruct((NODES, 2, 128), f32), [VMEM])(sums)
    sums = lax.all_to_all(sums, ("zh", "zl"), split_axis=0, concat_axis=0, tiled=True)
    combined = call(
        second_merge_kernel,
        jax.ShapeDtypeStruct((rows, width), f32),
        [VMEM, VMEM],
        flops=2 * quarter * width,
        size=4 * quarter * width,
    )(sums, nodes)
    return projected, combined


def solution(mesh):
    devices = mesh.devices.reshape(4, 4, LEAVES, 4, 2)
    finer = Mesh(devices, ("y", "zh", "zl", "x", "c"))
    dp, mp = ("y", "zh", "zl"), ("x", "c")
    return jax.shard_map(
        local,
        mesh=finer,
        in_specs=(P(dp, mp), P(mp, None), P((*dp, *mp), None)),
        out_specs=(P((*dp, *mp), None), P((*mp, *dp), None)),
        check_vma=False,
    )
```

```python
import functools

import jax
import jax.numpy as jnp
from jax import lax
from jax.experimental import pallas as pl
from jax.experimental.pallas import tpu as pltpu
from jax.sharding import Mesh, PartitionSpec as P

epsilon = 1e-06
LEAVES = 4
NODES = 16
LIMIT = 24 * 1024 * 1024
TOP = 16384.0
FLOOR = 1e-15

f32 = jnp.float32
bf16 = jnp.bfloat16
SMEM = pl.BlockSpec(memory_space=pltpu.SMEM)
VMEM = pl.BlockSpec(memory_space=pltpu.VMEM)
ANY = pl.BlockSpec(memory_space=pl.ANY)


def call(kernel, out_shape, in_specs, flops=0, size=0, scratch=()):
    many = isinstance(out_shape, (list, tuple))
    return pl.pallas_call(
        kernel,
        out_shape=out_shape,
        in_specs=in_specs,
        out_specs=[VMEM] * len(out_shape) if many else VMEM,
        scratch_shapes=list(scratch),
        compiler_params=pltpu.CompilerParams(vmem_limit_bytes=LIMIT),
        cost_estimate=pl.CostEstimate(flops=flops, bytes_accessed=size, transcendentals=0),
    )


def from_everyone(array, axes):
    copies = jnp.broadcast_to(array, (lax.axis_size(axes), *array.shape))
    return lax.all_to_all(copies, axes, split_axis=0, concat_axis=0, tiled=True)


def deal_kernel(me_ref, pre_ref, grad_ref, copy_ref, *refs):
    out_refs, deal_ref = refs[:LEAVES], refs[LEAVES]
    width = pre_ref.shape[1]

    @pl.when(pl.program_id(0) == 0)
    def _():
        row = lax.broadcasted_iota(jnp.int32, (width, width), 0)
        col = lax.broadcasted_iota(jnp.int32, (width, width), 1)
        block = col >> 5
        place = (((block & 3) ^ me_ref[0]) << 7) + ((block >> 2) << 5) + (col & 31)
        deal_ref[...] = jnp.where(place == row, 1.0, 0.0).astype(bf16)
        copy_ref[...] = grad_ref[...]

    part = jnp.maximum(pre_ref[...], jnp.zeros((), bf16))
    dealt = lax.dot_general(
        deal_ref[...], part, (((1,), (1,)), ((), ())), preferred_element_type=f32
    ).astype(bf16)
    for k in range(LEAVES):
        out_refs[k][...] = dealt[k * 128 : (k + 1) * 128, :]


def deal(me, pre_act, out_grad):
    tokens, hidden = pre_act.shape
    shard, width = out_grad.shape
    group = 512
    return pl.pallas_call(
        deal_kernel,
        grid_spec=pltpu.PrefetchScalarGridSpec(
            num_scalar_prefetch=1,
            grid=(hidden // group,),
            in_specs=[
                pl.BlockSpec((tokens, group), lambda g, me: (0, g)),
                pl.BlockSpec((shard, width), lambda g, me: (0, 0)),
            ],
            out_specs=[pl.BlockSpec((shard, width), lambda g, me: (0, 0))]
            + [pl.BlockSpec((group // LEAVES, tokens), lambda g, me: (g, 0))] * LEAVES,
            scratch_shapes=[pltpu.VMEM((group, group), bf16)],
        ),
        out_shape=[jax.ShapeDtypeStruct((shard, width), bf16)]
        + [jax.ShapeDtypeStruct((hidden // LEAVES, tokens), bf16)] * LEAVES,
        compiler_params=pltpu.CompilerParams(vmem_limit_bytes=63 * 1024 * 1024),
        cost_estimate=pl.CostEstimate(
            flops=2 * tokens * hidden * group, bytes_accessed=4 * tokens * hidden, transcendentals=0
        ),
    )(me, pre_act, out_grad)


def arrived_kernel(*refs):
    refs[-1][...] = jnp.zeros_like(refs[-1])


def project_kernel(spot_ref, weight_ref, late_ref, *refs):
    act_refs, (mine_ref, theirs_ref, held_ref) = refs[:LEAVES], refs[LEAVES:]
    count = mine_ref.shape[0]
    me, x, core = spot_ref[0], spot_ref[1], spot_ref[2]
    total = None
    for k in range(LEAVES):
        weight = weight_ref[:, me ^ k].reshape(act_refs[k].shape[0], -1)
        part = lax.dot_general(
            act_refs[k][...], weight, (((0,), (0,)), ((), ())), preferred_element_type=f32
        )
        total = part if total is None else total + part
    held_ref[...] = total.reshape(held_ref.shape)
    for k in range(count):
        mine_ref[k] = held_ref[x ^ k, core]
        theirs_ref[k] = held_ref[x ^ k, 1 - core]


def lanes_of(total):
    return total[:, :128] + total[:, 128:256] + total[:, 256:384] + total[:, 384:512]


def first_gram_kernel(spot_ref, grads_ref, late_ref, *refs):
    act_refs, held, out_ref = refs[:LEAVES], refs[LEAVES:-1], refs[-1]
    peers, _, rows, width = grads_ref.shape
    me = spot_ref[0]
    for k in range(LEAVES):
        out_grad = grads_ref[:, (0, 2, 1, 3)[k]].reshape(peers * rows, width)
        held[k][...] = jnp.dot(act_refs[k][...], out_grad, preferred_element_type=f32)
    lane = lax.broadcasted_iota(jnp.int32, (1, 128), 1)
    whole = jnp.zeros((1, 128), f32)
    for a in range(LEAVES):
        for b in range(a, LEAVES):
            lanes = lanes_of(jnp.sum(held[a][...] * held[b][...], axis=0, keepdims=True))
            value = jnp.sum(lanes, axis=1, keepdims=True)
            here = lane == LEAVES * (a ^ me) + (b ^ me)
            if a != b:
                here = here | (lane == LEAVES * (b ^ me) + (a ^ me))
            whole = jnp.where(here, value, whole)
    for copy in range(out_ref.shape[0]):
        out_ref[copy] = whole


def tree(gram, count):
    coef = [None] * count
    weight = [jnp.ones_like(gram[0][0])] * count
    size = 1
    while size < count:
        for low in range(0, count, 2 * size):
            first, second = range(low, low + size), range(low + size, low + 2 * size)

            def inner(left, right):
                return sum(weight[i] * weight[j] * gram[i][j] for i in left for j in right)

            cross = inner(first, second)
            first_sq = jnp.maximum(inner(first, first), 0.0)
            second_sq = jnp.maximum(inner(second, second), 0.0)
            first_coef = 1.0 - cross / (2.0 * (first_sq + epsilon))
            second_coef = 1.0 - cross / (2.0 * (second_sq + epsilon))
            for i in first:
                coef[i] = weight[i] * first_coef
            for i in second:
                coef[i] = weight[i] * second_coef
        weight = list(coef)
        size *= 2
    return weight


def first_merge_kernel(me_ref, sums_ref, *refs):
    leaf_refs, node_ref, inverse_ref = refs[:LEAVES], refs[LEAVES], refs[LEAVES + 1]
    me = me_ref[0]
    total = jnp.sum(sums_ref[...], axis=0)
    lane = lax.broadcasted_iota(jnp.int32, total.shape, 1)
    gram = [
        [
            jnp.sum(jnp.where(lane == LEAVES * i + j, total, 0.0), axis=1, keepdims=True)
            for j in range(LEAVES)
        ]
        for i in range(LEAVES)
    ]
    coef = tree(gram, LEAVES)
    bound = sum(jnp.abs(coef[i]) * jnp.sqrt(gram[i][i]) for i in range(LEAVES))
    bound = jnp.maximum(bound, FLOOR)
    scale = TOP / bound
    inverse_ref[...] = jnp.broadcast_to(bound * (1.0 / TOP), inverse_ref.shape)
    merged = None
    for k in range(LEAVES):
        mine = coef[k]
        for other in range(1, LEAVES):
            mine = jnp.where(me == other, coef[k ^ other], mine)
        term = (mine * scale) * leaf_refs[k][...]
        merged = term if merged is None else merged + term
    node_ref[...] = merged


def second_gram_kernel(copies, share, node_ref, nodes_ref, inverse_ref, late_ref, out_ref):
    node = node_ref[0]
    total, width = nodes_ref.shape
    rows = total // NODES
    held = nodes_ref[...]
    high = held.astype(bf16)
    low = (held - high.astype(f32)).astype(bf16)
    last = (((1,), (1,)), ((), ()))
    products = (
        lax.dot_general(high, high, last, preferred_element_type=f32)
        + lax.dot_general(high, low, last, preferred_element_type=f32)
        + lax.dot_general(low, high, last, preferred_element_type=f32)
        + lax.dot_general(low, low, last, preferred_element_type=f32)
    )
    row = lax.broadcasted_iota(jnp.int32, (total, total), 0)
    col = lax.broadcasted_iota(jnp.int32, (total, total), 1)
    products = jnp.where((row & (rows - 1)) == (col & (rows - 1)), products, 0.0)
    by_node = jnp.sum(products.reshape(NODES, rows, total), axis=1)
    source = lax.broadcasted_iota(jnp.int32, (total, 128), 0)
    lane = lax.broadcasted_iota(jnp.int32, (total, 128), 1)
    spread = jnp.where(source // rows == (lane & (NODES - 1)), 1.0, 0.0)
    gram = jnp.dot(by_node, spread, preferred_element_type=f32, precision=lax.Precision.HIGHEST)
    place = lax.broadcasted_iota(jnp.int32, (NODES, 128), 0)
    lane = lax.broadcasted_iota(jnp.int32, (NODES, 128), 1)
    packed = jnp.where(lane // NODES == (place & 7), gram, 0.0)
    lane = lane[:1]
    upper = jnp.sum(packed[:8], axis=0, keepdims=True)
    lower = jnp.sum(packed[8:], axis=0, keepdims=True)
    inverse = jnp.where(lane == (node & 7) + 2 * (node & 8), inverse_ref[:1] * share, 0.0)
    lower = jnp.where((lane & (NODES - 1)) < 8, inverse, lower)
    whole = jnp.concatenate([upper, lower], axis=0)
    for copy in range(copies):
        out_ref[copy] = whole


def pass_on_kernel(sums_ref, out_ref):
    whole = jnp.sum(sums_ref[...], axis=0)
    for copy in range(out_ref.shape[0]):
        out_ref[copy] = whole


def second_merge_kernel(sums_ref, nodes_ref, out_ref):
    total = jnp.sum(sums_ref[...], axis=0)
    place = lax.broadcasted_iota(jnp.int32, (NODES, 128), 0)
    lane = lax.broadcasted_iota(jnp.int32, (NODES, 128), 1)
    gram = jnp.where(place < 8, total[0:1], total[1:2])
    gram = jnp.where(lane // NODES == (place & 7), gram, 0.0)
    free = (lane & 8) == 0
    gram = jnp.where((place >= 8) & free, 0.0, gram)
    inverse_row = jnp.where((lane[:1] < NODES) & free[:1], total[1:2], 0.0)
    second = jnp.where((lane[:1] >= NODES) & (lane[:1] < NODES + 8), total[1:2], 0.0)
    inverse_row = inverse_row + pltpu.roll(second, 128 - 8, 1)
    for turn in (16, 32, 64):
        gram = gram + pltpu.roll(gram, turn, 1)
        inverse_row = inverse_row + pltpu.roll(inverse_row, turn, 1)
    other = lane & (NODES - 1)
    first = lane < NODES
    corner = jnp.where((place < 8) & (other >= 8), gram, 0.0)
    unit = jnp.where(place == other, 1.0, 0.0)
    mirrored = lax.dot_general(
        corner,
        unit,
        (((0,), (0,)), ((), ())),
        preferred_element_type=f32,
        precision=lax.Precision.HIGHEST,
    )
    gram = gram + mirrored[:NODES]

    def column(row):
        return jnp.sum(jnp.where(lane == place, row, 0.0), axis=1, keepdims=True)

    inverse_col = column(inverse_row)
    gram = gram * inverse_row * inverse_col
    size, weight = 1, jnp.ones((NODES, 1), f32)
    while size < NODES:
        mine = (place // size) == (other // size)
        sibling = (place // size) == ((other // size) ^ 1)
        own_col = jnp.sum(jnp.where(mine, gram, 0.0), axis=0, keepdims=True)
        cross_col = jnp.sum(jnp.where(sibling, gram, 0.0), axis=0, keepdims=True)
        here = mine & first
        own = jnp.sum(jnp.where(here, own_col, 0.0), axis=1, keepdims=True)
        cross = jnp.sum(jnp.where(here, cross_col, 0.0), axis=1, keepdims=True)
        coef = 1.0 - cross / (2.0 * (jnp.maximum(own, 0.0) + epsilon))
        coef_row = jnp.sum(jnp.where(place == other, coef, 0.0), axis=0, keepdims=True)
        gram = gram * coef * coef_row
        weight = weight * coef
        size *= 2
    weight = weight * inverse_col
    combined = None
    for node in range(NODES):
        term = weight[node : node + 1, :] * nodes_ref[node]
        combined = term if combined is None else combined + term
    out_ref[...] = combined


def local(pre_act, out_weight, out_grad):
    tokens, hidden = pre_act.shape
    width = out_weight.shape[1]
    mp = ("x", "c")
    hi = ("y", "zh")
    peers = lax.axis_size(mp)
    spot = jnp.stack([lax.axis_index(axis) for axis in ("zl", "x", "c")]).astype(jnp.int32)
    me = spot[:1]
    node = lax.axis_index(hi).astype(jnp.int32).reshape(1)
    quarter = hidden // LEAVES
    along = lax.axis_size("x")

    def swapped(value, axis, apart):
        return lax.ppermute(value, axis, [(i, i ^ apart) for i in range(lax.axis_size(axis))])

    copy, *dealt = deal(me, pre_act, out_grad)
    acts = {0: dealt[0]}
    for k in (2, 1, 3):
        acts[k] = swapped(dealt[k], "zl", k)
    pair = jnp.stack([copy, swapped(copy, "zl", 2)])
    shards = jnp.concatenate([pair, swapped(pair, "zl", 1)])
    grads = from_everyone(shards, mp)
    arrived = pl.pallas_call(
        arrived_kernel,
        out_shape=jax.ShapeDtypeStruct((8, 128), f32),
        in_specs=[ANY] * (LEAVES - 1),
        compiler_params=pltpu.CompilerParams(vmem_limit_bytes=1024 * 1024),
        cost_estimate=pl.CostEstimate(flops=10**11, bytes_accessed=0, transcendentals=0),
    )(acts[2], acts[1], acts[3])

    leaf_shape = jax.ShapeDtypeStruct((quarter, width), f32)
    group = ("zl", *mp)
    *leaves, sums = call(
        first_gram_kernel,
        [leaf_shape] * LEAVES + [jax.ShapeDtypeStruct((LEAVES * peers, 1, 128), f32)],
        [SMEM, VMEM, VMEM] + [VMEM] * LEAVES,
        flops=2 * tokens * hidden * width,
        size=16 * quarter * width,
    )(spot, grads, arrived, *[acts[k] for k in range(LEAVES)])
    sums = lax.all_to_all(sums, group, split_axis=0, concat_axis=0, tiled=True)
    scaled, inverse = call(
        first_merge_kernel,
        [leaf_shape, jax.ShapeDtypeStruct((8, 128), f32)],
        [SMEM] + [VMEM] * (LEAVES + 1),
        flops=8 * quarter * width,
        size=20 * quarter * width,
    )(me, sums, *leaves)

    half = jax.ShapeDtypeStruct((along, tokens // peers, width), f32)
    mine, theirs = call(
        project_kernel,
        [half, half],
        [SMEM] + [VMEM] * (LEAVES + 2),
        flops=2 * tokens * hidden * width,
        size=4 * tokens * hidden,
        scratch=[pltpu.VMEM((along, 2, tokens // peers, width), f32)],
    )(spot, out_weight.reshape(NODES, LEAVES, -1, width), inverse, *dealt)
    both = mine + swapped(theirs, "c", 1)
    projected = both[0]
    for k in range(1, along):
        projected = projected + swapped(both[k], "x", k)
    projected = projected.astype(bf16)

    rows = quarter // NODES
    sent = scaled.astype(jnp.float16).reshape(NODES, rows, width)
    nodes = lax.all_to_all(sent, hi, split_axis=0, concat_axis=0, tiled=True).astype(f32)
    share = 1.0 / (LEAVES * peers)
    sums = call(
        functools.partial(second_gram_kernel, peers * along, share),
        jax.ShapeDtypeStruct((peers * along, 2, 128), f32),
        [SMEM, VMEM, VMEM, VMEM],
        flops=8 * quarter * quarter * width,
        size=4 * quarter * width,
    )(node, nodes.reshape(quarter, width), inverse, projected)
    sums = lax.all_to_all(sums, ("y", *mp), split_axis=0, concat_axis=0, tiled=True)
    sums = call(pass_on_kernel, jax.ShapeDtypeStruct((NODES, 2, 128), f32), [VMEM])(sums)
    sums = lax.all_to_all(sums, ("zh", "zl"), split_axis=0, concat_axis=0, tiled=True)
    combined = call(
        second_merge_kernel,
        jax.ShapeDtypeStruct((rows, width), f32),
        [VMEM, VMEM],
        flops=2 * quarter * width,
        size=4 * quarter * width,
    )(sums, nodes)
    return projected, combined


def solution(mesh):
    devices = mesh.devices.reshape(4, 4, LEAVES, 4, 2)
    finer = Mesh(devices, ("y", "zh", "zl", "x", "c"))
    dp, mp = ("y", "zh", "zl"), ("x", "c")
    return jax.shard_map(
        local,
        mesh=finer,
        in_specs=(P(dp, mp), P(mp, None), P((*dp, *mp), None)),
        out_specs=(P((*dp, *mp), None), P((*mp, *dp), None)),
        check_vma=False,
    )
```

```python
import functools

import jax
import jax.numpy as jnp
from jax import lax
from jax.experimental import pallas as pl
from jax.experimental.pallas import tpu as pltpu
from jax.sharding import Mesh, PartitionSpec as P

epsilon = 1e-06
LEAVES = 4
NODES = 16
LIMIT = 24 * 1024 * 1024
TOP = 16384.0
FLOOR = 1e-15

f32 = jnp.float32
bf16 = jnp.bfloat16
SMEM = pl.BlockSpec(memory_space=pltpu.SMEM)
VMEM = pl.BlockSpec(memory_space=pltpu.VMEM)
ANY = pl.BlockSpec(memory_space=pl.ANY)


def call(kernel, out_shape, in_specs, flops=0, size=0, scratch=()):
    many = isinstance(out_shape, (list, tuple))
    return pl.pallas_call(
        kernel,
        out_shape=out_shape,
        in_specs=in_specs,
        out_specs=[VMEM] * len(out_shape) if many else VMEM,
        scratch_shapes=list(scratch),
        compiler_params=pltpu.CompilerParams(vmem_limit_bytes=LIMIT),
        cost_estimate=pl.CostEstimate(flops=flops, bytes_accessed=size, transcendentals=0),
    )


def from_everyone(array, axes):
    copies = jnp.broadcast_to(array, (lax.axis_size(axes), *array.shape))
    return lax.all_to_all(copies, axes, split_axis=0, concat_axis=0, tiled=True)


def inner_of(me):
    return (me ^ (me >> 1)) & 1


def leaf_ids(me):
    inner = inner_of(me)
    return (me, me ^ (2 - inner), me ^ (1 + inner), me ^ 3)


def deal_kernel(me_ref, pre_ref, *refs):
    out_refs, deal_ref = refs[:LEAVES], refs[LEAVES]
    width = pre_ref.shape[1]

    @pl.when(pl.program_id(0) == 0)
    def _():
        row = lax.broadcasted_iota(jnp.int32, (width, width), 0)
        col = lax.broadcasted_iota(jnp.int32, (width, width), 1)
        block = row >> 5
        apart = (block & 3) ^ me_ref[0]
        turned = (apart >> 1) | ((apart & 1) << 1)
        slot = apart + inner_of(me_ref[0]) * (turned - apart)
        place = (slot << 7) + ((block >> 2) << 5) + (row & 31)
        deal_ref[...] = jnp.where(place == col, 1.0, 0.0).astype(bf16)

    part = jnp.maximum(pre_ref[...], jnp.zeros((), bf16))
    dealt = jnp.dot(part, deal_ref[...], preferred_element_type=f32).astype(bf16)
    for k in range(LEAVES):
        out_refs[k][...] = dealt[:, k * 128 : (k + 1) * 128]


def deal(me, pre_act):
    tokens, hidden = pre_act.shape
    group = 512
    return pl.pallas_call(
        deal_kernel,
        grid_spec=pltpu.PrefetchScalarGridSpec(
            num_scalar_prefetch=1,
            grid=(hidden // group,),
            in_specs=[pl.BlockSpec((tokens, group), lambda g, me: (0, g))],
            out_specs=[pl.BlockSpec((tokens, group // LEAVES), lambda g, me: (0, g))] * LEAVES,
            scratch_shapes=[pltpu.VMEM((group, group), bf16)],
        ),
        out_shape=[jax.ShapeDtypeStruct((tokens, hidden // LEAVES), bf16)] * LEAVES,
        compiler_params=pltpu.CompilerParams(vmem_limit_bytes=LIMIT),
        cost_estimate=pl.CostEstimate(
            flops=2 * tokens * hidden * group, bytes_accessed=4 * tokens * hidden, transcendentals=0
        ),
    )(me, pre_act)


def arrived_kernel(*refs):
    refs[-1][...] = jnp.zeros_like(refs[-1])


def project_kernel(spot_ref, pre_ref, weight_ref, late_ref, mine_ref, theirs_ref, held_ref):
    count = mine_ref.shape[0]
    x, core = spot_ref[1], spot_ref[2]
    act = jnp.maximum(pre_ref[...], jnp.zeros((), bf16))
    total = jnp.dot(act, weight_ref[...], preferred_element_type=f32)
    held_ref[...] = total.reshape(held_ref.shape)
    for k in range(count):
        mine_ref[k] = held_ref[x ^ k, core]
        theirs_ref[k] = held_ref[x ^ k, 1 - core]


def lanes_of(total):
    return total[:, :128] + total[:, 128:256] + total[:, 256:384] + total[:, 384:512]


def first_gram_kernel(spot_ref, grads_ref, late_ref, *refs):
    act_refs, held, out_ref = refs[:LEAVES], refs[LEAVES:-1], refs[-1]
    peers, _, rows, width = grads_ref.shape
    ids = leaf_ids(spot_ref[0])
    for k in range(LEAVES):
        out_grad = grads_ref[:, ids[k]].reshape(peers * rows, width)
        held[k][...] = lax.dot_general(
            act_refs[k][...], out_grad, (((0,), (0,)), ((), ())), preferred_element_type=f32
        )
    lane = lax.broadcasted_iota(jnp.int32, (1, 128), 1)
    whole = jnp.zeros((1, 128), f32)
    for a in range(LEAVES):
        for b in range(a, LEAVES):
            lanes = lanes_of(jnp.sum(held[a][...] * held[b][...], axis=0, keepdims=True))
            value = jnp.sum(lanes, axis=1, keepdims=True)
            here = lane == LEAVES * ids[a] + ids[b]
            if a != b:
                here = here | (lane == LEAVES * ids[b] + ids[a])
            whole = jnp.where(here, value, whole)
    for copy in range(out_ref.shape[0]):
        out_ref[copy] = whole


def tree(gram, count):
    coef = [None] * count
    weight = [jnp.ones_like(gram[0][0])] * count
    size = 1
    while size < count:
        for low in range(0, count, 2 * size):
            first, second = range(low, low + size), range(low + size, low + 2 * size)

            def inner(left, right):
                return sum(weight[i] * weight[j] * gram[i][j] for i in left for j in right)

            cross = inner(first, second)
            first_sq = jnp.maximum(inner(first, first), 0.0)
            second_sq = jnp.maximum(inner(second, second), 0.0)
            first_coef = 1.0 - cross / (2.0 * (first_sq + epsilon))
            second_coef = 1.0 - cross / (2.0 * (second_sq + epsilon))
            for i in first:
                coef[i] = weight[i] * first_coef
            for i in second:
                coef[i] = weight[i] * second_coef
        weight = list(coef)
        size *= 2
    return weight


def first_merge_kernel(me_ref, sums_ref, *refs):
    leaf_refs, node_ref, inverse_ref = refs[:LEAVES], refs[LEAVES], refs[LEAVES + 1]
    ids = leaf_ids(me_ref[0])
    total = jnp.sum(sums_ref[...], axis=0)
    lane = lax.broadcasted_iota(jnp.int32, total.shape, 1)
    gram = [
        [
            jnp.sum(jnp.where(lane == LEAVES * i + j, total, 0.0), axis=1, keepdims=True)
            for j in range(LEAVES)
        ]
        for i in range(LEAVES)
    ]
    coef = tree(gram, LEAVES)
    bound = sum(jnp.abs(coef[i]) * jnp.sqrt(gram[i][i]) for i in range(LEAVES))
    bound = jnp.maximum(bound, FLOOR)
    scale = TOP / bound
    inverse_ref[...] = jnp.broadcast_to(bound * (1.0 / TOP), inverse_ref.shape)
    merged = None
    for k in range(LEAVES):
        mine = coef[0]
        for leaf in range(1, LEAVES):
            mine = jnp.where(ids[k] == leaf, coef[leaf], mine)
        term = (mine * scale) * leaf_refs[k][...]
        merged = term if merged is None else merged + term
    node_ref[...] = merged


def second_gram_kernel(copies, share, node_ref, nodes_ref, inverse_ref, late_ref, out_ref):
    node = node_ref[0]
    total, width = nodes_ref.shape
    rows = total // NODES
    held = nodes_ref[...]
    high = held.astype(bf16)
    low = (held - high.astype(f32)).astype(bf16)
    last = (((1,), (1,)), ((), ()))
    products = (
        lax.dot_general(high, high, last, preferred_element_type=f32)
        + lax.dot_general(high, low, last, preferred_element_type=f32)
        + lax.dot_general(low, high, last, preferred_element_type=f32)
        + lax.dot_general(low, low, last, preferred_element_type=f32)
    )
    row = lax.broadcasted_iota(jnp.int32, (total, total), 0)
    col = lax.broadcasted_iota(jnp.int32, (total, total), 1)
    products = jnp.where((row & (rows - 1)) == (col & (rows - 1)), products, 0.0)
    by_node = jnp.sum(products.reshape(NODES, rows, total), axis=1)
    source = lax.broadcasted_iota(jnp.int32, (total, 128), 0)
    lane = lax.broadcasted_iota(jnp.int32, (total, 128), 1)
    spread = jnp.where(source // rows == (lane & (NODES - 1)), 1.0, 0.0)
    gram = jnp.dot(by_node, spread, preferred_element_type=f32, precision=lax.Precision.HIGHEST)
    place = lax.broadcasted_iota(jnp.int32, (NODES, 128), 0)
    lane = lax.broadcasted_iota(jnp.int32, (NODES, 128), 1)
    packed = jnp.where(lane // NODES == (place & 7), gram, 0.0)
    lane = lane[:1]
    upper = jnp.sum(packed[:8], axis=0, keepdims=True)
    lower = jnp.sum(packed[8:], axis=0, keepdims=True)
    inverse = jnp.where(lane == (node & 7) + 2 * (node & 8), inverse_ref[:1] * share, 0.0)
    lower = jnp.where((lane & (NODES - 1)) < 8, inverse, lower)
    whole = jnp.concatenate([upper, lower], axis=0)
    for copy in range(copies):
        out_ref[copy] = whole


def pass_on_kernel(sums_ref, out_ref):
    whole = jnp.sum(sums_ref[...], axis=0)
    for copy in range(out_ref.shape[0]):
        out_ref[copy] = whole


def second_merge_kernel(sums_ref, nodes_ref, out_ref):
    total = jnp.sum(sums_ref[...], axis=0)
    place = lax.broadcasted_iota(jnp.int32, (NODES, 128), 0)
    lane = lax.broadcasted_iota(jnp.int32, (NODES, 128), 1)
    gram = jnp.where(place < 8, total[0:1], total[1:2])
    gram = jnp.where(lane // NODES == (place & 7), gram, 0.0)
    free = (lane & 8) == 0
    gram = jnp.where((place >= 8) & free, 0.0, gram)
    inverse_row = jnp.where((lane[:1] < NODES) & free[:1], total[1:2], 0.0)
    second = jnp.where((lane[:1] >= NODES) & (lane[:1] < NODES + 8), total[1:2], 0.0)
    inverse_row = inverse_row + pltpu.roll(second, 128 - 8, 1)
    for turn in (16, 32, 64):
        gram = gram + pltpu.roll(gram, turn, 1)
        inverse_row = inverse_row + pltpu.roll(inverse_row, turn, 1)
    other = lane & (NODES - 1)
    first = lane < NODES
    corner = jnp.where((place < 8) & (other >= 8), gram, 0.0)
    unit = jnp.where(place == other, 1.0, 0.0)
    mirrored = lax.dot_general(
        corner,
        unit,
        (((0,), (0,)), ((), ())),
        preferred_element_type=f32,
        precision=lax.Precision.HIGHEST,
    )
    gram = gram + mirrored[:NODES]

    def column(row):
        return jnp.sum(jnp.where(lane == place, row, 0.0), axis=1, keepdims=True)

    inverse_col = column(inverse_row)
    gram = gram * inverse_row * inverse_col
    size, weight = 1, jnp.ones((NODES, 1), f32)
    while size < NODES:
        mine = (place // size) == (other // size)
        sibling = (place // size) == ((other // size) ^ 1)
        own_col = jnp.sum(jnp.where(mine, gram, 0.0), axis=0, keepdims=True)
        cross_col = jnp.sum(jnp.where(sibling, gram, 0.0), axis=0, keepdims=True)
        here = mine & first
        own = jnp.sum(jnp.where(here, own_col, 0.0), axis=1, keepdims=True)
        cross = jnp.sum(jnp.where(here, cross_col, 0.0), axis=1, keepdims=True)
        coef = 1.0 - cross / (2.0 * (jnp.maximum(own, 0.0) + epsilon))
        coef_row = jnp.sum(jnp.where(place == other, coef, 0.0), axis=0, keepdims=True)
        gram = gram * coef * coef_row
        weight = weight * coef
        size *= 2
    weight = weight * inverse_col
    combined = None
    for node in range(NODES):
        term = weight[node : node + 1, :] * nodes_ref[node]
        combined = term if combined is None else combined + term
    out_ref[...] = combined


def local(pre_act, out_weight, out_grad):
    tokens, hidden = pre_act.shape
    width = out_weight.shape[1]
    mp = ("x", "c")
    hi = ("y", "zh")
    peers = lax.axis_size(mp)
    spot = jnp.stack([lax.axis_index(axis) for axis in ("zl", "x", "c")]).astype(jnp.int32)
    me = spot[:1]
    node = lax.axis_index(hi).astype(jnp.int32).reshape(1)
    quarter = hidden // LEAVES
    along = lax.axis_size("x")

    def swapped(value, axis, apart):
        return lax.ppermute(value, axis, [(i, i ^ apart) for i in range(lax.axis_size(axis))])

    shards = from_everyone(out_grad, "zl")
    grads = from_everyone(shards, mp)
    dealt = deal(me, pre_act)
    acts = {0: dealt[0]}
    acts[2] = lax.ppermute(dealt[2], "zl", [(0, 2), (3, 1), (1, 0), (2, 3)])
    acts[3] = lax.ppermute(dealt[3], "zl", [(0, 3), (3, 0), (1, 2), (2, 1)])
    acts[1] = lax.ppermute(dealt[1], "zl", [(0, 1), (3, 2), (1, 3), (2, 0)])
    arrived = pl.pallas_call(
        arrived_kernel,
        out_shape=jax.ShapeDtypeStruct((8, 128), f32),
        in_specs=[ANY] * (LEAVES - 1),
        compiler_params=pltpu.CompilerParams(vmem_limit_bytes=1024 * 1024),
        cost_estimate=pl.CostEstimate(flops=10**11, bytes_accessed=0, transcendentals=0),
    )(acts[2], acts[3], acts[1])

    leaf_shape = jax.ShapeDtypeStruct((quarter, width), f32)
    group = ("zl", *mp)
    *leaves, sums = call(
        first_gram_kernel,
        [leaf_shape] * LEAVES + [jax.ShapeDtypeStruct((LEAVES * peers, 1, 128), f32)],
        [SMEM, VMEM, VMEM] + [VMEM] * LEAVES,
        flops=2 * tokens * hidden * width,
        size=16 * quarter * width,
    )(spot, grads, arrived, *[acts[k] for k in range(LEAVES)])
    sums = lax.all_to_all(sums, group, split_axis=0, concat_axis=0, tiled=True)
    scaled, inverse = call(
        first_merge_kernel,
        [leaf_shape, jax.ShapeDtypeStruct((8, 128), f32)],
        [SMEM] + [VMEM] * (LEAVES + 1),
        flops=8 * quarter * width,
        size=20 * quarter * width,
    )(me, sums, *leaves)

    half = jax.ShapeDtypeStruct((along, tokens // peers, width), f32)
    mine, theirs = call(
        project_kernel,
        [half, half],
        [SMEM, VMEM, VMEM, VMEM],
        flops=2 * tokens * hidden * width,
        size=4 * tokens * hidden,
        scratch=[pltpu.VMEM((along, 2, tokens // peers, width), f32)],
    )(spot, pre_act, out_weight, inverse)
    both = mine + swapped(theirs, "c", 1)
    projected = both[0]
    for k in range(1, along):
        projected = projected + swapped(both[k], "x", k)
    projected = projected.astype(bf16)

    rows = quarter // NODES
    sent = scaled.astype(jnp.float16).reshape(NODES, rows, width)
    nodes = lax.all_to_all(sent, hi, split_axis=0, concat_axis=0, tiled=True).astype(f32)
    share = 1.0 / (LEAVES * peers)
    sums = call(
        functools.partial(second_gram_kernel, peers, share),
        jax.ShapeDtypeStruct((peers, 2, 128), f32),
        [SMEM, VMEM, VMEM, VMEM],
        flops=8 * quarter * quarter * width,
        size=4 * quarter * width,
    )(node, nodes.reshape(quarter, width), inverse, projected)
    sums = lax.all_to_all(sums, mp, split_axis=0, concat_axis=0, tiled=True)
    dp = ("y", "zh", "zl")
    sums = call(pass_on_kernel, jax.ShapeDtypeStruct((LEAVES * NODES, 2, 128), f32), [VMEM])(sums)
    sums = lax.all_to_all(sums, dp, split_axis=0, concat_axis=0, tiled=True)
    combined = call(
        second_merge_kernel,
        jax.ShapeDtypeStruct((rows, width), f32),
        [VMEM, VMEM],
        flops=2 * quarter * width,
        size=4 * quarter * width,
    )(sums, nodes)
    return projected, combined


def solution(mesh):
    devices = mesh.devices.reshape(4, 4, LEAVES, 4, 2)
    finer = Mesh(devices, ("y", "zh", "zl", "x", "c"))
    dp, mp = ("y", "zh", "zl"), ("x", "c")
    return jax.shard_map(
        local,
        mesh=finer,
        in_specs=(P(dp, mp), P(mp, None), P((*dp, *mp), None)),
        out_specs=(P((*dp, *mp), None), P((*mp, *dp), None)),
        check_vma=False,
    )
```

```python
import functools

import jax
import jax.numpy as jnp
from jax import lax
from jax.experimental import pallas as pl
from jax.experimental.pallas import tpu as pltpu
from jax.sharding import Mesh, PartitionSpec as P

epsilon = 1e-06
LEAVES = 4
NODES = 16
LIMIT = 24 * 1024 * 1024
TOP = 16384.0
FLOOR = 1e-15

f32 = jnp.float32
bf16 = jnp.bfloat16
SMEM = pl.BlockSpec(memory_space=pltpu.SMEM)
VMEM = pl.BlockSpec(memory_space=pltpu.VMEM)
ANY = pl.BlockSpec(memory_space=pl.ANY)


def call(kernel, out_shape, in_specs, flops=0, size=0, scratch=()):
    many = isinstance(out_shape, (list, tuple))
    return pl.pallas_call(
        kernel,
        out_shape=out_shape,
        in_specs=in_specs,
        out_specs=[VMEM] * len(out_shape) if many else VMEM,
        scratch_shapes=list(scratch),
        compiler_params=pltpu.CompilerParams(vmem_limit_bytes=LIMIT),
        cost_estimate=pl.CostEstimate(flops=flops, bytes_accessed=size, transcendentals=0),
    )


def copies_kernel(array_ref, out_ref, done):
    copies = [pltpu.make_async_copy(array_ref, out_ref.at[k], done.at[k]) for k in range(LEAVES)]
    for copy in copies:
        copy.start()
    for copy in copies:
        copy.wait()


def from_everyone(array, axes):
    copies = jnp.broadcast_to(array, (lax.axis_size(axes), *array.shape))
    return lax.all_to_all(copies, axes, split_axis=0, concat_axis=0, tiled=True)


def deal_kernel(me_ref, pre_ref, *refs):
    out_refs, deal_ref = refs[:LEAVES], refs[LEAVES]
    width = pre_ref.shape[1]

    @pl.when(pl.program_id(0) == 0)
    def _():
        row = lax.broadcasted_iota(jnp.int32, (width, width), 0)
        col = lax.broadcasted_iota(jnp.int32, (width, width), 1)
        block = row >> 5
        place = (((block & 3) ^ me_ref[0]) << 7) + ((block >> 2) << 5) + (row & 31)
        deal_ref[...] = jnp.where(place == col, 1.0, 0.0).astype(bf16)

    part = jnp.maximum(pre_ref[...], jnp.zeros((), bf16))
    dealt = jnp.dot(part, deal_ref[...], preferred_element_type=f32).astype(bf16)
    for k in range(LEAVES):
        out_refs[k][...] = dealt[:, k * 128 : (k + 1) * 128]


def deal(me, pre_act):
    tokens, hidden = pre_act.shape
    group = 512
    return pl.pallas_call(
        deal_kernel,
        grid_spec=pltpu.PrefetchScalarGridSpec(
            num_scalar_prefetch=1,
            grid=(hidden // group,),
            in_specs=[pl.BlockSpec((tokens, group), lambda g, me: (0, g))],
            out_specs=[pl.BlockSpec((tokens, group // LEAVES), lambda g, me: (0, g))] * LEAVES,
            scratch_shapes=[pltpu.VMEM((group, group), bf16)],
        ),
        out_shape=[jax.ShapeDtypeStruct((tokens, hidden // LEAVES), bf16)] * LEAVES,
        compiler_params=pltpu.CompilerParams(vmem_limit_bytes=LIMIT),
        cost_estimate=pl.CostEstimate(
            flops=2 * tokens * hidden * group, bytes_accessed=4 * tokens * hidden, transcendentals=0
        ),
    )(me, pre_act)


def arrived_kernel(*refs):
    refs[-1][...] = jnp.zeros_like(refs[-1])


def project_kernel(spot_ref, pre_ref, weight_ref, late_ref, mine_ref, theirs_ref, held_ref):
    count = mine_ref.shape[0]
    x, core = spot_ref[1], spot_ref[2]
    act = jnp.maximum(pre_ref[...], jnp.zeros((), bf16))
    total = jnp.dot(act, weight_ref[...], preferred_element_type=f32)
    held_ref[...] = total.reshape(held_ref.shape)
    for k in range(count):
        mine_ref[k] = held_ref[x ^ k, core]
        theirs_ref[k] = held_ref[x ^ k, 1 - core]


def lanes_of(total):
    return total[:, :128] + total[:, 128:256] + total[:, 256:384] + total[:, 384:512]


def first_gram_kernel(spot_ref, grads_ref, late_ref, *refs):
    act_refs, held, out_ref = refs[:LEAVES], refs[LEAVES:-1], refs[-1]
    peers, _, rows, width = grads_ref.shape
    me = spot_ref[0]
    for k in range(LEAVES):
        out_grad = grads_ref[:, me ^ k].reshape(peers * rows, width)
        held[k][...] = lax.dot_general(
            act_refs[k][...], out_grad, (((0,), (0,)), ((), ())), preferred_element_type=f32
        )
    lane = lax.broadcasted_iota(jnp.int32, (1, 128), 1)
    whole = jnp.zeros((1, 128), f32)
    for a in range(LEAVES):
        for b in range(a, LEAVES):
            lanes = lanes_of(jnp.sum(held[a][...] * held[b][...], axis=0, keepdims=True))
            value = jnp.sum(lanes, axis=1, keepdims=True)
            here = lane == LEAVES * (a ^ me) + (b ^ me)
            if a != b:
                here = here | (lane == LEAVES * (b ^ me) + (a ^ me))
            whole = jnp.where(here, value, whole)
    for copy in range(out_ref.shape[0]):
        out_ref[copy] = whole


def tree(gram, count):
    coef = [None] * count
    weight = [jnp.ones_like(gram[0][0])] * count
    size = 1
    while size < count:
        for low in range(0, count, 2 * size):
            first, second = range(low, low + size), range(low + size, low + 2 * size)

            def inner(left, right):
                return sum(weight[i] * weight[j] * gram[i][j] for i in left for j in right)

            cross = inner(first, second)
            first_sq = jnp.maximum(inner(first, first), 0.0)
            second_sq = jnp.maximum(inner(second, second), 0.0)
            first_coef = 1.0 - cross / (2.0 * (first_sq + epsilon))
            second_coef = 1.0 - cross / (2.0 * (second_sq + epsilon))
            for i in first:
                coef[i] = weight[i] * first_coef
            for i in second:
                coef[i] = weight[i] * second_coef
        weight = list(coef)
        size *= 2
    return weight


def first_merge_kernel(me_ref, sums_ref, *refs):
    leaf_refs, node_ref, inverse_ref = refs[:LEAVES], refs[LEAVES], refs[LEAVES + 1]
    me = me_ref[0]
    total = jnp.sum(sums_ref[...], axis=0)
    lane = lax.broadcasted_iota(jnp.int32, total.shape, 1)
    gram = [
        [
            jnp.sum(jnp.where(lane == LEAVES * i + j, total, 0.0), axis=1, keepdims=True)
            for j in range(LEAVES)
        ]
        for i in range(LEAVES)
    ]
    coef = tree(gram, LEAVES)
    bound = sum(jnp.abs(coef[i]) * jnp.sqrt(gram[i][i]) for i in range(LEAVES))
    bound = jnp.maximum(bound, FLOOR)
    scale = TOP / bound
    inverse_ref[...] = jnp.broadcast_to(bound * (1.0 / TOP), inverse_ref.shape)
    merged = None
    for k in range(LEAVES):
        mine = coef[k]
        for other in range(1, LEAVES):
            mine = jnp.where(me == other, coef[k ^ other], mine)
        term = (mine * scale) * leaf_refs[k][...]
        merged = term if merged is None else merged + term
    node_ref[...] = merged


def second_gram_kernel(copies, share, node_ref, nodes_ref, inverse_ref, late_ref, out_ref):
    node = node_ref[0]
    total, width = nodes_ref.shape
    rows = total // NODES
    held = nodes_ref[...]
    high = held.astype(bf16)
    low = (held - high.astype(f32)).astype(bf16)
    last = (((1,), (1,)), ((), ()))
    products = (
        lax.dot_general(high, high, last, preferred_element_type=f32)
        + lax.dot_general(high, low, last, preferred_element_type=f32)
        + lax.dot_general(low, high, last, preferred_element_type=f32)
        + lax.dot_general(low, low, last, preferred_element_type=f32)
    )
    row = lax.broadcasted_iota(jnp.int32, (total, total), 0)
    col = lax.broadcasted_iota(jnp.int32, (total, total), 1)
    products = jnp.where((row & (rows - 1)) == (col & (rows - 1)), products, 0.0)
    by_node = jnp.sum(products.reshape(NODES, rows, total), axis=1)
    source = lax.broadcasted_iota(jnp.int32, (total, 128), 0)
    lane = lax.broadcasted_iota(jnp.int32, (total, 128), 1)
    spread = jnp.where(source // rows == (lane & (NODES - 1)), 1.0, 0.0)
    gram = jnp.dot(by_node, spread, preferred_element_type=f32, precision=lax.Precision.HIGHEST)
    place = lax.broadcasted_iota(jnp.int32, (NODES, 128), 0)
    lane = lax.broadcasted_iota(jnp.int32, (NODES, 128), 1)
    packed = jnp.where(lane // NODES == (place & 7), gram, 0.0)
    lane = lane[:1]
    upper = jnp.sum(packed[:8], axis=0, keepdims=True)
    lower = jnp.sum(packed[8:], axis=0, keepdims=True)
    inverse = jnp.where(lane == (node & 7) + 2 * (node & 8), inverse_ref[:1] * share, 0.0)
    lower = jnp.where((lane & (NODES - 1)) < 8, inverse, lower)
    whole = jnp.concatenate([upper, lower], axis=0)
    for copy in range(copies):
        out_ref[copy] = whole


def pass_on_kernel(sums_ref, out_ref):
    whole = jnp.sum(sums_ref[...], axis=0)
    for copy in range(out_ref.shape[0]):
        out_ref[copy] = whole


def second_merge_kernel(sums_ref, nodes_ref, out_ref):
    total = jnp.sum(sums_ref[...], axis=0)
    place = lax.broadcasted_iota(jnp.int32, (NODES, 128), 0)
    lane = lax.broadcasted_iota(jnp.int32, (NODES, 128), 1)
    gram = jnp.where(place < 8, total[0:1], total[1:2])
    gram = jnp.where(lane // NODES == (place & 7), gram, 0.0)
    free = (lane & 8) == 0
    gram = jnp.where((place >= 8) & free, 0.0, gram)
    inverse_row = jnp.where((lane[:1] < NODES) & free[:1], total[1:2], 0.0)
    second = jnp.where((lane[:1] >= NODES) & (lane[:1] < NODES + 8), total[1:2], 0.0)
    inverse_row = inverse_row + pltpu.roll(second, 128 - 8, 1)
    for turn in (16, 32, 64):
        gram = gram + pltpu.roll(gram, turn, 1)
        inverse_row = inverse_row + pltpu.roll(inverse_row, turn, 1)
    other = lane & (NODES - 1)
    first = lane < NODES
    corner = jnp.where((place < 8) & (other >= 8), gram, 0.0)
    unit = jnp.where(place == other, 1.0, 0.0)
    mirrored = lax.dot_general(
        corner,
        unit,
        (((0,), (0,)), ((), ())),
        preferred_element_type=f32,
        precision=lax.Precision.HIGHEST,
    )
    gram = gram + mirrored[:NODES]

    def column(row):
        return jnp.sum(jnp.where(lane == place, row, 0.0), axis=1, keepdims=True)

    inverse_col = column(inverse_row)
    gram = gram * inverse_row * inverse_col
    size, weight = 1, jnp.ones((NODES, 1), f32)
    while size < NODES:
        mine = (place // size) == (other // size)
        sibling = (place // size) == ((other // size) ^ 1)
        own_col = jnp.sum(jnp.where(mine, gram, 0.0), axis=0, keepdims=True)
        cross_col = jnp.sum(jnp.where(sibling, gram, 0.0), axis=0, keepdims=True)
        here = mine & first
        own = jnp.sum(jnp.where(here, own_col, 0.0), axis=1, keepdims=True)
        cross = jnp.sum(jnp.where(here, cross_col, 0.0), axis=1, keepdims=True)
        coef = 1.0 - cross / (2.0 * (jnp.maximum(own, 0.0) + epsilon))
        coef_row = jnp.sum(jnp.where(place == other, coef, 0.0), axis=0, keepdims=True)
        gram = gram * coef * coef_row
        weight = weight * coef
        size *= 2
    weight = weight * inverse_col
    combined = None
    for node in range(NODES):
        term = weight[node : node + 1, :] * nodes_ref[node]
        combined = term if combined is None else combined + term
    out_ref[...] = combined


def local(pre_act, out_weight, out_grad):
    tokens, hidden = pre_act.shape
    width = out_weight.shape[1]
    mp = ("x", "c")
    hi = ("y", "zh")
    peers = lax.axis_size(mp)
    spot = jnp.stack([lax.axis_index(axis) for axis in ("zl", "x", "c")]).astype(jnp.int32)
    me = spot[:1]
    node = lax.axis_index(hi).astype(jnp.int32).reshape(1)
    quarter = hidden // LEAVES
    along = lax.axis_size("x")

    def swapped(value, axis, apart):
        return lax.ppermute(value, axis, [(i, i ^ apart) for i in range(lax.axis_size(axis))])

    copies = pl.pallas_call(
        copies_kernel,
        out_shape=jax.ShapeDtypeStruct((LEAVES, *out_grad.shape), bf16),
        in_specs=[ANY],
        out_specs=ANY,
        scratch_shapes=[pltpu.SemaphoreType.DMA((LEAVES,))],
    )(out_grad)
    shards = lax.all_to_all(copies, "zl", split_axis=0, concat_axis=0, tiled=True)
    grads = from_everyone(shards, mp)
    dealt = deal(me, pre_act)
    acts = {0: dealt[0]}
    for k in (3, 2, 1):
        acts[k] = swapped(dealt[k], "zl", k)
    arrived = pl.pallas_call(
        arrived_kernel,
        out_shape=jax.ShapeDtypeStruct((8, 128), f32),
        in_specs=[ANY] * (LEAVES - 1),
        compiler_params=pltpu.CompilerParams(vmem_limit_bytes=1024 * 1024),
        cost_estimate=pl.CostEstimate(flops=10**11, bytes_accessed=0, transcendentals=0),
    )(acts[3], acts[2], acts[1])

    leaf_shape = jax.ShapeDtypeStruct((quarter, width), f32)
    group = ("zl", *mp)
    *leaves, sums = call(
        first_gram_kernel,
        [leaf_shape] * LEAVES + [jax.ShapeDtypeStruct((LEAVES * peers, 1, 128), f32)],
        [SMEM, VMEM, VMEM] + [VMEM] * LEAVES,
        flops=2 * tokens * hidden * width,
        size=16 * quarter * width,
    )(spot, grads, arrived, *[acts[k] for k in range(LEAVES)])
    sums = lax.all_to_all(sums, group, split_axis=0, concat_axis=0, tiled=True)
    scaled, inverse = call(
        first_merge_kernel,
        [leaf_shape, jax.ShapeDtypeStruct((8, 128), f32)],
        [SMEM] + [VMEM] * (LEAVES + 1),
        flops=8 * quarter * width,
        size=20 * quarter * width,
    )(me, sums, *leaves)

    half = jax.ShapeDtypeStruct((along, tokens // peers, width), f32)
    mine, theirs = call(
        project_kernel,
        [half, half],
        [SMEM, VMEM, VMEM, VMEM],
        flops=2 * tokens * hidden * width,
        size=4 * tokens * hidden,
        scratch=[pltpu.VMEM((along, 2, tokens // peers, width), f32)],
    )(spot, pre_act, out_weight, inverse)
    both = mine + swapped(theirs, "c", 1)
    projected = both[0]
    for k in range(1, along):
        projected = projected + swapped(both[k], "x", k)
    projected = projected.astype(bf16)

    rows = quarter // NODES
    sent = scaled.astype(jnp.float16).reshape(NODES, rows, width)
    nodes = lax.all_to_all(sent, hi, split_axis=0, concat_axis=0, tiled=True).astype(f32)
    share = 1.0 / (LEAVES * peers)
    sums = call(
        functools.partial(second_gram_kernel, peers, share),
        jax.ShapeDtypeStruct((peers, 2, 128), f32),
        [SMEM, VMEM, VMEM, VMEM],
        flops=8 * quarter * quarter * width,
        size=4 * quarter * width,
    )(node, nodes.reshape(quarter, width), inverse, projected)
    sums = lax.all_to_all(sums, mp, split_axis=0, concat_axis=0, tiled=True)
    dp = ("y", "zh", "zl")
    sums = call(pass_on_kernel, jax.ShapeDtypeStruct((LEAVES * NODES, 2, 128), f32), [VMEM])(sums)
    sums = lax.all_to_all(sums, dp, split_axis=0, concat_axis=0, tiled=True)
    combined = call(
        second_merge_kernel,
        jax.ShapeDtypeStruct((rows, width), f32),
        [VMEM, VMEM],
        flops=2 * quarter * width,
        size=4 * quarter * width,
    )(sums, nodes)
    return projected, combined


def solution(mesh):
    devices = mesh.devices.reshape(4, 4, LEAVES, 4, 2)
    finer = Mesh(devices, ("y", "zh", "zl", "x", "c"))
    dp, mp = ("y", "zh", "zl"), ("x", "c")
    return jax.shard_map(
        local,
        mesh=finer,
        in_specs=(P(dp, mp), P(mp, None), P((*dp, *mp), None)),
        out_specs=(P((*dp, *mp), None), P((*mp, *dp), None)),
        check_vma=False,
    )
```
